32 devices in a mesh: dp: 2 (over x), expert: 16 (over z, y, core).
Axes of the slice: x: 2, y: 2, z: 4, core: 2. Of those that a mesh axis runs over, the one named last changes fastest.
Arguments:
- head_outputs: bfloat16 [4096, 8, 128], P(('dp', 'expert')), may hold values from -6 to 6
- out_grad: bfloat16 [4096, 4096], P(('dp', 'expert')), may hold values from -0.29882812 to 0.29882812
- gate_weights: bfloat16 [4096, 8], P(('dp', 'expert')), may hold values from 0.099609375 to 1
- route_ids: int32 [4096, 8], P(('dp', 'expert')), may hold values from 0 to 15, all different within a row; in each aligned block of 128 rows (0 to 127, 128 to 255, ...) at most 72 rows name the same one
- out_proj: bfloat16 [16, 128, 4096], P('expert'), may hold values from -0.5 to 0.5
Outputs:
- grad_head: bfloat16 [4096, 8, 128], P(('dp', 'expert'))
- grad_gate: bfloat16 [4096, 8], P(('dp', 'expert'))
- grad_proj: float32 [16, 128, 4096], P('expert', 'dp')
The draws below stay inside these ranges and needn't reach their ends.
Inputs may be any that keep to these rules, and one draw needn't show every extreme that they name: `route_ids`: each row names 8 different head experts. Within the 128 rows of one device no head expert is named by more than 72 rows, and in some devices' rows one is named by exactly 72.
All inputs are finite; a program needn't handle non-finite values.
Results may differ from the reference program's by a relative error of at most 0.0049.
Values may be sent and summed in bfloat16 or wider, within the bound.
No kernel may reach another device: no remote copies, remote signals or barrier semaphores. Data moves between devices by JAX's collectives and lax.ppermute only.
A program may use at most 128 MiB of HBM per device.

```python
import math
import jax
import jax.numpy as jnp
import numpy as np
from jax import lax

D = 4096
HD = 128
TOPK = 8
T_DEV = 128
EXPERTS = 16
TOKENS = 4096
CAP = 72
DEVICES = 32


def steps_of(own_key, dims, shards, smallest, largest):
    factor_of, own = 1.0, jax.random.fold_in(own_key, 6)
    for dim, parts in shards:
        draws = jnp.exp(jax.random.uniform(jax.random.fold_in(own, dim), (parts,), jnp.float32, smallest / len(shards), largest / len(shards)))
        factor_of = factor_of * jnp.repeat(draws, dims[dim] // parts).reshape([-1 if axis == dim else 1 for axis in range(len(dims))])
    return factor_of


def deal_out(own_key, own, number, rows, amount, top, limit, slope):
    ranking = jax.random.permutation(own_key, amount)
    packed, common = portions_of(amount, rows * top, limit, slope, True), portions_of(amount, rows * top, limit, slope, False)
    places = jnp.arange(amount)

    def named(lengths, rotation):
        used = int((lengths > 0).sum())
        fixed = max(1, used // 4)
        shifted = fixed + (places - fixed + rotation * (used - fixed)) % max(1, amount - fixed)
        return jnp.zeros((amount,), jnp.int32).at[ranking[jnp.where(places < fixed, places, shifted)]].set(jnp.asarray(lengths, jnp.int32))

    lengths = jnp.where(number % 4 == 0, named(packed, number // 4), named(common, number - number // 4 - 1))
    mixed = jax.random.permutation(jax.random.fold_in(own, 3), amount)
    source_of, sink = mixed[0:amount // 2 * 2:2], mixed[1:amount // 2 * 2:2]
    margin = jnp.minimum(lengths[source_of] - 1, limit - lengths[sink]) // 2
    margin = jnp.where((source_of == ranking[0]) | (sink == ranking[0]) | (lengths[sink] == 0), 0, jnp.maximum(margin, 0))
    shifted = jax.random.randint(jax.random.fold_in(own, 4), (amount // 2,), 0, 1 << 20) % (margin + 1)
    lengths = lengths.at[source_of].add(-shifted).at[sink].add(shifted)
    members = jnp.searchsorted(jnp.cumsum(lengths), jnp.arange(rows * top), side="right").astype(jnp.int32)
    table = members.reshape(top, rows).T
    table = table[jax.random.permutation(jax.random.fold_in(own, 1), rows)]
    rotation = jax.random.randint(jax.random.fold_in(own, 2), (rows, 1), 0, top)
    return jnp.take_along_axis(table, (jnp.arange(top)[None, :] + rotation) % top, axis=1)


def portions_of(count, total, bound, skew, full):
    portions = [(1 << 20) // math.isqrt(rank ** skew) + 1 for rank in range(1, count + 1)]
    largest = bound if full else min(bound, max(-(-total // count), total * portions[0] // sum(portions)))
    least = 1 if total - largest >= count - 1 else 0
    holding, rest = [largest] + [least] * (count - 1), total - largest - least * (count - 1)
    while rest > 0:
        free = [i for i in range(1, count) if holding[i] < largest] or [i for i in range(1, count) if holding[i] < bound]
        whole, left = sum([portions[i] for i in free]), rest
        for i in free:
            extra = min(bound - holding[i], max(1, left * portions[i] // whole), rest)
            holding[i] = holding[i] + extra
            rest = rest - extra
    return np.array(holding)


def noise(key, extent, deviation, bound, cuts=(), kind=jnp.bfloat16):
    entries = deviation * jax.random.normal(key, extent, jnp.float32)
    if cuts:
        entries = entries * steps_of(key, extent, cuts, -0.22, 0.18)
    return jnp.clip(entries, -bound, bound).astype(kind)


def setup_inputs(seed: int = 0) -> dict:
    keys = jax.random.split(jax.random.key(seed), 6)
    head_outputs = noise(keys[0], (TOKENS, TOPK, HD), 1.0, 6.0, ((0, 32),))
    out_grad = noise(keys[1], (TOKENS, D), 0.05, 0.29882812, ((0, 32),))
    gate_weights = jnp.clip(0.099609375 + 0.9003906 * jax.random.uniform(keys[2], (TOKENS, TOPK), jnp.float32) ** steps_of(keys[2], (TOKENS, TOPK), ((0, 32),), -0.2, 0.2), 0.099609375, 1.0).astype(jnp.bfloat16)
    route_ids_keys = jax.random.split(jax.random.fold_in(keys[3], 1), TOKENS // T_DEV)
    route_ids_turns = jax.random.permutation(jax.random.fold_in(keys[3], 3), TOKENS // T_DEV)
    route_ids = jax.vmap(lambda own, number: deal_out(jax.random.fold_in(keys[3], 2), own, number, T_DEV, EXPERTS, TOPK, CAP, 2))(route_ids_keys, route_ids_turns).reshape((TOKENS, TOPK))
    out_proj = noise(keys[4], (EXPERTS, HD, D), HD ** -0.5, 0.5, ((0, 16),))
    return dict(head_outputs=head_outputs, out_grad=out_grad, gate_weights=gate_weights, route_ids=route_ids, out_proj=out_proj)


soft_cap = 1.5


def reference(head_outputs, out_grad, gate_weights, route_ids, out_proj):
    pair_count = TOKENS * TOPK
    local_pairs = T_DEV * TOPK
    slot_total = DEVICES * CAP
    flat_routes = route_ids.reshape(pair_count)
    one_hot = (flat_routes[:, None] == jnp.arange(EXPERTS, dtype=jnp.int32)[None, :]).astype(jnp.int32)
    one_hot = one_hot.reshape(DEVICES, local_pairs, EXPERTS)
    before = jnp.cumsum(one_hot, axis=1) - one_hot
    position = jnp.sum(before * one_hot, axis=2).reshape(pair_count).astype(jnp.int32)
    device_of = (jnp.arange(pair_count, dtype=jnp.int32) // local_pairs).astype(jnp.int32)
    target = (flat_routes * slot_total + device_of * CAP + position).astype(jnp.int32)
    slot_table = jnp.full((EXPERTS * slot_total,), pair_count, jnp.int32)
    slot_table = slot_table.at[target].set(jnp.arange(pair_count, dtype=jnp.int32)).reshape(EXPERTS, slot_total)
    heads_flat = head_outputs.reshape(pair_count, HD)
    gates_flat = gate_weights.reshape(pair_count)

    def one_expert(expert_item):
        slot_index, weight = expert_item
        grad_rows = jnp.take(out_grad, slot_index // TOPK, axis=0, mode="fill", fill_value=0)
        head_rows = jnp.take(heads_flat, slot_index, axis=0, mode="fill", fill_value=0)
        gate_rows = jnp.take(gates_flat, slot_index, axis=0, mode="fill", fill_value=0)
        pre_cap = jnp.dot(head_rows, weight, preferred_element_type=jnp.float32)
        capped = jnp.tanh(pre_cap / soft_cap)
        grad_pre = (gate_rows[:, None].astype(jnp.float32) * grad_rows.astype(jnp.float32) * (1.0 - capped * capped)).astype(jnp.bfloat16)
        head_grad = jnp.dot(grad_pre, weight.T, preferred_element_type=jnp.float32).astype(jnp.bfloat16)
        gate_grad = jnp.sum(grad_rows.astype(jnp.float32) * (soft_cap * capped), axis=1).astype(jnp.bfloat16)
        weight_grad = jnp.dot(head_rows.T, grad_pre, preferred_element_type=jnp.float32)
        return head_grad, gate_grad, weight_grad

    head_grads, gate_grads, grad_proj = lax.map(one_expert, (slot_table, out_proj))
    flat_table = slot_table.reshape(EXPERTS * slot_total)
    grad_head = jnp.zeros((pair_count, HD), jnp.bfloat16).at[flat_table].set(head_grads.reshape(EXPERTS * slot_total, HD), mode="drop")
    grad_gate = jnp.zeros((pair_count,), jnp.bfloat16).at[flat_table].set(gate_grads.reshape(EXPERTS * slot_total), mode="drop")
    return grad_head.reshape(TOKENS, TOPK, HD), grad_gate.reshape(TOKENS, TOPK), grad_proj
```

```python
import functools

import jax
import jax.numpy as jnp
from jax import lax
from jax.experimental import pallas as pl
from jax.experimental.pallas import tpu as pltpu
from jax.sharding import PartitionSpec as P

soft_cap = 1.5
AXES = ("dp", "expert")
GROUP = 4
LANES = 128


class Plan:
    def __init__(self, mesh, tokens, top, head_dim, features):
        self.dp = mesh.shape["dp"]
        self.experts = mesh.shape["expert"]
        self.rows = GROUP // 2
        self.planes = self.experts // GROUP
        self.splits = self.dp * self.rows
        self.sources = self.splits * 2
        self.tokens, self.top, self.head_dim = tokens, top, head_dim
        self.part = features // self.splits
        cap = 9 * tokens * top // (8 * self.experts)
        self.cap = -(-cap // 8) * 8
        self.back = self.rows * self.cap + 16
        self.width = self.part + top * head_dim + LANES

    def index(self, x, z, y, c):
        return x * self.experts + z * GROUP + y * 2 + c

    def pairs(self, dx=0, dz=0, dy=0, dc=0):
        out = []
        for x in range(self.dp):
            for z in range(self.planes):
                for y in range(self.rows):
                    for c in range(2):
                        target = self.index(
                            (x + dx) % self.dp,
                            (z + dz) % self.planes,
                            (y + dy) % self.rows,
                            c ^ dc,
                        )
                        out.append((self.index(x, z, y, c), target))
        return out

    def shift(self, value, **by):
        if not any(by.values()):
            return value
        return lax.ppermute(value, AXES, self.pairs(**by))

    def splits_list(self):
        return [(dx, dy) for dx in range(self.dp) for dy in range(self.rows)]


def slot_kernel(plan, ids, *refs):
    packs = refs[: plan.sources]
    w_ref, p_ref, back_ref, buf, grads, heads, sems = refs[plan.sources :]
    tokens, cap, part, top, head_dim = plan.tokens, plan.cap, plan.part, plan.top, plan.head_dim
    pair_rows = 2 * cap
    pair_total = plan.sources // 2

    def copies(q):
        slot = q % 2
        return [
            pltpu.make_async_copy(
                packs[2 * q + b], buf.at[slot, pl.ds(b * tokens, tokens), :], sems.at[slot, b]
            )
            for b in range(2)
        ]

    for copy in copies(0):
        copy.start()
    row_of = lax.broadcasted_iota(jnp.int32, (cap, tokens), 0)
    lane_of = lax.broadcasted_iota(jnp.int32, (cap, tokens), 1)
    diagonal = (row_of == lane_of).astype(jnp.float32)
    before = (
        lax.broadcasted_iota(jnp.int32, (tokens, tokens), 0)
        < lax.broadcasted_iota(jnp.int32, (tokens, tokens), 1)
    ).astype(jnp.bfloat16)
    block_row = lax.broadcasted_iota(jnp.int32, (16, LANES), 0)
    chunk = min(part, 512)
    for q in range(pair_total):
        slot = q % 2
        if q + 1 < pair_total:
            for copy in copies(q + 1):
                copy.start()
        for copy in copies(q):
            copy.wait()
        masks, gate_rows, occupied = {}, {}, []
        for b in range(2):
            meta = buf[slot, pl.ds(b * tokens, 16), pl.ds(part + top * head_dim, LANES)].astype(
                jnp.float32
            )
            for i in range(plan.rows):
                mask = (meta[top : 2 * top] == ids[i].astype(jnp.float32)).astype(jnp.float32)
                masks[i, b] = mask
                gate_rows[i, b] = jnp.sum(mask * meta[:top], axis=0, keepdims=True)
                occupied.append(jnp.sum(mask, axis=0, keepdims=True))
        count = len(occupied)
        padded = jnp.concatenate(
            occupied + [jnp.zeros((-count % 16, tokens), jnp.float32)] * (count % 16 > 0), axis=0
        )
        places = jnp.dot(
            padded.astype(jnp.bfloat16), before, preferred_element_type=jnp.float32
        )
        ones, gates = [], []
        for i in range(plan.rows):
            halves, columns = [], []
            for b in range(2):
                at = b * plan.rows + i
                place = places[at : at + 1].astype(jnp.int32)
                hot = jnp.where(row_of == place, occupied[at], 0.0)
                columns.append(jnp.sum(hot * gate_rows[i, b], axis=1, keepdims=True))
                pieces = [(hot * masks[i, b][k : k + 1]).astype(jnp.bfloat16) for k in range(top)]
                wide = jnp.concatenate(pieces, axis=1)
                raw = jnp.concatenate(
                    [
                        buf[slot, pl.ds(b * tokens, tokens), pl.ds(part + k * head_dim, head_dim)]
                        for k in range(top)
                    ],
                    axis=0,
                )
                chosen = jnp.dot(wide, raw, preferred_element_type=jnp.float32)
                halves.append((hot, chosen))
            empty = jnp.zeros((cap, tokens), jnp.float32)
            ones.append(
                jnp.concatenate(
                    [
                        jnp.concatenate([halves[0][0], empty], axis=1),
                        jnp.concatenate([empty, halves[1][0]], axis=1),
                    ],
                    axis=0,
                ).astype(jnp.bfloat16)
            )
            gates.append(jnp.concatenate(columns, axis=0))
            heads[i, pl.ds(q * pair_rows, pair_rows), :] = jnp.concatenate(
                [halves[0][1], halves[1][1]], axis=0
            ).astype(jnp.bfloat16)
        all_ones = jnp.concatenate(ones, axis=0)
        sums = [jnp.zeros((pair_rows, 1), jnp.float32) for _ in range(plan.rows)]
        for start in range(0, part, chunk):
            grad = jnp.dot(
                all_ones, buf[slot, :, pl.ds(start, chunk)], preferred_element_type=jnp.float32
            )
            for i in range(plan.rows):
                grad_block = grad[i * pair_rows : (i + 1) * pair_rows]
                weight = w_ref[pl.ds(pl.multiple_of(ids[plan.rows + i], 128), head_dim), pl.ds(start, chunk)]
                pre = jnp.dot(
                    heads[i, pl.ds(q * pair_rows, pair_rows), :],
                    weight,
                    preferred_element_type=jnp.float32,
                )
                capped = jnp.tanh(pre * (1.0 / soft_cap))
                sums[i] = sums[i] + jnp.sum(grad_block * capped, axis=1, keepdims=True)
                grads[i, pl.ds(q * pair_rows, pair_rows), pl.ds(start, chunk)] = (
                    gates[i] * grad_block * (1.0 - capped * capped)
                ).astype(jnp.bfloat16)
        for b in range(2):
            block = jnp.zeros((16, LANES), jnp.float32)
            for i in range(plan.rows):
                column = soft_cap * sums[i][b * cap : (b + 1) * cap]
                line = jnp.sum(diagonal * column, axis=0, keepdims=True)
                block = jnp.where(block_row == i, line, block)
            back_ref[2 * q + b, pl.ds(plan.rows * cap, 16), :] = block.astype(jnp.bfloat16)
    for i in range(plan.rows):
        weight = w_ref[pl.ds(pl.multiple_of(ids[plan.rows + i], 128), head_dim), :]
        grad_all = grads[i]
        p_ref[pl.ds(i * head_dim, head_dim), :] = lax.dot_general(
            heads[i], grad_all, (((0,), (0,)), ((), ())), preferred_element_type=jnp.float32
        ).astype(p_ref.dtype)
        rows = lax.dot_general(
            grad_all, weight, (((1,), (1,)), ((), ())), preferred_element_type=jnp.float32
        ).astype(jnp.bfloat16)
        for s in range(plan.sources):
            back_ref[s, pl.ds(i * cap, cap), :] = rows[s * cap : (s + 1) * cap]


def slot_work(plan, ids, packs, weight, kind):
    rows = plan.sources * plan.cap
    flops = 6 * plan.rows * rows * plan.head_dim * plan.part
    return pl.pallas_call(
        functools.partial(slot_kernel, plan),
        out_shape=(
            jax.ShapeDtypeStruct((plan.rows * plan.head_dim, plan.part), kind),
            jax.ShapeDtypeStruct((plan.sources, plan.back, LANES), jnp.bfloat16),
        ),
        in_specs=[pl.BlockSpec(memory_space=pltpu.SMEM)]
        + [pl.BlockSpec(memory_space=pl.ANY)] * plan.sources
        + [pl.BlockSpec(memory_space=pltpu.VMEM)],
        out_specs=(
            pl.BlockSpec(memory_space=pltpu.VMEM),
            pl.BlockSpec(memory_space=pltpu.VMEM),
        ),
        scratch_shapes=[
            pltpu.VMEM((2, 2 * plan.tokens, plan.width), jnp.bfloat16),
            pltpu.VMEM((plan.rows, rows, plan.part), jnp.bfloat16),
            pltpu.VMEM((plan.rows, rows, plan.head_dim), jnp.bfloat16),
            pltpu.SemaphoreType.DMA((2, 2)),
        ],
        compiler_params=pltpu.CompilerParams(vmem_limit_bytes=32 * 1024 * 1024),
        cost_estimate=pl.CostEstimate(
            flops=flops,
            bytes_accessed=plan.sources * plan.tokens * plan.width * 2,
            transcendentals=plan.rows * rows * plan.part,
        ),
    )(ids, *packs, weight)


def final_kernel(plan, target_ref, gate_ref, place_ref, *refs):
    parts = refs[: plan.sources]
    head_ref, out_gate_ref, table = refs[plan.sources :]
    length = plan.planes * plan.back
    for dc in range(2):
        total = None
        for s in range(plan.splits):
            piece = parts[2 * s + dc][...].astype(jnp.float32)
            total = piece if total is None else total + piece
        table[pl.ds(dc * length, length), :] = total.astype(jnp.bfloat16)
    block = 256
    count = plan.tokens * plan.top
    for start in range(0, count, block):
        slot_of = lax.broadcasted_iota(jnp.int32, (block, 2 * length), 1)
        hot = (slot_of == target_ref[pl.ds(start, block), :]).astype(jnp.bfloat16)
        head_ref[pl.ds(start, block), :] = jnp.dot(
            hot, table[...], preferred_element_type=jnp.float32
        ).astype(jnp.bfloat16)
        hot = (slot_of == gate_ref[pl.ds(start, block), :]).astype(jnp.bfloat16)
        lines = jnp.dot(hot, table[...], preferred_element_type=jnp.float32)
        lane_of = lax.broadcasted_iota(jnp.int32, (block, LANES), 1)
        out_gate_ref[pl.ds(start, block), :] = jnp.sum(
            jnp.where(lane_of == place_ref[pl.ds(start, block), :], lines, 0.0),
            axis=1,
            keepdims=True,
        )


def final_work(plan, target, gate_line, place, parts):
    count = plan.tokens * plan.top
    return pl.pallas_call(
        functools.partial(final_kernel, plan),
        out_shape=(
            jax.ShapeDtypeStruct((count, plan.head_dim), jnp.bfloat16),
            jax.ShapeDtypeStruct((count, 1), jnp.float32),
        ),
        in_specs=[pl.BlockSpec(memory_space=pltpu.VMEM)] * (3 + plan.sources),
        out_specs=(
            pl.BlockSpec(memory_space=pltpu.VMEM),
            pl.BlockSpec(memory_space=pltpu.VMEM),
        ),
        scratch_shapes=[pltpu.VMEM((2 * plan.planes * plan.back, LANES), jnp.bfloat16)],
        compiler_params=pltpu.CompilerParams(vmem_limit_bytes=48 * 1024 * 1024),
    )(target, gate_line, place, *parts)


def local(mesh, head_outputs, out_grad, gate_weights, route_ids, out_proj):
    tokens, top, head_dim = head_outputs.shape
    features = out_grad.shape[1]
    plan = Plan(mesh, tokens, top, head_dim, features)
    x = lax.axis_index("dp")
    me = lax.axis_index("expert")
    z, y, c = me // GROUP, (me % GROUP) // 2, me % 2

    flat_heads = head_outputs.reshape(tokens, top * head_dim)
    meta = jnp.concatenate(
        [
            gate_weights.T,
            route_ids.T.astype(jnp.bfloat16),
            jnp.zeros((LANES - 2 * top, tokens), jnp.bfloat16),
        ],
        axis=0,
    )

    def pack(dx, dy):
        split = ((x + dx) % plan.dp) * plan.rows + (y + dy) % plan.rows
        piece = lax.dynamic_slice_in_dim(out_grad, split * plan.part, plan.part, 1)
        return jnp.concatenate([piece, flat_heads, meta], axis=1)

    near = [plan.shift(pack(dx, dy), dx=dx, dy=dy) for dx, dy in plan.splits_list()]
    packs = []
    for value in near:
        packs += [value, plan.shift(value, dc=1)]

    weight_parts = []
    for dy in range(plan.rows):
        split = x * plan.rows + (y + dy) % plan.rows
        piece = lax.dynamic_slice_in_dim(out_proj[0], split * plan.part, plan.part, 1)
        weight_parts.append(plan.shift(piece, dy=dy))
    own_weights = jnp.concatenate(weight_parts, axis=0)
    weights = [plan.shift(own_weights, dz=-k % plan.planes) for k in range(plan.planes)]

    rows_at = jnp.arange(plan.rows, dtype=jnp.int32)
    weight_at = ((y - rows_at) % plan.rows) * head_dim
    projections, backs = [None] * plan.planes, [None] * plan.planes
    order = list(range(1, plan.planes)) + [0]
    for k in order:
        expert_ids = ((z + k) % plan.planes) * GROUP + rows_at * 2 + c
        ids = jnp.concatenate([expert_ids, weight_at]).astype(jnp.int32)
        kind = jnp.float32 if k == 0 else jnp.bfloat16
        projections[k], backs[k] = slot_work(plan, ids, packs, weights[k], kind)

    total = projections[0]
    for k in range(1, plan.planes):
        total = total + plan.shift(projections[k], dz=k).astype(jnp.float32)
    own_rows = head_dim // plan.dp
    grad_proj = jnp.zeros((own_rows, features), jnp.float32)
    for dx, dy in plan.splits_list():
        start = ((y + dy) % plan.rows) * head_dim + ((x + dx) % plan.dp) * own_rows
        piece = lax.dynamic_slice_in_dim(total, start, own_rows, 0)
        if dx or dy:
            piece = plan.shift(piece.astype(jnp.bfloat16), dx=dx, dy=dy).astype(jnp.float32)
        split = ((x - dx) % plan.dp) * plan.rows + (y - dy) % plan.rows
        grad_proj = lax.dynamic_update_slice_in_dim(grad_proj, piece, split * plan.part, 1)

    parts = []
    source = 0
    for dx, dy in plan.splits_list():
        for dc in range(2):
            rows = jnp.concatenate([backs[k][source] for k in range(plan.planes)], axis=0)
            parts.append(
                plan.shift(rows, dx=-dx % plan.dp, dy=-dy % plan.rows, dc=dc)
            )
            source += 1
    routes = route_ids.reshape(tokens * top)
    hot = (routes[:, None] == jnp.arange(plan.experts, dtype=jnp.int32)[None, :]).astype(jnp.float32)
    per_token = hot.reshape(tokens, top, plan.experts).sum(axis=1)
    earlier = jnp.tril(jnp.ones((tokens, tokens), jnp.float32), -1)
    places = jnp.dot(earlier, per_token)
    place = jnp.sum(
        hot.reshape(tokens, top, plan.experts) * places[:, None, :], axis=2
    ).astype(jnp.int32).reshape(tokens * top)
    plane = (routes // GROUP - z) % plan.planes
    row = (routes % GROUP) // 2
    side = (routes % 2) ^ c
    base = side * (plan.planes * plan.back) + plane * plan.back
    target = base + row * plan.cap + place
    gate_line = base + plan.rows * plan.cap + row
    grad_head, grad_gate = final_work(
        plan, target[:, None], gate_line[:, None], place[:, None], parts
    )
    return (
        grad_head.reshape(tokens, top, head_dim),
        grad_gate.reshape(tokens, top).astype(jnp.bfloat16),
        grad_proj[None],
    )


def solution(mesh):
    return jax.shard_map(
        functools.partial(local, mesh),
        mesh=mesh,
        in_specs=(
            P(("dp", "expert"), None, None),
            P(("dp", "expert"), None),
            P(("dp", "expert"), None),
            P(("dp", "expert"), None),
            P("expert", None, None),
        ),
        out_specs=(
            P(("dp", "expert"), None, None),
            P(("dp", "expert"), None),
            P("expert", "dp", None),
        ),
        check_vma=False,
    )
```

```python
import functools

import jax
import jax.numpy as jnp
from jax import lax
from jax.experimental import pallas as pl
from jax.experimental.pallas import tpu as pltpu
from jax.sharding import PartitionSpec as P

soft_cap = 1.5
AXES = ("dp", "expert")
GROUP = 4
LANES = 128


class Plan:
    def __init__(self, mesh, tokens, top, head_dim, features):
        self.dp = mesh.shape["dp"]
        self.experts = mesh.shape["expert"]
        self.rows = GROUP // 2
        self.planes = self.experts // GROUP
        self.splits = self.dp * self.rows
        self.sources = self.splits * 2
        self.tokens, self.top, self.head_dim = tokens, top, head_dim
        self.part = features // self.splits
        cap = 9 * tokens * top // (8 * self.experts)
        self.cap = -(-cap // 8) * 8
        self.back = self.rows * self.cap + 16
        self.width = self.part + top * head_dim + LANES

    def index(self, x, z, y, c):
        return x * self.experts + z * GROUP + y * 2 + c

    def pairs(self, dx=0, dz=0, dy=0, dc=0):
        out = []
        for x in range(self.dp):
            for z in range(self.planes):
                for y in range(self.rows):
                    for c in range(2):
                        target = self.index(
                            (x + dx) % self.dp,
                            (z + dz) % self.planes,
                            (y + dy) % self.rows,
                            c ^ dc,
                        )
                        out.append((self.index(x, z, y, c), target))
        return out

    def shift(self, value, **by):
        if not any(by.values()):
            return value
        return lax.ppermute(value, AXES, self.pairs(**by))

    def along(self, value, moves):
        out = []
        for x in range(self.dp):
            for a, b in moves:
                for r in range(GROUP):
                    out.append((self.index(x, a, 0, 0) + r, self.index(x, b, 0, 0) + r))
        return lax.ppermute(value, AXES, out)

    def splits_list(self):
        return [(dx, dy) for dx in range(self.dp) for dy in range(self.rows)]


def slot_kernel(plan, ids, *refs):
    packs = refs[: plan.sources]
    w_ref, p_ref, back_ref, buf, grads, heads, sems = refs[plan.sources :]
    tokens, cap, part, top, head_dim = plan.tokens, plan.cap, plan.part, plan.top, plan.head_dim
    pair_rows = 2 * cap
    pair_total = plan.sources // 2

    def copies(q):
        slot = q % 2
        return [
            pltpu.make_async_copy(
                packs[2 * q + b], buf.at[slot, pl.ds(b * tokens, tokens), :], sems.at[slot, b]
            )
            for b in range(2)
        ]

    for copy in copies(0):
        copy.start()
    row_of = lax.broadcasted_iota(jnp.int32, (cap, tokens), 0)
    lane_of = lax.broadcasted_iota(jnp.int32, (cap, tokens), 1)
    diagonal = (row_of == lane_of).astype(jnp.float32)
    before = (
        lax.broadcasted_iota(jnp.int32, (tokens, tokens), 0)
        < lax.broadcasted_iota(jnp.int32, (tokens, tokens), 1)
    ).astype(jnp.bfloat16)
    block_row = lax.broadcasted_iota(jnp.int32, (16, LANES), 0)
    chunk = min(part, 512)
    for q in range(pair_total):
        slot = q % 2
        if q + 1 < pair_total:
            for copy in copies(q + 1):
                copy.start()
        for copy in copies(q):
            copy.wait()
        masks, gate_rows, occupied = {}, {}, []
        for b in range(2):
            meta = buf[slot, pl.ds(b * tokens, 16), pl.ds(part + top * head_dim, LANES)].astype(
                jnp.float32
            )
            for i in range(plan.rows):
                mask = (meta[top : 2 * top] == ids[i].astype(jnp.float32)).astype(jnp.float32)
                masks[i, b] = mask
                gate_rows[i, b] = jnp.sum(mask * meta[:top], axis=0, keepdims=True)
                occupied.append(jnp.sum(mask, axis=0, keepdims=True))
        count = len(occupied)
        padded = jnp.concatenate(
            occupied + [jnp.zeros((-count % 16, tokens), jnp.float32)] * (count % 16 > 0), axis=0
        )
        places = jnp.dot(
            padded.astype(jnp.bfloat16), before, preferred_element_type=jnp.float32
        )
        ones, gates = [], []
        for i in range(plan.rows):
            halves, columns = [], []
            for b in range(2):
                at = b * plan.rows + i
                place = places[at : at + 1].astype(jnp.int32)
                hot = jnp.where(row_of == place, occupied[at], 0.0)
                columns.append(jnp.sum(hot * gate_rows[i, b], axis=1, keepdims=True))
                pieces = [(hot * masks[i, b][k : k + 1]).astype(jnp.bfloat16) for k in range(top)]
                wide = jnp.concatenate(pieces, axis=1)
                raw = jnp.concatenate(
                    [
                        buf[slot, pl.ds(b * tokens, tokens), pl.ds(part + k * head_dim, head_dim)]
                        for k in range(top)
                    ],
                    axis=0,
                )
                chosen = jnp.dot(wide, raw, preferred_element_type=jnp.float32)
                halves.append((hot, chosen))
            empty = jnp.zeros((cap, tokens), jnp.float32)
            ones.append(
                jnp.concatenate(
                    [
                        jnp.concatenate([halves[0][0], empty], axis=1),
                        jnp.concatenate([empty, halves[1][0]], axis=1),
                    ],
                    axis=0,
                ).astype(jnp.bfloat16)
            )
            gates.append(jnp.concatenate(columns, axis=0))
            heads[i, pl.ds(q * pair_rows, pair_rows), :] = jnp.concatenate(
                [halves[0][1], halves[1][1]], axis=0
            ).astype(jnp.bfloat16)
        all_ones = jnp.concatenate(ones, axis=0)
        sums = [jnp.zeros((pair_rows, 1), jnp.float32) for _ in range(plan.rows)]
        for start in range(0, part, chunk):
            grad = jnp.dot(
                all_ones, buf[slot, :, pl.ds(start, chunk)], preferred_element_type=jnp.float32
            )
            for i in range(plan.rows):
                grad_block = grad[i * pair_rows : (i + 1) * pair_rows]
                weight = w_ref[pl.ds(pl.multiple_of(ids[plan.rows + i], 128), head_dim), pl.ds(start, chunk)]
                pre = jnp.dot(
                    heads[i, pl.ds(q * pair_rows, pair_rows), :],
                    weight,
                    preferred_element_type=jnp.float32,
                )
                capped = jnp.tanh(pre * (1.0 / soft_cap))
                sums[i] = sums[i] + jnp.sum(grad_block * capped, axis=1, keepdims=True)
                grads[i, pl.ds(q * pair_rows, pair_rows), pl.ds(start, chunk)] = (
                    gates[i] * grad_block * (1.0 - capped * capped)
                ).astype(jnp.bfloat16)
        for b in range(2):
            block = jnp.zeros((16, LANES), jnp.float32)
            for i in range(plan.rows):
                column = soft_cap * sums[i][b * cap : (b + 1) * cap]
                line = jnp.sum(diagonal * column, axis=0, keepdims=True)
                block = jnp.where(block_row == i, line, block)
            back_ref[2 * q + b, pl.ds(plan.rows * cap, 16), :] = block.astype(jnp.bfloat16)
    for i in range(plan.rows):
        weight = w_ref[pl.ds(pl.multiple_of(ids[plan.rows + i], 128), head_dim), :]
        grad_all = grads[i]
        p_ref[pl.ds(i * head_dim, head_dim), :] = lax.dot_general(
            heads[i], grad_all, (((0,), (0,)), ((), ())), preferred_element_type=jnp.float32
        ).astype(p_ref.dtype)
        rows = lax.dot_general(
            grad_all, weight, (((1,), (1,)), ((), ())), preferred_element_type=jnp.float32
        ).astype(jnp.bfloat16)
        for s in range(plan.sources):
            back_ref[s, pl.ds(i * cap, cap), :] = rows[s * cap : (s + 1) * cap]


def slot_work(plan, ids, packs, weight, kind):
    rows = plan.sources * plan.cap
    return pl.pallas_call(
        functools.partial(slot_kernel, plan),
        out_shape=(
            jax.ShapeDtypeStruct((plan.rows * plan.head_dim, plan.part), kind),
            jax.ShapeDtypeStruct((plan.sources, plan.back, LANES), jnp.bfloat16),
        ),
        in_specs=[pl.BlockSpec(memory_space=pltpu.SMEM)]
        + [pl.BlockSpec(memory_space=pl.ANY)] * plan.sources
        + [pl.BlockSpec(memory_space=pltpu.VMEM)],
        out_specs=(
            pl.BlockSpec(memory_space=pltpu.VMEM),
            pl.BlockSpec(memory_space=pltpu.VMEM),
        ),
        scratch_shapes=[
            pltpu.VMEM((2, 2 * plan.tokens, plan.width), jnp.bfloat16),
            pltpu.VMEM((plan.rows, rows, plan.part), jnp.bfloat16),
            pltpu.VMEM((plan.rows, rows, plan.head_dim), jnp.bfloat16),
            pltpu.SemaphoreType.DMA((2, 2)),
        ],
        compiler_params=pltpu.CompilerParams(vmem_limit_bytes=32 * 1024 * 1024),
    )(ids, *packs, weight)


def final_kernel(plan, target_ref, gate_ref, place_ref, *refs):
    parts = refs[: plan.sources]
    head_ref, out_gate_ref, table = refs[plan.sources :]
    length = plan.planes * plan.back
    for dc in range(2):
        total = None
        for s in range(plan.splits):
            piece = parts[2 * s + dc][...].astype(jnp.float32)
            total = piece if total is None else total + piece
        table[pl.ds(dc * length, length), :] = total.astype(jnp.bfloat16)
    block = 256
    count = plan.tokens * plan.top
    for start in range(0, count, block):
        slot_of = lax.broadcasted_iota(jnp.int32, (block, 2 * length), 1)
        hot = (slot_of == target_ref[pl.ds(start, block), :]).astype(jnp.bfloat16)
        head_ref[pl.ds(start, block), :] = jnp.dot(
            hot, table[...], preferred_element_type=jnp.float32
        ).astype(jnp.bfloat16)
        hot = (slot_of == gate_ref[pl.ds(start, block), :]).astype(jnp.bfloat16)
        lines = jnp.dot(hot, table[...], preferred_element_type=jnp.float32)
        lane_of = lax.broadcasted_iota(jnp.int32, (block, LANES), 1)
        out_gate_ref[pl.ds(start, block), :] = jnp.sum(
            jnp.where(lane_of == place_ref[pl.ds(start, block), :], lines, 0.0),
            axis=1,
            keepdims=True,
        )


def final_work(plan, target, gate_line, place, parts):
    count = plan.tokens * plan.top
    return pl.pallas_call(
        functools.partial(final_kernel, plan),
        out_shape=(
            jax.ShapeDtypeStruct((count, plan.head_dim), jnp.bfloat16),
            jax.ShapeDtypeStruct((count, 1), jnp.float32),
        ),
        in_specs=[pl.BlockSpec(memory_space=pltpu.VMEM)] * (3 + plan.sources),
        out_specs=(
            pl.BlockSpec(memory_space=pltpu.VMEM),
            pl.BlockSpec(memory_space=pltpu.VMEM),
        ),
        scratch_shapes=[pltpu.VMEM((2 * plan.planes * plan.back, LANES), jnp.bfloat16)],
        compiler_params=pltpu.CompilerParams(vmem_limit_bytes=48 * 1024 * 1024),
    )(target, gate_line, place, *parts)


def local(mesh, head_outputs, out_grad, gate_weights, route_ids, out_proj):
    tokens, top, head_dim = head_outputs.shape
    features = out_grad.shape[1]
    plan = Plan(mesh, tokens, top, head_dim, features)
    x = lax.axis_index("dp")
    me = lax.axis_index("expert")
    z, y, c = me // GROUP, (me % GROUP) // 2, me % 2

    flat_heads = head_outputs.reshape(tokens, top * head_dim)
    meta = jnp.concatenate(
        [
            gate_weights.T,
            route_ids.T.astype(jnp.bfloat16),
            jnp.zeros((LANES - 2 * top, tokens), jnp.bfloat16),
        ],
        axis=0,
    )

    def pack(dx, dy):
        split = ((x + dx) % plan.dp) * plan.rows + (y + dy) % plan.rows
        piece = lax.dynamic_slice_in_dim(out_grad, split * plan.part, plan.part, 1)
        return jnp.concatenate([piece, flat_heads, meta], axis=1)

    near = [plan.shift(pack(dx, dy), dx=dx, dy=dy) for dx, dy in plan.splits_list()]
    packs = []
    for value in near:
        packs += [value, plan.shift(value, dc=1)]

    weight_parts = []
    for dy in range(plan.rows):
        split = x * plan.rows + (y + dy) % plan.rows
        piece = lax.dynamic_slice_in_dim(out_proj[0], split * plan.part, plan.part, 1)
        weight_parts.append(plan.shift(piece, dy=dy))
    own_weights = jnp.concatenate(weight_parts, axis=0)
    rows_at = jnp.arange(plan.rows, dtype=jnp.int32)
    weight_at = ((y - rows_at) % plan.rows) * head_dim

    def work(plane, weight, kind, after=None):
        ids = jnp.concatenate([plane * GROUP + rows_at * 2 + c, weight_at]).astype(jnp.int32)
        if after is not None:
            ids, _ = lax.optimization_barrier((ids, after))
        return slot_work(plan, ids, packs, weight, kind)

    if plan.planes == 4:
        inner = (z == 1) | (z == 2)
        mates, middle = [(0, 1), (1, 0), (2, 3), (3, 2)], [(1, 2), (2, 1)]
        outward, inward, across = [(1, 0), (2, 3)], [(0, 1), (3, 2)], [(1, 3), (2, 0)]
        at = {"own": z, "mate": z ^ 1, "near": jnp.where(z < 2, 2, 1), "far": jnp.where(z < 2, 3, 0)}
        weights = {"own": own_weights, "mate": plan.along(own_weights, mates)}
        near_in = plan.along(own_weights, middle)
        near_out = plan.along(near_in, outward)
        far_in = plan.along(weights["mate"], middle)
        far_out = plan.along(far_in, outward)
        weights["near"] = jnp.where(inner, near_in, near_out)
        weights["far"] = jnp.where(inner, far_in, far_out)
        sums, back_at, back = {}, {}, None
        for name in ("near", "far", "mate", "own"):
            kind = jnp.float32 if name == "own" else jnp.bfloat16
            sums[name], back = work(at[name], weights[name], kind, back)
            back_at[name] = back
        near_sum = sums["near"] + plan.along(sums["near"], inward)
        far_sum = sums["far"] + plan.along(sums["far"], inward)
        total = (
            sums["own"]
            + plan.along(sums["mate"], mates).astype(jnp.float32)
            + plan.along(near_sum, middle).astype(jnp.float32)
            + plan.along(far_sum, across).astype(jnp.float32)
        )
        names = ("own", "mate", "near", "far")
        backs = [back_at[name] for name in names]
        backs, _ = lax.optimization_barrier((backs, (near_sum, far_sum)))
        plane_of = jnp.stack([at[name] for name in names])
    else:
        backs, total = [], None
        for k in range(plan.planes):
            weight = plan.shift(own_weights, dz=-k % plan.planes)
            part, back = work((z + k) % plan.planes, weight, jnp.bfloat16 if k else jnp.float32)
            backs.append(back)
            part = plan.shift(part, dz=k).astype(jnp.float32)
            total = part if total is None else total + part
        plane_of = (z + jnp.arange(plan.planes, dtype=jnp.int32)) % plan.planes

    own_rows = head_dim // plan.dp
    grad_proj = jnp.zeros((own_rows, features), jnp.float32)
    for dx, dy in plan.splits_list():
        start = ((y + dy) % plan.rows) * head_dim + ((x + dx) % plan.dp) * own_rows
        piece = lax.dynamic_slice_in_dim(total, start, own_rows, 0)
        if dx or dy:
            piece = plan.shift(piece.astype(jnp.bfloat16), dx=dx, dy=dy).astype(jnp.float32)
        split = ((x - dx) % plan.dp) * plan.rows + (y - dy) % plan.rows
        grad_proj = lax.dynamic_update_slice_in_dim(grad_proj, piece, split * plan.part, 1)

    parts = []
    source = 0
    for dx, dy in plan.splits_list():
        for dc in range(2):
            rows = jnp.concatenate([backs[k][source] for k in range(plan.planes)], axis=0)
            parts.append(
                plan.shift(rows, dx=-dx % plan.dp, dy=-dy % plan.rows, dc=dc)
            )
            source += 1
    routes = route_ids.reshape(tokens * top)
    hot = (routes[:, None] == jnp.arange(plan.experts, dtype=jnp.int32)[None, :]).astype(jnp.float32)
    per_token = hot.reshape(tokens, top, plan.experts).sum(axis=1)
    earlier = jnp.tril(jnp.ones((tokens, tokens), jnp.float32), -1)
    places = jnp.dot(earlier, per_token)
    place = jnp.sum(
        hot.reshape(tokens, top, plan.experts) * places[:, None, :], axis=2
    ).astype(jnp.int32).reshape(tokens * top)
    slots = jnp.arange(plan.planes, dtype=jnp.int32)
    plane = jnp.sum(
        jnp.where((routes // GROUP)[:, None] == plane_of[None, :], slots[None, :], 0), axis=1
    )
    row = (routes % GROUP) // 2
    side = (routes % 2) ^ c
    base = side * (plan.planes * plan.back) + plane * plan.back
    target = base + row * plan.cap + place
    gate_line = base + plan.rows * plan.cap + row
    target, _ = lax.optimization_barrier((target, total))
    grad_head, grad_gate = final_work(
        plan, target[:, None], gate_line[:, None], place[:, None], parts
    )
    return (
        grad_head.reshape(tokens, top, head_dim),
        grad_gate.reshape(tokens, top).astype(jnp.bfloat16),
        grad_proj[None],
    )


def solution(mesh):
    return jax.shard_map(
        functools.partial(local, mesh),
        mesh=mesh,
        in_specs=(
            P(("dp", "expert"), None, None),
            P(("dp", "expert"), None),
            P(("dp", "expert"), None),
            P(("dp", "expert"), None),
            P("expert", None, None),
        ),
        out_specs=(
            P(("dp", "expert"), None, None),
            P(("dp", "expert"), None),
            P("expert", "dp", None),
        ),
        check_vma=False,
    )
```

```python
import functools

import jax
import jax.numpy as jnp
from jax import lax
from jax.experimental import pallas as pl
from jax.experimental.pallas import tpu as pltpu
from jax.sharding import PartitionSpec as P

soft_cap = 1.5
AXES = ("dp", "expert")
GROUP = 4
LANES = 128


class Plan:
    def __init__(self, mesh, tokens, top, head_dim, features):
        self.dp = mesh.shape["dp"]
        self.experts = mesh.shape["expert"]
        self.rows = GROUP // 2
        self.planes = self.experts // GROUP
        self.splits = self.dp * self.rows
        self.sources = self.splits * 2
        self.tokens, self.top, self.head_dim = tokens, top, head_dim
        self.part = features // self.splits
        cap = 9 * tokens * top // (8 * self.experts)
        self.cap = -(-cap // 8) * 8
        self.back = self.rows * self.cap + 16

    def index(self, x, z, y, c):
        return x * self.experts + z * GROUP + y * 2 + c

    def pairs(self, dx=0, dz=0, dy=0, dc=0):
        out = []
        for x in range(self.dp):
            for z in range(self.planes):
                for y in range(self.rows):
                    for c in range(2):
                        target = self.index(
                            (x + dx) % self.dp,
                            (z + dz) % self.planes,
                            (y + dy) % self.rows,
                            c ^ dc,
                        )
                        out.append((self.index(x, z, y, c), target))
        return out

    def shift(self, value, **by):
        if not any(by.values()):
            return value
        return lax.ppermute(value, AXES, self.pairs(**by))

    def along(self, value, moves):
        out = []
        for x in range(self.dp):
            for a, b in moves:
                for r in range(GROUP):
                    out.append((self.index(x, a, 0, 0) + r, self.index(x, b, 0, 0) + r))
        return lax.ppermute(value, AXES, out)

    def splits_list(self):
        return [(dx, dy) for dx in range(self.dp) for dy in range(self.rows)]


def select_kernel(plan, ids, pack_ref, hot_ref, head_ref, gate_ref):
    tokens, cap, top, head_dim = plan.tokens, plan.cap, plan.top, plan.head_dim
    experts = plan.planes * plan.rows
    row_of = lax.broadcasted_iota(jnp.int32, (cap, tokens), 0)
    before = (
        lax.broadcasted_iota(jnp.int32, (tokens, tokens), 0)
        < lax.broadcasted_iota(jnp.int32, (tokens, tokens), 1)
    ).astype(jnp.bfloat16)
    empty = jnp.zeros((cap, tokens), jnp.bfloat16)

    def pair(q, carry):
        for b in range(2):
            start = pl.multiple_of((2 * q + b) * tokens, tokens)
            meta = pack_ref[pl.ds(start, 2 * top), pl.ds(top * head_dim, LANES)].astype(jnp.float32)
            masks, gate_rows, occupied = [], [], []
            for e in range(experts):
                mask = (meta[top:] == ids[e].astype(jnp.float32)).astype(jnp.float32)
                masks.append(mask)
                gate_rows.append(jnp.sum(mask * meta[:top], axis=0, keepdims=True))
                occupied.append(jnp.sum(mask, axis=0, keepdims=True))
            filled = occupied + [jnp.zeros((1, tokens), jnp.float32)] * (-experts % 16)
            places = jnp.dot(
                jnp.concatenate(filled, axis=0).astype(jnp.bfloat16),
                before,
                preferred_element_type=jnp.float32,
            )
            wide = []
            for e in range(experts):
                place = places[e : e + 1].astype(jnp.int32)
                hot = jnp.where(row_of == place, occupied[e], 0.0)
                gates = jnp.sum(hot * gate_rows[e], axis=1, keepdims=True)
                slot, i = divmod(e, plan.rows)
                at = (2 * i + b) * cap
                hot_ref[slot, q, pl.ds(at, cap), :] = jnp.concatenate(
                    [hot.astype(jnp.bfloat16), empty] if b == 0 else [empty, hot.astype(jnp.bfloat16)],
                    axis=1,
                )
                gate_ref[slot, q, pl.ds(at, cap), :] = jnp.broadcast_to(gates, (cap, LANES)).astype(
                    jnp.bfloat16
                )
                wide.append(
                    jnp.concatenate(
                        [(hot * masks[e][k : k + 1]).astype(jnp.bfloat16) for k in range(top)], axis=1
                    )
                )
            raw = jnp.concatenate(
                [
                    pack_ref[pl.ds(start, tokens), pl.ds(k * head_dim, head_dim)]
                    for k in range(top)
                ],
                axis=0,
            )
            chosen = jnp.dot(
                jnp.concatenate(wide, axis=0), raw, preferred_element_type=jnp.float32
            ).astype(jnp.bfloat16)
            for e in range(experts):
                slot, i = divmod(e, plan.rows)
                head_ref[slot, q, pl.ds((2 * i + b) * cap, cap), :] = chosen[e * cap : (e + 1) * cap]
        return carry

    lax.fori_loop(0, plan.sources // 2, pair, 0)


def select_work(plan, ids, packs):
    rows = plan.rows * 2 * plan.cap
    lead = (plan.planes, plan.sources // 2, rows)
    return pl.pallas_call(
        functools.partial(select_kernel, plan),
        out_shape=(
            jax.ShapeDtypeStruct((*lead, 2 * plan.tokens), jnp.bfloat16),
            jax.ShapeDtypeStruct((*lead, plan.head_dim), jnp.bfloat16),
            jax.ShapeDtypeStruct((*lead, LANES), jnp.bfloat16),
        ),
        in_specs=[
            pl.BlockSpec(memory_space=pltpu.SMEM),
            pl.BlockSpec(memory_space=pltpu.VMEM),
        ],
        out_specs=(pl.BlockSpec(memory_space=pltpu.VMEM),) * 3,
        compiler_params=pltpu.CompilerParams(vmem_limit_bytes=56 * 1024 * 1024),
    )(ids, packs)


def slot_kernel(plan, slot_index, earlier, ids, *refs):
    packs = refs[: plan.sources]
    hot_any, head_any, gate_any, w_ref = refs[plan.sources : plan.sources + 4]
    rest = refs[plan.sources + 4 :]
    earlier_refs, rest = rest[:earlier], rest[earlier:]
    count = plan.sources if earlier else 1
    p_ref, back_refs, (buf, hots, heads, gates, grads, sems) = rest[0], rest[1 : 1 + count], rest[1 + count :]
    tokens, cap, part, head_dim = plan.tokens, plan.cap, plan.part, plan.head_dim
    pair_rows = 2 * cap
    pair_total = plan.sources // 2
    base = (plan.planes - 1) * plan.back if earlier else 0

    def copies(q):
        slot = q % 2
        return [
            pltpu.make_async_copy(
                packs[2 * q + b], buf.at[slot, pl.ds(b * tokens, tokens), :], sems.at[slot, b]
            )
            for b in range(2)
        ]

    chosen = [
        pltpu.make_async_copy(hot_any.at[slot_index], hots, sems.at[2, 0]),
        pltpu.make_async_copy(head_any.at[slot_index], heads, sems.at[2, 1]),
        pltpu.make_async_copy(gate_any.at[slot_index], gates, sems.at[3, 0]),
    ]
    for copy in chosen + copies(0):
        copy.start()
    lines = lax.broadcasted_iota(jnp.int32, (cap, LANES), 0)
    lanes = lax.broadcasted_iota(jnp.int32, (cap, LANES), 1)
    diagonal = (lines == lanes).astype(jnp.float32)
    block_row = lax.broadcasted_iota(jnp.int32, (16, LANES), 0)
    chunk = min(part, 512)
    for copy in chosen:
        copy.wait()
    for q in range(pair_total):
        slot = q % 2
        if q + 1 < pair_total:
            for copy in copies(q + 1):
                copy.start()
        for copy in copies(q):
            copy.wait()
        sums = [jnp.zeros((pair_rows, LANES), jnp.float32) for _ in range(plan.rows)]
        for start in range(0, part, chunk):
            grad = jnp.dot(
                hots[q], buf[slot, :, pl.ds(start, chunk)], preferred_element_type=jnp.float32
            )
            for i in range(plan.rows):
                at = i * pair_rows
                weight = w_ref[
                    pl.ds(pl.multiple_of(ids[plan.rows + i], 128), head_dim), pl.ds(start, chunk)
                ]
                pre = jnp.dot(
                    heads[q, pl.ds(at, pair_rows), :], weight, preferred_element_type=jnp.float32
                )
                gate = gates[q, pl.ds(at, pair_rows), :].astype(jnp.float32)
                for lane in range(0, chunk, LANES):
                    grad_block = grad[at : at + pair_rows, lane : lane + LANES]
                    capped = jnp.tanh(pre[:, lane : lane + LANES] * (1.0 / soft_cap))
                    sums[i] = sums[i] + grad_block * capped
                    grads[i, pl.ds(q * pair_rows, pair_rows), pl.ds(start + lane, LANES)] = (
                        gate * grad_block * (1.0 - capped * capped)
                    ).astype(jnp.bfloat16)
        for b in range(2):
            block = jnp.zeros((16, LANES), jnp.float32)
            for i in range(plan.rows):
                column = jnp.sum(sums[i][b * cap : (b + 1) * cap], axis=1, keepdims=True) * soft_cap
                line = jnp.sum(diagonal * column, axis=0, keepdims=True)
                block = jnp.where(block_row == i, line, block)
            s = 2 * q + b
            at = base + plan.rows * cap
            if earlier:
                back_refs[s][pl.ds(at, 16), :] = block.astype(jnp.bfloat16)
            else:
                back_refs[0][s, pl.ds(at, 16), :] = block.astype(jnp.bfloat16)
    for i in range(plan.rows):
        weight = w_ref[pl.ds(pl.multiple_of(ids[plan.rows + i], 128), head_dim), :]
        grad_all = grads[i]
        head_all = jnp.concatenate(
            [heads[q, pl.ds(i * pair_rows, pair_rows), :] for q in range(pair_total)], axis=0
        )
        p_ref[pl.ds(i * head_dim, head_dim), :] = lax.dot_general(
            head_all, grad_all, (((0,), (0,)), ((), ())), preferred_element_type=jnp.float32
        ).astype(p_ref.dtype)
        rows = lax.dot_general(
            grad_all, weight, (((1,), (1,)), ((), ())), preferred_element_type=jnp.float32
        ).astype(jnp.bfloat16)
        for s in range(plan.sources):
            value = rows[s * cap : (s + 1) * cap]
            if earlier:
                back_refs[s][pl.ds(base + i * cap, cap), :] = value
            else:
                back_refs[0][s, pl.ds(i * cap, cap), :] = value
    for j, ref in enumerate(earlier_refs):
        for s in range(plan.sources):
            back_refs[s][pl.ds(j * plan.back, plan.back), :] = ref[s]


def slot_work(plan, slot_index, ids, packs, selected, weight, kind, earlier=()):
    rows = plan.rows * 2 * plan.cap
    pair_total = plan.sources // 2
    if earlier:
        backs = (
            jax.ShapeDtypeStruct((plan.planes * plan.back, LANES), jnp.bfloat16),
        ) * plan.sources
    else:
        backs = (jax.ShapeDtypeStruct((plan.sources, plan.back, LANES), jnp.bfloat16),)
    vmem = pl.BlockSpec(memory_space=pltpu.VMEM)
    return pl.pallas_call(
        functools.partial(slot_kernel, plan, slot_index, len(earlier)),
        out_shape=(jax.ShapeDtypeStruct((plan.rows * plan.head_dim, plan.part), kind), *backs),
        in_specs=[pl.BlockSpec(memory_space=pltpu.SMEM)]
        + [pl.BlockSpec(memory_space=pl.ANY)] * (plan.sources + 3)
        + [vmem] * (1 + len(earlier)),
        out_specs=(vmem,) * (1 + len(backs)),
        scratch_shapes=[
            pltpu.VMEM((2, 2 * plan.tokens, plan.part), jnp.bfloat16),
            pltpu.VMEM((pair_total, rows, 2 * plan.tokens), jnp.bfloat16),
            pltpu.VMEM((pair_total, rows, plan.head_dim), jnp.bfloat16),
            pltpu.VMEM((pair_total, rows, LANES), jnp.bfloat16),
            pltpu.VMEM((plan.rows, plan.sources * plan.cap, plan.part), jnp.bfloat16),
            pltpu.SemaphoreType.DMA((4, 2)),
        ],
        compiler_params=pltpu.CompilerParams(vmem_limit_bytes=32 * 1024 * 1024),
    )(ids, *packs, *selected, weight, *earlier)


def sum_kernel(plan, starts, own_ref, *refs):
    received = refs[: len(refs) - plan.splits]
    pieces = refs[len(refs) - plan.splits :]
    rows = plan.head_dim // plan.dp
    for j, piece in enumerate(pieces):
        at = pl.ds(pl.multiple_of(starts[j], rows), rows)
        total = own_ref[at, :]
        for ref in received:
            total = total + ref[at, :].astype(jnp.float32)
        piece[...] = total.astype(piece.dtype)


def sum_work(plan, starts, own, received):
    rows = plan.head_dim // plan.dp
    vmem = pl.BlockSpec(memory_space=pltpu.VMEM)
    return pl.pallas_call(
        functools.partial(sum_kernel, plan),
        out_shape=tuple(
            jax.ShapeDtypeStruct((rows, plan.part), jnp.bfloat16 if j else jnp.float32)
            for j in range(plan.splits)
        ),
        in_specs=[pl.BlockSpec(memory_space=pltpu.SMEM)] + [vmem] * (1 + len(received)),
        out_specs=(vmem,) * plan.splits,
    )(starts, own, *received)


def layout_kernel(plan, starts, *refs):
    out_ref = refs[-1]
    for j, piece in enumerate(refs[:-1]):
        at = pl.ds(pl.multiple_of(starts[j], plan.part), plan.part)
        out_ref[:, at] = piece[...].astype(jnp.float32)


def layout_work(plan, starts, pieces):
    rows = plan.head_dim // plan.dp
    vmem = pl.BlockSpec(memory_space=pltpu.VMEM)
    return pl.pallas_call(
        functools.partial(layout_kernel, plan),
        out_shape=jax.ShapeDtypeStruct((rows, plan.part * plan.splits), jnp.float32),
        in_specs=[pl.BlockSpec(memory_space=pltpu.SMEM)] + [vmem] * plan.splits,
        out_specs=vmem,
    )(starts, *pieces)


def final_kernel(plan, target_ref, gate_ref, place_ref, *refs):
    parts = refs[: plan.sources]
    head_ref, out_gate_ref, table = refs[plan.sources :]
    length = plan.planes * plan.back
    for dc in range(2):
        total = None
        for s in range(plan.splits):
            piece = parts[2 * s + dc][...].astype(jnp.float32)
            total = piece if total is None else total + piece
        table[pl.ds(dc * length, length), :] = total.astype(jnp.bfloat16)
    block = 256
    count = plan.tokens * plan.top
    for start in range(0, count, block):
        slot_of = lax.broadcasted_iota(jnp.int32, (block, 2 * length), 1)
        hot = (slot_of == target_ref[pl.ds(start, block), :]).astype(jnp.bfloat16)
        head_ref[pl.ds(start, block), :] = jnp.dot(
            hot, table[...], preferred_element_type=jnp.float32
        ).astype(jnp.bfloat16)
        hot = (slot_of == gate_ref[pl.ds(start, block), :]).astype(jnp.bfloat16)
        lines = jnp.dot(hot, table[...], preferred_element_type=jnp.float32)
        lane_of = lax.broadcasted_iota(jnp.int32, (block, LANES), 1)
        out_gate_ref[pl.ds(start, block), :] = jnp.sum(
            jnp.where(lane_of == place_ref[pl.ds(start, block), :], lines, 0.0),
            axis=1,
            keepdims=True,
        )


def final_work(plan, target, gate_line, place, parts):
    count = plan.tokens * plan.top
    return pl.pallas_call(
        functools.partial(final_kernel, plan),
        out_shape=(
            jax.ShapeDtypeStruct((count, plan.head_dim), jnp.bfloat16),
            jax.ShapeDtypeStruct((count, 1), jnp.float32),
        ),
        in_specs=[pl.BlockSpec(memory_space=pltpu.VMEM)] * (3 + plan.sources),
        out_specs=(
            pl.BlockSpec(memory_space=pltpu.VMEM),
            pl.BlockSpec(memory_space=pltpu.VMEM),
        ),
        scratch_shapes=[pltpu.VMEM((2 * plan.planes * plan.back, LANES), jnp.bfloat16)],
        compiler_params=pltpu.CompilerParams(vmem_limit_bytes=48 * 1024 * 1024),
    )(target, gate_line, place, *parts)


def local(mesh, head_outputs, out_grad, gate_weights, route_ids, out_proj):
    tokens, top, head_dim = head_outputs.shape
    features = out_grad.shape[1]
    plan = Plan(mesh, tokens, top, head_dim, features)
    x = lax.axis_index("dp")
    me = lax.axis_index("expert")
    z, y, c = me // GROUP, (me % GROUP) // 2, me % 2

    weight_parts = []
    for dy in range(plan.rows):
        split = x * plan.rows + (y + dy) % plan.rows
        piece = lax.dynamic_slice_in_dim(out_proj[0], split * plan.part, plan.part, 1)
        weight_parts.append(plan.shift(piece, dy=dy))
    own_weights = jnp.concatenate(weight_parts, axis=0)

    meta = jnp.concatenate(
        [
            gate_weights.T,
            route_ids.T.astype(jnp.bfloat16),
            jnp.zeros((LANES - 2 * top, tokens), jnp.bfloat16),
        ],
        axis=0,
    )
    head_pack = jnp.concatenate([head_outputs.reshape(tokens, top * head_dim), meta], axis=1)

    def grad_part(dx, dy):
        split = ((x + dx) % plan.dp) * plan.rows + (y + dy) % plan.rows
        return lax.dynamic_slice_in_dim(out_grad, split * plan.part, plan.part, 1)

    def plane_gather(piece_of):
        out = []
        for dx, dy in plan.splits_list():
            value = plan.shift(piece_of(dx, dy), dx=dx, dy=dy)
            out += [value, plan.shift(value, dc=1)]
        return out

    head_packs = jnp.concatenate(plane_gather(lambda dx, dy: head_pack), axis=0)
    packs = plane_gather(grad_part)

    if plan.planes == 4:
        inner = (z == 1) | (z == 2)
        mates, middle = [(0, 1), (1, 0), (2, 3), (3, 2)], [(1, 2), (2, 1)]
        outward, inward, across = [(1, 0), (2, 3)], [(0, 1), (3, 2)], [(1, 3), (2, 0)]
        plane_of = jnp.stack([jnp.where(z < 2, 2, 1), jnp.where(z < 2, 3, 0), z ^ 1, z])
        mate = plan.along(own_weights, mates)
        near_in = plan.along(own_weights, middle)
        near_out = plan.along(near_in, outward)
        far_in = plan.along(mate, middle)
        far_out = plan.along(far_in, outward)
        weights = [
            jnp.where(inner, near_in, near_out),
            jnp.where(inner, far_in, far_out),
            mate,
            own_weights,
        ]
    else:
        steps = [k % plan.planes for k in range(1, plan.planes + 1)]
        plane_of = (z + jnp.array(steps, jnp.int32)) % plan.planes
        weights = [plan.shift(own_weights, dz=-k % plan.planes) for k in steps]

    routes = route_ids.reshape(tokens * top)
    hot = (routes[:, None] == jnp.arange(plan.experts, dtype=jnp.int32)[None, :]).astype(jnp.float32)
    per_token = hot.reshape(tokens, top, plan.experts).sum(axis=1)
    earlier = jnp.tril(jnp.ones((tokens, tokens), jnp.float32), -1)
    places = jnp.dot(earlier, per_token)
    place = jnp.sum(
        hot.reshape(tokens, top, plan.experts) * places[:, None, :], axis=2
    ).astype(jnp.int32).reshape(tokens * top)
    slots = jnp.arange(plan.planes, dtype=jnp.int32)
    slot = jnp.sum(
        jnp.where((routes // GROUP)[:, None] == plane_of[None, :], slots[None, :], 0), axis=1
    )
    row = (routes % GROUP) // 2
    side = (routes % 2) ^ c
    base = side * (plan.planes * plan.back) + slot * plan.back
    target = (base + row * plan.cap + place)[:, None]
    gate_line = (base + plan.rows * plan.cap + row)[:, None]
    place = place[:, None]

    rows_at = jnp.arange(plan.rows, dtype=jnp.int32)
    weight_at = ((y - rows_at) % plan.rows) * head_dim
    expert_ids = (plane_of[:, None] * GROUP + rows_at[None, :] * 2 + c).astype(jnp.int32)
    selected = select_work(plan, expert_ids.reshape(-1), head_packs)
    selected, (target, gate_line, place) = lax.optimization_barrier(
        (selected, (target, gate_line, place))
    )
    sums, backs = [], []
    for j in range(plan.planes):
        last = j == plan.planes - 1
        ids = jnp.concatenate([expert_ids[j], weight_at]).astype(jnp.int32)
        if backs:
            ids, _ = lax.optimization_barrier((ids, backs[-1]))
        part, *back = slot_work(
            plan,
            j,
            ids,
            packs,
            selected,
            weights[j],
            jnp.float32 if last else jnp.bfloat16,
            backs if last else (),
        )
        sums.append(part)
        backs = back if last else backs + back

    if plan.planes == 4:
        near_sum = sums[0] + plan.along(sums[0], inward)
        far_sum = sums[1] + plan.along(sums[1], inward)
        received = [
            plan.along(sums[2], mates),
            plan.along(near_sum, middle),
            plan.along(far_sum, across),
        ]
        backs, _ = lax.optimization_barrier((backs, (near_sum, far_sum)))
    else:
        received = [plan.shift(sums[j], dz=steps[j]) for j in range(plan.planes - 1)]
    own_rows = head_dim // plan.dp
    starts = jnp.stack(
        [
            ((y + dy) % plan.rows) * head_dim + ((x + dx) % plan.dp) * own_rows
            for dx, dy in plan.splits_list()
        ]
    ).astype(jnp.int32)
    pieces = sum_work(plan, starts, sums[-1], received)
    target, _ = lax.optimization_barrier((target, pieces[0]))
    pieces = [
        plan.shift(piece, dx=dx, dy=dy) for piece, (dx, dy) in zip(pieces, plan.splits_list())
    ]
    starts = jnp.stack(
        [
            (((x - dx) % plan.dp) * plan.rows + (y - dy) % plan.rows) * plan.part
            for dx, dy in plan.splits_list()
        ]
    ).astype(jnp.int32)
    grad_proj = layout_work(plan, starts, pieces)

    parts = []
    for dx, dy in plan.splits_list():
        for dc in range(2):
            parts.append(
                plan.shift(backs[len(parts)], dx=-dx % plan.dp, dy=-dy % plan.rows, dc=dc)
            )
    grad_head, grad_gate = final_work(plan, target, gate_line, place, parts)
    return (
        grad_head.reshape(tokens, top, head_dim),
        grad_gate.reshape(tokens, top).astype(jnp.bfloat16),
        grad_proj[None],
    )


def solution(mesh):
    return jax.shard_map(
        functools.partial(local, mesh),
        mesh=mesh,
        in_specs=(
            P(("dp", "expert"), None, None),
            P(("dp", "expert"), None),
            P(("dp", "expert"), None),
            P(("dp", "expert"), None),
            P("expert", None, None),
        ),
        out_specs=(
            P(("dp", "expert"), None, None),
            P(("dp", "expert"), None),
            P("expert", "dp", None),
        ),
        check_vma=False,
    )
```

```python
import functools

import jax
import jax.numpy as jnp
from jax import lax
from jax.experimental import pallas as pl
from jax.experimental.pallas import tpu as pltpu
from jax.sharding import PartitionSpec as P

soft_cap = 1.5
AXES = ("dp", "expert")
GROUP = 4
LANES = 128


class Plan:
    def __init__(self, mesh, tokens, top, head_dim, features):
        self.dp = mesh.shape["dp"]
        self.experts = mesh.shape["expert"]
        self.rows = GROUP // 2
        self.planes = self.experts // GROUP
        self.splits = self.dp * self.rows
        self.sources = self.splits * 2
        self.tokens, self.top, self.head_dim = tokens, top, head_dim
        self.part = features // self.splits
        cap = 9 * tokens * top // (8 * self.experts)
        self.cap = -(-cap // 8) * 8
        self.back = self.rows * self.cap + 16

    def index(self, x, z, y, c):
        return x * self.experts + z * GROUP + y * 2 + c

    def pairs(self, dx=0, dz=0, dy=0, dc=0):
        out = []
        for x in range(self.dp):
            for z in range(self.planes):
                for y in range(self.rows):
                    for c in range(2):
                        target = self.index(
                            (x + dx) % self.dp,
                            (z + dz) % self.planes,
                            (y + dy) % self.rows,
                            c ^ dc,
                        )
                        out.append((self.index(x, z, y, c), target))
        return out

    def shift(self, value, **by):
        if not any(by.values()):
            return value
        return lax.ppermute(value, AXES, self.pairs(**by))

    def along(self, value, moves):
        out = []
        for x in range(self.dp):
            for a, b in moves:
                for r in range(GROUP):
                    out.append((self.index(x, a, 0, 0) + r, self.index(x, b, 0, 0) + r))
        return lax.ppermute(value, AXES, out)

    def splits_list(self):
        return [(dx, dy) for dx in range(self.dp) for dy in range(self.rows)]


def slot_kernel(plan, weight_count, earlier, ids, *refs):
    packs, rest = refs[: plan.sources], refs[plan.sources :]
    weight_refs, rest = rest[:weight_count], rest[weight_count:]
    earlier_refs, rest = rest[:earlier], rest[earlier:]
    count = plan.sources if earlier else 1
    p_ref, back_refs, (grads, heads, weights) = rest[0], rest[1 : 1 + count], rest[1 + count :]
    tokens, cap, part, top, head_dim = plan.tokens, plan.cap, plan.part, plan.top, plan.head_dim
    pair_rows = 2 * cap
    pair_total = plan.sources // 2
    base = (plan.planes - 1) * plan.back if earlier else 0

    for i in range(plan.rows):
        at = pl.ds(pl.multiple_of(ids[plan.rows + i], head_dim), head_dim)
        if weight_count == 1:
            weights[i] = weight_refs[0][at, :]
        else:
            for j in range(2):

                @pl.when(ids[2 * plan.rows] == j)
                def _():
                    weights[i] = weight_refs[j][at, :]

    row_of = lax.broadcasted_iota(jnp.int32, (cap, tokens), 0)
    diagonal = (row_of == lax.broadcasted_iota(jnp.int32, (cap, tokens), 1)).astype(jnp.float32)
    before = (
        lax.broadcasted_iota(jnp.int32, (tokens, tokens), 0)
        < lax.broadcasted_iota(jnp.int32, (tokens, tokens), 1)
    ).astype(jnp.bfloat16)
    block_row = lax.broadcasted_iota(jnp.int32, (16, LANES), 0)
    empty = jnp.zeros((cap, tokens), jnp.bfloat16)
    chunk = min(part, 512)
    for q in range(pair_total):
        hots, gates, chosen = {}, {}, {}
        for b in range(2):
            pack = packs[2 * q + b]
            meta = pack[pl.ds(0, 2 * top), pl.ds(part + top * head_dim, LANES)].astype(jnp.float32)
            masks, occupied = [], []
            for i in range(plan.rows):
                mask = (meta[top:] == ids[i].astype(jnp.float32)).astype(jnp.float32)
                masks.append(mask)
                occupied.append(jnp.sum(mask, axis=0, keepdims=True))
            filled = occupied + [jnp.zeros((1, tokens), jnp.float32)] * (-plan.rows % 16)
            places = jnp.dot(
                jnp.concatenate(filled, axis=0).astype(jnp.bfloat16),
                before,
                preferred_element_type=jnp.float32,
            )
            wide = []
            for i in range(plan.rows):
                place = places[i : i + 1].astype(jnp.int32)
                hot = jnp.where(row_of == place, occupied[i], 0.0)
                gate_row = jnp.sum(masks[i] * meta[:top], axis=0, keepdims=True)
                gates[i, b] = jnp.sum(hot * gate_row, axis=1, keepdims=True)
                hots[i, b] = hot.astype(jnp.bfloat16)
                wide.append(
                    jnp.concatenate(
                        [(hot * masks[i][k : k + 1]).astype(jnp.bfloat16) for k in range(top)], axis=1
                    )
                )
            raw = jnp.concatenate(
                [pack[:, pl.ds(part + k * head_dim, head_dim)] for k in range(top)], axis=0
            )
            rows = jnp.dot(
                jnp.concatenate(wide, axis=0), raw, preferred_element_type=jnp.float32
            ).astype(jnp.bfloat16)
            for i in range(plan.rows):
                heads[i, pl.ds(q * pair_rows + b * cap, cap), :] = rows[i * cap : (i + 1) * cap]
        all_hots = jnp.concatenate(
            [
                jnp.concatenate([hots[i, b], empty] if b == 0 else [empty, hots[i, b]], axis=1)
                for i in range(plan.rows)
                for b in range(2)
            ],
            axis=0,
        )
        sums = [jnp.zeros((pair_rows, LANES), jnp.float32) for _ in range(plan.rows)]
        for start in range(0, part, chunk):
            both = jnp.concatenate(
                [packs[2 * q + b][:, pl.ds(start, chunk)] for b in range(2)], axis=0
            )
            grad = jnp.dot(all_hots, both, preferred_element_type=jnp.float32)
            for i in range(plan.rows):
                at = i * pair_rows
                pre = jnp.dot(
                    heads[i, pl.ds(q * pair_rows, pair_rows), :],
                    weights[i, :, pl.ds(start, chunk)],
                    preferred_element_type=jnp.float32,
                )
                gate = jnp.broadcast_to(
                    jnp.concatenate([gates[i, 0], gates[i, 1]], axis=0), (pair_rows, LANES)
                )
                for lane in range(0, chunk, LANES):
                    grad_block = grad[at : at + pair_rows, lane : lane + LANES]
                    capped = jnp.tanh(pre[:, lane : lane + LANES] * (1.0 / soft_cap))
                    sums[i] = sums[i] + grad_block * capped
                    grads[i, pl.ds(q * pair_rows, pair_rows), pl.ds(start + lane, LANES)] = (
                        gate * grad_block * (1.0 - capped * capped)
                    ).astype(jnp.bfloat16)
        for b in range(2):
            block = jnp.zeros((16, LANES), jnp.float32)
            for i in range(plan.rows):
                column = jnp.sum(sums[i][b * cap : (b + 1) * cap], axis=1, keepdims=True) * soft_cap
                line = jnp.sum(diagonal * column, axis=0, keepdims=True)
                block = jnp.where(block_row == i, line, block)
            s = 2 * q + b
            at = base + plan.rows * cap
            if earlier:
                back_refs[s][pl.ds(at, 16), :] = block.astype(jnp.bfloat16)
            else:
                back_refs[0][s, pl.ds(at, 16), :] = block.astype(jnp.bfloat16)
    for i in range(plan.rows):
        grad_all = grads[i]
        p_ref[pl.ds(i * head_dim, head_dim), :] = lax.dot_general(
            heads[i], grad_all, (((0,), (0,)), ((), ())), preferred_element_type=jnp.float32
        ).astype(p_ref.dtype)
        rows = lax.dot_general(
            grad_all, weights[i], (((1,), (1,)), ((), ())), preferred_element_type=jnp.float32
        ).astype(jnp.bfloat16)
        for s in range(plan.sources):
            value = rows[s * cap : (s + 1) * cap]
            if earlier:
                back_refs[s][pl.ds(base + i * cap, cap), :] = value
            else:
                back_refs[0][s, pl.ds(i * cap, cap), :] = value
    for j, ref in enumerate(earlier_refs):
        for s in range(plan.sources):
            back_refs[s][pl.ds(j * plan.back, plan.back), :] = ref[s]


def slot_work(plan, ids, packs, weights, kind, earlier=()):
    rows = plan.sources * plan.cap
    if earlier:
        backs = (
            jax.ShapeDtypeStruct((plan.planes * plan.back, LANES), jnp.bfloat16),
        ) * plan.sources
    else:
        backs = (jax.ShapeDtypeStruct((plan.sources, plan.back, LANES), jnp.bfloat16),)
    vmem = pl.BlockSpec(memory_space=pltpu.VMEM)
    return pl.pallas_call(
        functools.partial(slot_kernel, plan, len(weights), len(earlier)),
        out_shape=(jax.ShapeDtypeStruct((plan.rows * plan.head_dim, plan.part), kind), *backs),
        in_specs=[pl.BlockSpec(memory_space=pltpu.SMEM)]
        + [vmem] * (plan.sources + len(weights) + len(earlier)),
        out_specs=(vmem,) * (1 + len(backs)),
        scratch_shapes=[
            pltpu.VMEM((plan.rows, rows, plan.part), jnp.bfloat16),
            pltpu.VMEM((plan.rows, rows, plan.head_dim), jnp.bfloat16),
            pltpu.VMEM((plan.rows, plan.head_dim, plan.part), jnp.bfloat16),
        ],
        compiler_params=pltpu.CompilerParams(vmem_limit_bytes=20 * 1024 * 1024),
    )(ids, *packs, *weights, *earlier)


def sum_kernel(plan, starts, own_ref, *refs):
    received = refs[: len(refs) - plan.splits]
    pieces = refs[len(refs) - plan.splits :]
    rows = plan.head_dim // plan.dp
    for j, piece in enumerate(pieces):
        at = pl.ds(pl.multiple_of(starts[j], rows), rows)
        total = own_ref[at, :]
        for ref in received:
            total = total + ref[at, :].astype(jnp.float32)
        piece[...] = total.astype(piece.dtype)


def sum_work(plan, starts, own, received):
    rows = plan.head_dim // plan.dp
    vmem = pl.BlockSpec(memory_space=pltpu.VMEM)
    return pl.pallas_call(
        functools.partial(sum_kernel, plan),
        out_shape=tuple(
            jax.ShapeDtypeStruct((rows, plan.part), jnp.bfloat16 if j else jnp.float32)
            for j in range(plan.splits)
        ),
        in_specs=[pl.BlockSpec(memory_space=pltpu.SMEM)] + [vmem] * (1 + len(received)),
        out_specs=(vmem,) * plan.splits,
    )(starts, own, *received)


def layout_kernel(plan, starts, *refs):
    out_ref = refs[-1]
    for j, piece in enumerate(refs[:-1]):
        at = pl.ds(pl.multiple_of(starts[j], plan.part), plan.part)
        out_ref[:, at] = piece[...].astype(jnp.float32)


def layout_work(plan, starts, pieces):
    rows = plan.head_dim // plan.dp
    vmem = pl.BlockSpec(memory_space=pltpu.VMEM)
    return pl.pallas_call(
        functools.partial(layout_kernel, plan),
        out_shape=jax.ShapeDtypeStruct((rows, plan.part * plan.splits), jnp.float32),
        in_specs=[pl.BlockSpec(memory_space=pltpu.SMEM)] + [vmem] * plan.splits,
        out_specs=vmem,
    )(starts, *pieces)


def final_kernel(plan, target_ref, gate_ref, place_ref, *refs):
    parts = refs[: plan.sources]
    head_ref, out_gate_ref, table = refs[plan.sources :]
    length = plan.planes * plan.back
    for dc in range(2):
        total = None
        for s in range(plan.splits):
            piece = parts[2 * s + dc][...].astype(jnp.float32)
            total = piece if total is None else total + piece
        table[pl.ds(dc * length, length), :] = total.astype(jnp.bfloat16)
    block = 256
    count = plan.tokens * plan.top
    for start in range(0, count, block):
        slot_of = lax.broadcasted_iota(jnp.int32, (block, 2 * length), 1)
        hot = (slot_of == target_ref[pl.ds(start, block), :]).astype(jnp.bfloat16)
        head_ref[pl.ds(start, block), :] = jnp.dot(
            hot, table[...], preferred_element_type=jnp.float32
        ).astype(jnp.bfloat16)
        hot = (slot_of == gate_ref[pl.ds(start, block), :]).astype(jnp.bfloat16)
        lines = jnp.dot(hot, table[...], preferred_element_type=jnp.float32)
        lane_of = lax.broadcasted_iota(jnp.int32, (block, LANES), 1)
        out_gate_ref[pl.ds(start, block), :] = jnp.sum(
            jnp.where(lane_of == place_ref[pl.ds(start, block), :], lines, 0.0),
            axis=1,
            keepdims=True,
        )


def final_work(plan, target, gate_line, place, parts):
    count = plan.tokens * plan.top
    return pl.pallas_call(
        functools.partial(final_kernel, plan),
        out_shape=(
            jax.ShapeDtypeStruct((count, plan.head_dim), jnp.bfloat16),
            jax.ShapeDtypeStruct((count, 1), jnp.float32),
        ),
        in_specs=[pl.BlockSpec(memory_space=pltpu.VMEM)] * (3 + plan.sources),
        out_specs=(
            pl.BlockSpec(memory_space=pltpu.VMEM),
            pl.BlockSpec(memory_space=pltpu.VMEM),
        ),
        scratch_shapes=[pltpu.VMEM((2 * plan.planes * plan.back, LANES), jnp.bfloat16)],
        compiler_params=pltpu.CompilerParams(vmem_limit_bytes=48 * 1024 * 1024),
    )(target, gate_line, place, *parts)


def local(mesh, head_outputs, out_grad, gate_weights, route_ids, out_proj):
    tokens, top, head_dim = head_outputs.shape
    features = out_grad.shape[1]
    plan = Plan(mesh, tokens, top, head_dim, features)
    x = lax.axis_index("dp")
    me = lax.axis_index("expert")
    z, y, c = me // GROUP, (me % GROUP) // 2, me % 2

    weight_parts = []
    for dy in range(plan.rows):
        split = x * plan.rows + (y + dy) % plan.rows
        weight_parts.append(lax.dynamic_slice_in_dim(out_proj[0], split * plan.part, plan.part, 1))
    out_grad, weight_parts = lax.optimization_barrier((out_grad, weight_parts))
    own_weights = jnp.concatenate(
        [plan.shift(piece, dy=dy) for dy, piece in enumerate(weight_parts)], axis=0
    )

    meta = jnp.concatenate(
        [
            gate_weights.T,
            route_ids.T.astype(jnp.bfloat16),
            jnp.zeros((LANES - 2 * top, tokens), jnp.bfloat16),
        ],
        axis=0,
    )
    flat_heads = head_outputs.reshape(tokens, top * head_dim)
    near_packs = []
    for dx, dy in plan.splits_list():
        split = ((x + dx) % plan.dp) * plan.rows + (y + dy) % plan.rows
        piece = lax.dynamic_slice_in_dim(out_grad, split * plan.part, plan.part, 1)
        value = jnp.concatenate([piece, flat_heads, meta], axis=1)
        if dx or dy:
            value = plan.shift(value, dx=dx, dy=dy)
        else:
            value, own_weights = lax.optimization_barrier((value, own_weights))
        near_packs.append(value)

    if plan.planes == 4:
        inner = (z == 1) | (z == 2)
        mates, middle = [(0, 1), (1, 0), (2, 3), (3, 2)], [(1, 2), (2, 1)]
        outward, inward, across = [(1, 0), (2, 3)], [(0, 1), (3, 2)], [(1, 3), (2, 0)]
        plane_of = jnp.stack([jnp.where(z < 2, 2, 1), jnp.where(z < 2, 3, 0), z ^ 1, z])
        mate = plan.along(own_weights, mates)
        near_in = plan.along(own_weights, middle)
        near_out = plan.along(near_in, outward)
        far_in, near_out = lax.optimization_barrier((plan.along(mate, middle), near_out))
        far_out = plan.along(far_in, outward)
        near_packs[1:], near_in = lax.optimization_barrier((near_packs[1:], near_in))
        weights = [(near_in, near_out), (far_in, far_out), (mate,), (own_weights,)]
        which = jnp.where(inner, 0, 1)
    else:
        steps = [k % plan.planes for k in range(1, plan.planes + 1)]
        plane_of = (z + jnp.array(steps, jnp.int32)) % plan.planes
        weights = [(plan.shift(own_weights, dz=-k % plan.planes),) for k in steps]
        which = z * 0
    packs = []
    for value in near_packs:
        packs += [value, plan.shift(value, dc=1)]

    routes, own_weights = lax.optimization_barrier((route_ids.reshape(tokens * top), own_weights))
    hot = (routes[:, None] == jnp.arange(plan.experts, dtype=jnp.int32)[None, :]).astype(jnp.float32)
    per_token = hot.reshape(tokens, top, plan.experts).sum(axis=1)
    earlier = jnp.tril(jnp.ones((tokens, tokens), jnp.float32), -1)
    places = jnp.dot(earlier, per_token)
    place = jnp.sum(
        hot.reshape(tokens, top, plan.experts) * places[:, None, :], axis=2
    ).astype(jnp.int32).reshape(tokens * top)
    slots = jnp.arange(plan.planes, dtype=jnp.int32)
    slot = jnp.sum(
        jnp.where((routes // GROUP)[:, None] == plane_of[None, :], slots[None, :], 0), axis=1
    )
    row = (routes % GROUP) // 2
    side = (routes % 2) ^ c
    base = side * (plan.planes * plan.back) + slot * plan.back
    target = (base + row * plan.cap + place)[:, None]
    gate_line = (base + plan.rows * plan.cap + row)[:, None]
    place = place[:, None]

    rows_at = jnp.arange(plan.rows, dtype=jnp.int32)
    weight_at = ((y - rows_at) % plan.rows) * head_dim
    expert_ids = (plane_of[:, None] * GROUP + rows_at[None, :] * 2 + c).astype(jnp.int32)
    sums, backs, done = [], [], (target, gate_line, place)
    for j in range(plan.planes):
        last = j == plan.planes - 1
        ids = jnp.concatenate([expert_ids[j], weight_at, which[None]]).astype(jnp.int32)
        if last and plan.planes == 4:
            near_sum = sums[0] + plan.along(sums[0], inward)
            done = (done, near_sum)
        ids, done = lax.optimization_barrier((ids, done))
        if j == 0:
            target, gate_line, place = done
        kind = jnp.float32 if last else jnp.bfloat16
        part, *back = slot_work(plan, ids, packs, weights[j], kind, backs if last else ())
        sums.append(part)
        backs = back if last else backs + back
        done = back[0]

    if plan.planes == 4:
        far_sum = sums[1] + plan.along(sums[1], inward)
        received = [
            plan.along(sums[2], mates),
            plan.along(near_sum, middle),
            plan.along(far_sum, across),
        ]
        backs, _ = lax.optimization_barrier((backs, far_sum))
    else:
        received = [plan.shift(sums[j], dz=steps[j]) for j in range(plan.planes - 1)]
    own_rows = head_dim // plan.dp
    starts = jnp.stack(
        [
            ((y + dy) % plan.rows) * head_dim + ((x + dx) % plan.dp) * own_rows
            for dx, dy in plan.splits_list()
        ]
    ).astype(jnp.int32)
    pieces = sum_work(plan, starts, sums[-1], received)
    target, _ = lax.optimization_barrier((target, pieces[0]))
    pieces = [
        plan.shift(piece, dx=dx, dy=dy) for piece, (dx, dy) in zip(pieces, plan.splits_list())
    ]
    starts = jnp.stack(
        [
            (((x - dx) % plan.dp) * plan.rows + (y - dy) % plan.rows) * plan.part
            for dx, dy in plan.splits_list()
        ]
    ).astype(jnp.int32)
    grad_proj = layout_work(plan, starts, pieces)

    parts = []
    for dx, dy in plan.splits_list():
        for dc in range(2):
            parts.append(
                plan.shift(backs[len(parts)], dx=-dx % plan.dp, dy=-dy % plan.rows, dc=dc)
            )
    grad_head, grad_gate = final_work(plan, target, gate_line, place, parts)
    return (
        grad_head.reshape(tokens, top, head_dim),
        grad_gate.reshape(tokens, top).astype(jnp.bfloat16),
        grad_proj[None],
    )


def solution(mesh):
    return jax.shard_map(
        functools.partial(local, mesh),
        mesh=mesh,
        in_specs=(
            P(("dp", "expert"), None, None),
            P(("dp", "expert"), None),
            P(("dp", "expert"), None),
            P(("dp", "expert"), None),
            P("expert", None, None),
        ),
        out_specs=(
            P(("dp", "expert"), None, None),
            P(("dp", "expert"), None),
            P("expert", "dp", None),
        ),
        check_vma=False,
    )
```

```python
import functools

import jax
import jax.numpy as jnp
from jax import lax
from jax.experimental import pallas as pl
from jax.experimental.pallas import tpu as pltpu
from jax.sharding import PartitionSpec as P

soft_cap = 1.5
AXES = ("dp", "expert")
GROUP = 4
LANES = 128


class Plan:
    def __init__(self, mesh, tokens, top, head_dim, features):
        self.dp = mesh.shape["dp"]
        self.experts = mesh.shape["expert"]
        self.rows = GROUP // 2
        self.planes = self.experts // GROUP
        self.splits = self.dp * self.rows
        self.sources = self.splits * 2
        self.tokens, self.top, self.head_dim = tokens, top, head_dim
        self.part = features // self.splits
        cap = 9 * tokens * top // (8 * self.experts)
        self.cap = -(-cap // 8) * 8
        self.back = self.rows * self.cap + 16

    def index(self, x, z, y, c):
        return x * self.experts + z * GROUP + y * 2 + c

    def pairs(self, dx=0, dz=0, dy=0, dc=0):
        out = []
        for x in range(self.dp):
            for z in range(self.planes):
                for y in range(self.rows):
                    for c in range(2):
                        target = self.index(
                            (x + dx) % self.dp,
                            (z + dz) % self.planes,
                            (y + dy) % self.rows,
                            c ^ dc,
                        )
                        out.append((self.index(x, z, y, c), target))
        return out

    def shift(self, value, **by):
        if not any(by.values()):
            return value
        return lax.ppermute(value, AXES, self.pairs(**by))

    def along(self, value, moves, dx=0, dy=0):
        out = []
        for x in range(self.dp):
            for a, b in moves:
                for y in range(self.rows):
                    for c in range(2):
                        target = self.index((x + dx) % self.dp, b, (y + dy) % self.rows, c)
                        out.append((self.index(x, a, y, c), target))
        return lax.ppermute(value, AXES, out)

    def splits_list(self):
        return [(dx, dy) for dx in range(self.dp) for dy in range(self.rows)]


def slot_kernel(plan, weight_rows, earlier, ids, *refs):
    weight_count = len(weight_rows)
    packs, rest = refs[: plan.sources], refs[plan.sources :]
    weight_refs, rest = rest[:weight_count], rest[weight_count:]
    earlier_refs, rest = rest[:earlier], rest[earlier:]
    count = plan.splits if earlier else 1
    p_ref, back_refs, (grads, heads, weights) = rest[0], rest[1 : 1 + count], rest[1 + count :]
    tokens, cap, part, top, head_dim = plan.tokens, plan.cap, plan.part, plan.top, plan.head_dim
    pair_rows = 2 * cap
    pair_total = plan.sources // 2
    length = plan.planes * plan.back

    def put(s, slot, at, value):
        if earlier:
            start = (s % 2) * length + slot * plan.back + at
            back_refs[s // 2][pl.ds(start, value.shape[0]), :] = value
        else:
            back_refs[0][s, pl.ds(at, value.shape[0]), :] = value


    for i in range(plan.rows):
        row = ids[plan.rows + i]
        for ref, (first, where) in zip(weight_refs, weight_rows):
            for r in range(ref.shape[0] // head_dim):
                wanted = row == first + r
                if where is not None:
                    wanted = wanted & (ids[2 * plan.rows] == where)

                @pl.when(wanted)
                def _():
                    weights[i] = ref[pl.ds(r * head_dim, head_dim), :]

    row_of = lax.broadcasted_iota(jnp.int32, (cap, tokens), 0)
    diagonal = (row_of == lax.broadcasted_iota(jnp.int32, (cap, tokens), 1)).astype(jnp.float32)
    before = (
        lax.broadcasted_iota(jnp.int32, (tokens, tokens), 0)
        < lax.broadcasted_iota(jnp.int32, (tokens, tokens), 1)
    ).astype(jnp.bfloat16)
    block_row = lax.broadcasted_iota(jnp.int32, (16, LANES), 0)
    empty = jnp.zeros((cap, tokens), jnp.bfloat16)
    chunk = min(part, 512)
    for q in range(pair_total):
        hots, gates, chosen = {}, {}, {}
        for b in range(2):
            pack = packs[2 * q + b]
            meta = pack[pl.ds(0, 2 * top), pl.ds(part + top * head_dim, LANES)].astype(jnp.float32)
            masks, occupied = [], []
            for i in range(plan.rows):
                mask = (meta[top:] == ids[i].astype(jnp.float32)).astype(jnp.float32)
                masks.append(mask)
                occupied.append(jnp.sum(mask, axis=0, keepdims=True))
            filled = occupied + [jnp.zeros((1, tokens), jnp.float32)] * (-plan.rows % 16)
            places = jnp.dot(
                jnp.concatenate(filled, axis=0).astype(jnp.bfloat16),
                before,
                preferred_element_type=jnp.float32,
            )
            wide = []
            for i in range(plan.rows):
                place = places[i : i + 1].astype(jnp.int32)
                hot = jnp.where(row_of == place, occupied[i], 0.0)
                gate_row = jnp.sum(masks[i] * meta[:top], axis=0, keepdims=True)
                gates[i, b] = jnp.sum(hot * gate_row, axis=1, keepdims=True)
                hots[i, b] = hot.astype(jnp.bfloat16)
                wide.append(
                    jnp.concatenate(
                        [(hot * masks[i][k : k + 1]).astype(jnp.bfloat16) for k in range(top)], axis=1
                    )
                )
            raw = jnp.concatenate(
                [pack[:, pl.ds(part + k * head_dim, head_dim)] for k in range(top)], axis=0
            )
            rows = jnp.dot(
                jnp.concatenate(wide, axis=0), raw, preferred_element_type=jnp.float32
            ).astype(jnp.bfloat16)
            for i in range(plan.rows):
                heads[i, pl.ds(q * pair_rows + b * cap, cap), :] = rows[i * cap : (i + 1) * cap]
        all_hots = jnp.concatenate(
            [
                jnp.concatenate([hots[i, b], empty] if b == 0 else [empty, hots[i, b]], axis=1)
                for i in range(plan.rows)
                for b in range(2)
            ],
            axis=0,
        )
        sums = [jnp.zeros((pair_rows, LANES), jnp.float32) for _ in range(plan.rows)]
        for start in range(0, part, chunk):
            both = jnp.concatenate(
                [packs[2 * q + b][:, pl.ds(start, chunk)] for b in range(2)], axis=0
            )
            grad = jnp.dot(all_hots, both, preferred_element_type=jnp.float32)
            for i in range(plan.rows):
                at = i * pair_rows
                pre = jnp.dot(
                    heads[i, pl.ds(q * pair_rows, pair_rows), :],
                    weights[i, :, pl.ds(start, chunk)],
                    preferred_element_type=jnp.float32,
                )
                gate = jnp.broadcast_to(
                    jnp.concatenate([gates[i, 0], gates[i, 1]], axis=0), (pair_rows, LANES)
                )
                for lane in range(0, chunk, LANES):
                    grad_block = grad[at : at + pair_rows, lane : lane + LANES]
                    capped = jnp.tanh(pre[:, lane : lane + LANES] * (1.0 / soft_cap))
                    sums[i] = sums[i] + grad_block * capped
                    grads[i, pl.ds(q * pair_rows, pair_rows), pl.ds(start + lane, LANES)] = (
                        gate * grad_block * (1.0 - capped * capped)
                    ).astype(jnp.bfloat16)
        for b in range(2):
            block = jnp.zeros((16, LANES), jnp.float32)
            for i in range(plan.rows):
                column = jnp.sum(sums[i][b * cap : (b + 1) * cap], axis=1, keepdims=True) * soft_cap
                line = jnp.sum(diagonal * column, axis=0, keepdims=True)
                block = jnp.where(block_row == i, line, block)
            put(2 * q + b, plan.planes - 1, plan.rows * cap, block.astype(jnp.bfloat16))
    for i in range(plan.rows):
        grad_all = grads[i]
        p_ref[pl.ds(i * head_dim, head_dim), :] = lax.dot_general(
            heads[i], grad_all, (((0,), (0,)), ((), ())), preferred_element_type=jnp.float32
        ).astype(p_ref.dtype)
        rows = lax.dot_general(
            grad_all, weights[i], (((1,), (1,)), ((), ())), preferred_element_type=jnp.float32
        ).astype(jnp.bfloat16)
        for s in range(plan.sources):
            put(s, plan.planes - 1, i * cap, rows[s * cap : (s + 1) * cap])
    for j, ref in enumerate(earlier_refs):
        for s in range(plan.sources):
            put(s, j, 0, ref[s])


def slot_work(plan, ids, packs, weights, kind, earlier=()):
    rows = plan.sources * plan.cap
    if earlier:
        backs = (
            jax.ShapeDtypeStruct((2 * plan.planes * plan.back, LANES), jnp.bfloat16),
        ) * plan.splits
    else:
        backs = (jax.ShapeDtypeStruct((plan.sources, plan.back, LANES), jnp.bfloat16),)
    vmem = pl.BlockSpec(memory_space=pltpu.VMEM)
    return pl.pallas_call(
        functools.partial(slot_kernel, plan, [rows for _, *rows in weights], len(earlier)),
        out_shape=(jax.ShapeDtypeStruct((plan.rows * plan.head_dim, plan.part), kind), *backs),
        in_specs=[pl.BlockSpec(memory_space=pltpu.SMEM)]
        + [vmem] * (plan.sources + len(weights) + len(earlier)),
        out_specs=(vmem,) * (1 + len(backs)),
        scratch_shapes=[
            pltpu.VMEM((plan.rows, rows, plan.part), jnp.bfloat16),
            pltpu.VMEM((plan.rows, rows, plan.head_dim), jnp.bfloat16),
            pltpu.VMEM((plan.rows, plan.head_dim, plan.part), jnp.bfloat16),
        ],
        compiler_params=pltpu.CompilerParams(vmem_limit_bytes=20 * 1024 * 1024),
    )(ids, *packs, *[array for array, *_ in weights], *earlier)


def sum_kernel(plan, starts, *refs):
    parts, pieces = refs[: len(refs) - plan.splits], refs[len(refs) - plan.splits :]
    rows = plan.head_dim // plan.dp
    for j, piece in enumerate(pieces):
        at = pl.ds(pl.multiple_of(starts[j], rows), rows)
        total = parts[0][at, :].astype(jnp.float32)
        for ref in parts[1:]:
            total = total + ref[at, :].astype(jnp.float32)
        piece[...] = total.astype(piece.dtype)


def sum_work(plan, starts, parts, own_kind):
    rows = plan.head_dim // plan.dp
    vmem = pl.BlockSpec(memory_space=pltpu.VMEM)
    return pl.pallas_call(
        functools.partial(sum_kernel, plan),
        out_shape=tuple(
            jax.ShapeDtypeStruct((rows, plan.part), jnp.bfloat16 if j else own_kind)
            for j in range(plan.splits)
        ),
        in_specs=[pl.BlockSpec(memory_space=pltpu.SMEM)] + [vmem] * len(parts),
        out_specs=(vmem,) * plan.splits,
    )(starts, *parts)


def layout_kernel(plan, starts, *refs):
    out_ref = refs[-1]
    for j in range(plan.splits):
        at = pl.ds(pl.multiple_of(starts[j], plan.part), plan.part)
        total = None
        for ref in refs[j : -1 : plan.splits]:
            piece = ref[...].astype(jnp.float32)
            total = piece if total is None else total + piece
        out_ref[:, at] = total


def layout_work(plan, starts, pieces):
    rows = plan.head_dim // plan.dp
    vmem = pl.BlockSpec(memory_space=pltpu.VMEM)
    return pl.pallas_call(
        functools.partial(layout_kernel, plan),
        out_shape=jax.ShapeDtypeStruct((rows, plan.part * plan.splits), jnp.float32),
        in_specs=[pl.BlockSpec(memory_space=pltpu.SMEM)] + [vmem] * len(pieces),
        out_specs=vmem,
    )(starts, *pieces)


def merge_kernel(plan, *refs):
    parts, outs = refs[: plan.splits], refs[plan.splits :]
    length = plan.planes * plan.back
    for dc, out in enumerate(outs):
        total = None
        for ref in parts:
            piece = ref[pl.ds(dc * length, length), :].astype(jnp.float32)
            total = piece if total is None else total + piece
        out[...] = total.astype(out.dtype)


def merge_work(plan, parts):
    vmem = pl.BlockSpec(memory_space=pltpu.VMEM)
    rows = jax.ShapeDtypeStruct((plan.planes * plan.back, LANES), jnp.bfloat16)
    return pl.pallas_call(
        functools.partial(merge_kernel, plan),
        out_shape=(rows, rows),
        in_specs=[vmem] * plan.splits,
        out_specs=(vmem, vmem),
    )(*parts)


def final_kernel(plan, target_ref, gate_ref, place_ref, own_ref, other_ref, head_ref, out_gate_ref):
    length = plan.planes * plan.back
    table = jnp.concatenate([own_ref[...], other_ref[...]], axis=0)
    block = 256
    count = plan.tokens * plan.top
    for start in range(0, count, block):
        slot_of = lax.broadcasted_iota(jnp.int32, (block, 2 * length), 1)
        hot = (slot_of == target_ref[pl.ds(start, block), :]).astype(jnp.bfloat16)
        head_ref[pl.ds(start, block), :] = jnp.dot(
            hot, table, preferred_element_type=jnp.float32
        ).astype(jnp.bfloat16)
        hot = (slot_of == gate_ref[pl.ds(start, block), :]).astype(jnp.bfloat16)
        lines = jnp.dot(hot, table, preferred_element_type=jnp.float32)
        lane_of = lax.broadcasted_iota(jnp.int32, (block, LANES), 1)
        out_gate_ref[pl.ds(start, block), :] = jnp.sum(
            jnp.where(lane_of == place_ref[pl.ds(start, block), :], lines, 0.0),
            axis=1,
            keepdims=True,
        )


def final_work(plan, target, gate_line, place, own, other):
    count = plan.tokens * plan.top
    return pl.pallas_call(
        functools.partial(final_kernel, plan),
        out_shape=(
            jax.ShapeDtypeStruct((count, plan.head_dim), jnp.bfloat16),
            jax.ShapeDtypeStruct((count, 1), jnp.float32),
        ),
        in_specs=[pl.BlockSpec(memory_space=pltpu.VMEM)] * 5,
        out_specs=(
            pl.BlockSpec(memory_space=pltpu.VMEM),
            pl.BlockSpec(memory_space=pltpu.VMEM),
        ),
        compiler_params=pltpu.CompilerParams(vmem_limit_bytes=24 * 1024 * 1024),
    )(target, gate_line, place, own, other)


def local(mesh, head_outputs, out_grad, gate_weights, route_ids, out_proj):
    tokens, top, head_dim = head_outputs.shape
    features = out_grad.shape[1]
    plan = Plan(mesh, tokens, top, head_dim, features)
    x = lax.axis_index("dp")
    me = lax.axis_index("expert")
    z, y, c = me // GROUP, (me % GROUP) // 2, me % 2

    weight_parts = []
    for dy in range(plan.rows):
        split = x * plan.rows + (y + dy) % plan.rows
        weight_parts.append(lax.dynamic_slice_in_dim(out_proj[0], split * plan.part, plan.part, 1))
    out_grad, weight_parts = lax.optimization_barrier((out_grad, weight_parts))
    weight_parts = [plan.shift(piece, dy=dy) for dy, piece in enumerate(weight_parts)]
    own_weights = jnp.concatenate(weight_parts, axis=0)

    meta = jnp.concatenate(
        [
            gate_weights.T,
            route_ids.T.astype(jnp.bfloat16),
            jnp.zeros((LANES - 2 * top, tokens), jnp.bfloat16),
        ],
        axis=0,
    )
    flat_heads = head_outputs.reshape(tokens, top * head_dim)
    near_packs = []
    for dx, dy in plan.splits_list():
        split = ((x + dx) % plan.dp) * plan.rows + (y + dy) % plan.rows
        piece = lax.dynamic_slice_in_dim(out_grad, split * plan.part, plan.part, 1)
        value = jnp.concatenate([piece, flat_heads, meta], axis=1)
        if dx or dy:
            value = plan.shift(value, dx=dx, dy=dy)
        else:
            value, own_weights = lax.optimization_barrier((value, own_weights))
        near_packs.append(value)

    if plan.planes == 4:
        inner = (z == 1) | (z == 2)
        mates, middle = [(0, 1), (1, 0), (2, 3), (3, 2)], [(1, 2), (2, 1)]
        outward, inward, across = [(1, 0), (2, 3)], [(0, 1), (3, 2)], [(1, 3), (2, 0)]
        plane_of = jnp.stack([z, jnp.where(z < 2, 2, 1), jnp.where(z < 2, 3, 0), z ^ 1])
        mate = plan.along(own_weights, mates)
        near_in = [plan.along(piece, middle) for piece in weight_parts]
        near_out = [plan.along(piece, outward) for piece in near_in]
        far_in, near_out = lax.optimization_barrier((plan.along(mate, middle), near_out))
        far_out = plan.along(far_in, outward)
        near_packs[1:], near_in = lax.optimization_barrier((near_packs[1:], near_in))
        weights = [
            [(piece, dy, None) for dy, piece in enumerate(weight_parts)],
            [(piece, dy, 0) for dy, piece in enumerate(near_in)]
            + [(piece, dy, 1) for dy, piece in enumerate(near_out)],
            [(far_in, 0, 0), (far_out, 0, 1)],
            [(mate, 0, None)],
        ]
        which = jnp.where(inner, 0, 1)
    else:
        steps = list(range(plan.planes))
        plane_of = (z + jnp.array(steps, jnp.int32)) % plan.planes
        weights = [[(plan.shift(own_weights, dz=-k % plan.planes), 0, None)] for k in steps]
        which = z * 0
    packs = []
    for value in near_packs:
        packs += [value, plan.shift(value, dc=1)]

    routes, own_weights = lax.optimization_barrier((route_ids.reshape(tokens * top), own_weights))
    hot = (routes[:, None] == jnp.arange(plan.experts, dtype=jnp.int32)[None, :]).astype(jnp.float32)
    per_token = hot.reshape(tokens, top, plan.experts).sum(axis=1)
    earlier = jnp.tril(jnp.ones((tokens, tokens), jnp.float32), -1)
    places = jnp.dot(earlier, per_token)
    place = jnp.sum(
        hot.reshape(tokens, top, plan.experts) * places[:, None, :], axis=2
    ).astype(jnp.int32).reshape(tokens * top)
    slots = jnp.arange(plan.planes, dtype=jnp.int32)
    slot = jnp.sum(
        jnp.where((routes // GROUP)[:, None] == plane_of[None, :], slots[None, :], 0), axis=1
    )
    row = (routes % GROUP) // 2
    side = (routes % 2) ^ c
    base = side * (plan.planes * plan.back) + slot * plan.back
    target = (base + row * plan.cap + place)[:, None]
    gate_line = (base + plan.rows * plan.cap + row)[:, None]
    place = place[:, None]

    rows_at = jnp.arange(plan.rows, dtype=jnp.int32)
    weight_at = (y - rows_at) % plan.rows
    expert_ids = (plane_of[:, None] * GROUP + rows_at[None, :] * 2 + c).astype(jnp.int32)
    sums, backs, done = [], [], (target, gate_line, place)
    for j in range(plan.planes):
        last = j == plan.planes - 1
        ids = jnp.concatenate([expert_ids[j], weight_at, which[None]]).astype(jnp.int32)
        ids, done = lax.optimization_barrier((ids, done))
        if j == 0:
            target, gate_line, place = done
        kind = jnp.bfloat16 if j else jnp.float32
        part, *back = slot_work(plan, ids, packs, weights[j], kind, backs if last else ())
        sums.append(part)
        backs = back if last else backs + back
        done = back[0]

    own_rows = head_dim // plan.dp
    starts = jnp.stack(
        [
            ((y + dy) % plan.rows) * head_dim + ((x + dx) % plan.dp) * own_rows
            for dx, dy in plan.splits_list()
        ]
    ).astype(jnp.int32)
    far_pieces = []
    if plan.planes == 4:
        near_sum = sums[1] + plan.along(sums[1], inward)
        backs, near_sum = lax.optimization_barrier((backs, near_sum))
        received = [plan.along(sums[3], mates), plan.along(near_sum, middle)]
        far_pieces = sum_work(plan, starts, [sums[2], plan.along(sums[2], inward)], jnp.bfloat16)
    else:
        received = [plan.shift(sums[j], dz=steps[j]) for j in range(1, plan.planes)]
    pieces = sum_work(plan, starts, [sums[0]] + received, jnp.float32)
    sent = (pieces, far_pieces)
    if plan.planes == 4:
        far_pieces = [
            plan.along(piece, across, dx, dy)
            for piece, (dx, dy) in zip(far_pieces, plan.splits_list())
        ]
    pieces = [
        plan.shift(piece, dx=dx, dy=dy) for piece, (dx, dy) in zip(pieces, plan.splits_list())
    ]

    parts = [
        plan.shift(rows, dx=-dx % plan.dp, dy=-dy % plan.rows)
        for rows, (dx, dy) in zip(backs, plan.splits_list())
    ]
    half = len(far_pieces) // 2
    parts, far_pieces[:half], _ = lax.optimization_barrier((parts, far_pieces[:half], sent))
    own, other = merge_work(plan, parts)
    other = plan.shift(other, dc=1)
    other, far_pieces = lax.optimization_barrier((other, far_pieces))
    grad_head, grad_gate = final_work(plan, target, gate_line, place, own, other)

    starts = jnp.stack(
        [
            (((x - dx) % plan.dp) * plan.rows + (y - dy) % plan.rows) * plan.part
            for dx, dy in plan.splits_list()
        ]
    ).astype(jnp.int32)
    grad_proj = layout_work(plan, starts, pieces + far_pieces)
    return (
        grad_head.reshape(tokens, top, head_dim),
        grad_gate.reshape(tokens, top).astype(jnp.bfloat16),
        grad_proj[None],
    )


def solution(mesh):
    return jax.shard_map(
        functools.partial(local, mesh),
        mesh=mesh,
        in_specs=(
            P(("dp", "expert"), None, None),
            P(("dp", "expert"), None),
            P(("dp", "expert"), None),
            P(("dp", "expert"), None),
            P("expert", None, None),
        ),
        out_specs=(
            P(("dp", "expert"), None, None),
            P(("dp", "expert"), None),
            P("expert", "dp", None),
        ),
        check_vma=False,
    )
```

```python
import functools

import jax
import jax.numpy as jnp
from jax import lax
from jax.experimental import pallas as pl
from jax.experimental.pallas import tpu as pltpu
from jax.sharding import PartitionSpec as P

soft_cap = 1.5
AXES = ("dp", "expert")
GROUP = 4
LANES = 128


class Plan:
    def __init__(self, mesh, tokens, top, head_dim, features):
        self.dp = mesh.shape["dp"]
        self.experts = mesh.shape["expert"]
        self.rows = GROUP // 2
        self.planes = self.experts // GROUP
        self.sources = self.dp * GROUP
        self.tokens, self.top, self.head_dim = tokens, top, head_dim
        self.part = features // self.dp
        self.own_rows = head_dim // self.dp
        cap = 9 * tokens * top // (8 * self.experts)
        self.cap = -(-cap // 8) * 8
        self.back = self.cap + 8
        self.width = self.part + top * head_dim + LANES

    def index(self, x, z, y, c):
        return x * self.experts + z * GROUP + y * 2 + c

    def pairs(self, dx=0, dz=0, dy=0, dc=0):
        out = []
        for x in range(self.dp):
            for z in range(self.planes):
                for y in range(self.rows):
                    for c in range(2):
                        target = self.index(
                            (x + dx) % self.dp,
                            (z + dz) % self.planes,
                            (y + dy) % self.rows,
                            c ^ dc,
                        )
                        out.append((self.index(x, z, y, c), target))
        return out

    def shift(self, value, **by):
        if not any(by.values()):
            return value
        return lax.ppermute(value, AXES, self.pairs(**by))

    def along(self, value, moves, dx=0, dy=0):
        out = []
        for x in range(self.dp):
            for a, b in moves:
                for y in range(self.rows):
                    for c in range(2):
                        target = self.index((x + dx) % self.dp, b, (y + dy) % self.rows, c)
                        out.append((self.index(x, a, y, c), target))
        return lax.ppermute(value, AXES, out)

    def info(self, x, z, y, c, plane_of, which):
        values = [((x + dx) % self.dp) * self.own_rows for dx in range(self.dp)]
        self.lanes_at = len(values)
        values += [((x - dx) % self.dp) * self.part for dx in range(self.dp)]
        self.which_at = len(values)
        values += [which]
        self.experts_at = len(values)
        values += [plane_of[j] * GROUP + y * 2 + c for j in range(self.planes)]
        self.planes_at = len(values)
        values += list(plane_of) + [y, c]
        return jnp.stack([jnp.asarray(value, jnp.int32) for value in values])

    def chips(self):
        return [(dx, dy) for dx in range(self.dp) for dy in range(self.rows)]


def slot_kernel(plan, index, where, earlier, info, *refs):
    packs, rest = refs[: plan.sources], refs[plan.sources :]
    weight_refs, rest = rest[: len(where)], rest[len(where) :]
    earlier_refs, rest = rest[:earlier], rest[earlier:]
    count = plan.sources // 2 if earlier else 1
    p_ref, back_refs, (grads, heads, weights) = rest[0], rest[1 : 1 + count], rest[1 + count :]
    tokens, cap, part, top, head_dim = plan.tokens, plan.cap, plan.part, plan.top, plan.head_dim
    pair_rows = 2 * cap
    pair_total = plan.sources // 2
    length = plan.planes * plan.back

    def put(s, slot, at, value):
        if earlier:
            start = (s % 2) * length + slot * plan.back + at
            back_refs[s // 2][pl.ds(start, value.shape[0]), :] = value
        else:
            back_refs[0][s, pl.ds(at, value.shape[0]), :] = value

    if len(where) > 1:
        for ref, kind in zip(weight_refs, where):

            @pl.when(info[plan.which_at] == kind)
            def _():
                weights[...] = ref[...]

        weight_ref = weights
    else:
        weight_ref = weight_refs[0]
    expert = info[plan.experts_at + index].astype(jnp.float32)
    row_of = lax.broadcasted_iota(jnp.int32, (cap, tokens), 0)
    diagonal = (row_of == lax.broadcasted_iota(jnp.int32, (cap, tokens), 1)).astype(jnp.float32)
    before = (
        lax.broadcasted_iota(jnp.int32, (tokens, tokens), 0)
        < lax.broadcasted_iota(jnp.int32, (tokens, tokens), 1)
    ).astype(jnp.bfloat16)
    block_row = lax.broadcasted_iota(jnp.int32, (8, LANES), 0)
    empty = jnp.zeros((cap, tokens), jnp.bfloat16)
    chunk = min(part, 512)

    masks, occupied, gate_rows = [], [], []
    for s in range(plan.sources):
        meta = packs[s][pl.ds(0, 2 * top), pl.ds(part + top * head_dim, LANES)].astype(jnp.float32)
        mask = (meta[top:] == expert).astype(jnp.float32)
        masks.append(mask)
        occupied.append(jnp.sum(mask, axis=0, keepdims=True))
        gate_rows.append(jnp.sum(mask * meta[:top], axis=0, keepdims=True))
    filled = occupied + [jnp.zeros((1, tokens), jnp.float32)] * (-plan.sources % 16)
    places = jnp.dot(
        jnp.concatenate(filled, axis=0).astype(jnp.bfloat16),
        before,
        preferred_element_type=jnp.float32,
    ).astype(jnp.int32)
    for q in range(pair_total):
        hots, gates = [], []
        for b in range(2):
            s = 2 * q + b
            hot = jnp.where(row_of == places[s : s + 1], occupied[s], 0.0)
            gates.append(jnp.sum(hot * gate_rows[s], axis=1, keepdims=True))
            hots.append(hot.astype(jnp.bfloat16))
            wide = jnp.concatenate(
                [(hot * masks[s][k : k + 1]).astype(jnp.bfloat16) for k in range(top)], axis=1
            )
            raw = jnp.concatenate(
                [packs[s][:, pl.ds(part + k * head_dim, head_dim)] for k in range(top)], axis=0
            )
            heads[pl.ds(s * cap, cap), :] = jnp.dot(
                wide, raw, preferred_element_type=jnp.float32
            ).astype(jnp.bfloat16)
        all_hots = jnp.concatenate(
            [
                jnp.concatenate([hots[0], empty], axis=1),
                jnp.concatenate([empty, hots[1]], axis=1),
            ],
            axis=0,
        )
        gate = jnp.broadcast_to(jnp.concatenate(gates, axis=0), (pair_rows, LANES))
        total = jnp.zeros((pair_rows, LANES), jnp.float32)
        rows_at = pl.ds(q * pair_rows, pair_rows)
        for start in range(0, part, chunk):
            both = jnp.concatenate(
                [packs[2 * q + b][:, pl.ds(start, chunk)] for b in range(2)], axis=0
            )
            grad = jnp.dot(all_hots, both, preferred_element_type=jnp.float32)
            pre = jnp.dot(
                heads[rows_at, :], weight_ref[:, pl.ds(start, chunk)], preferred_element_type=jnp.float32
            )
            for lane in range(0, chunk, LANES):
                grad_block = grad[:, lane : lane + LANES]
                capped = jnp.tanh(pre[:, lane : lane + LANES] * (1.0 / soft_cap))
                total = total + grad_block * capped
                grads[rows_at, pl.ds(start + lane, LANES)] = (
                    gate * grad_block * (1.0 - capped * capped)
                ).astype(jnp.bfloat16)
        for b in range(2):
            column = jnp.sum(total[b * cap : (b + 1) * cap], axis=1, keepdims=True) * soft_cap
            line = jnp.sum(diagonal * column, axis=0, keepdims=True)
            block = jnp.where(block_row == 0, line, 0.0).astype(jnp.bfloat16)
            put(2 * q + b, plan.planes - 1, cap, block)
    grad_all = grads[...]
    p_ref[...] = lax.dot_general(
        heads[...], grad_all, (((0,), (0,)), ((), ())), preferred_element_type=jnp.float32
    ).astype(p_ref.dtype)
    rows = lax.dot_general(
        grad_all, weight_ref[...], (((1,), (1,)), ((), ())), preferred_element_type=jnp.float32
    ).astype(jnp.bfloat16)
    for s in range(plan.sources):
        put(s, plan.planes - 1, 0, rows[s * cap : (s + 1) * cap])
    for j, ref in enumerate(earlier_refs):
        for s in range(plan.sources):
            put(s, j, 0, ref[s])


def slot_work(plan, index, info, packs, weights, kind, earlier=()):
    rows = plan.sources * plan.cap
    if earlier:
        backs = (
            jax.ShapeDtypeStruct((2 * plan.planes * plan.back, LANES), jnp.bfloat16),
        ) * (plan.sources // 2)
    else:
        backs = (jax.ShapeDtypeStruct((plan.sources, plan.back, LANES), jnp.bfloat16),)
    vmem = pl.BlockSpec(memory_space=pltpu.VMEM)
    return pl.pallas_call(
        functools.partial(slot_kernel, plan, index, [where for _, where in weights], len(earlier)),
        out_shape=(jax.ShapeDtypeStruct((plan.head_dim, plan.part), kind), *backs),
        in_specs=[pl.BlockSpec(memory_space=pltpu.SMEM)]
        + [vmem] * (plan.sources + len(weights) + len(earlier)),
        out_specs=(vmem,) * (1 + len(backs)),
        scratch_shapes=[
            pltpu.VMEM((rows, plan.part), jnp.bfloat16),
            pltpu.VMEM((rows, plan.head_dim), jnp.bfloat16),
            pltpu.VMEM((plan.head_dim, plan.part), jnp.bfloat16),
        ],
        compiler_params=pltpu.CompilerParams(vmem_limit_bytes=20 * 1024 * 1024),
    )(info, *packs, *[array for array, _ in weights], *earlier)


def sum_kernel(plan, info, *refs):
    parts, pieces = refs[: len(refs) - plan.dp], refs[len(refs) - plan.dp :]
    rows = plan.own_rows
    for j, piece in enumerate(pieces):
        at = pl.ds(pl.multiple_of(info[j], rows), rows)
        total = parts[0][at, :].astype(jnp.float32)
        for ref in parts[1:]:
            total = total + ref[at, :].astype(jnp.float32)
        piece[...] = total.astype(piece.dtype)


def sum_work(plan, info, parts, own_kind):
    rows = plan.head_dim // plan.dp
    vmem = pl.BlockSpec(memory_space=pltpu.VMEM)
    return pl.pallas_call(
        functools.partial(sum_kernel, plan),
        out_shape=tuple(
            jax.ShapeDtypeStruct((rows, plan.part), jnp.bfloat16 if j else own_kind)
            for j in range(plan.dp)
        ),
        in_specs=[pl.BlockSpec(memory_space=pltpu.SMEM)] + [vmem] * len(parts),
        out_specs=(vmem,) * plan.dp,
    )(info, *parts)


def layout_kernel(plan, info, *refs):
    out_ref = refs[-1]
    for j in range(plan.dp):
        at = pl.ds(pl.multiple_of(info[plan.lanes_at + j], plan.part), plan.part)
        total = None
        for ref in refs[j : -1 : plan.dp]:
            piece = ref[...].astype(jnp.float32)
            total = piece if total is None else total + piece
        out_ref[:, at] = total


def layout_work(plan, info, pieces):
    rows = plan.head_dim // plan.dp
    vmem = pl.BlockSpec(memory_space=pltpu.VMEM)
    return pl.pallas_call(
        functools.partial(layout_kernel, plan),
        out_shape=jax.ShapeDtypeStruct((rows, plan.part * plan.dp), jnp.float32),
        in_specs=[pl.BlockSpec(memory_space=pltpu.SMEM)] + [vmem] * len(pieces),
        out_specs=vmem,
    )(info, *pieces)


def merge_kernel(plan, *refs):
    parts, outs = refs[: len(refs) - 2], refs[len(refs) - 2 :]
    length = plan.planes * plan.back
    for dc, out in enumerate(outs):
        for dy in range(plan.rows):
            total = None
            for ref in parts[dy :: plan.rows]:
                piece = ref[pl.ds(dc * length, length), :].astype(jnp.float32)
                total = piece if total is None else total + piece
            out[pl.ds(dy * length, length), :] = total.astype(out.dtype)


def merge_work(plan, parts):
    vmem = pl.BlockSpec(memory_space=pltpu.VMEM)
    rows = jax.ShapeDtypeStruct((plan.rows * plan.planes * plan.back, LANES), jnp.bfloat16)
    return pl.pallas_call(
        functools.partial(merge_kernel, plan),
        cost_estimate=pl.CostEstimate(flops=1, bytes_accessed=1, transcendentals=0),
        out_shape=(rows, rows),
        in_specs=[vmem] * len(parts),
        out_specs=(vmem, vmem),
    )(*parts)


def target_kernel(plan, info, route_ref, out_ref):
    tokens, top = plan.tokens, plan.top
    count = tokens * top
    lane = lax.broadcasted_iota(jnp.int32, (tokens, LANES), 1)
    routes = route_ref[...]
    named = jnp.zeros((tokens, LANES), jnp.float32)
    listed = jnp.zeros((tokens, LANES), jnp.float32)
    for k in range(top):
        column = routes[:, k : k + 1]
        named = named + (column == lane).astype(jnp.float32)
        listed = listed + jnp.where(lane == k, column, 0).astype(jnp.float32)
    earlier = (
        lax.broadcasted_iota(jnp.int32, (tokens, tokens), 1)
        < lax.broadcasted_iota(jnp.int32, (tokens, tokens), 0)
    ).astype(jnp.bfloat16)
    places = jnp.dot(earlier, named.astype(jnp.bfloat16), preferred_element_type=jnp.float32)
    pair = lax.broadcasted_iota(jnp.int32, (count, LANES), 0)
    lane = lax.broadcasted_iota(jnp.int32, (count, LANES), 1)
    spread = (pair // top == lane).astype(jnp.bfloat16)
    route = jnp.dot(spread, listed.astype(jnp.bfloat16), preferred_element_type=jnp.float32)
    route = jnp.sum(jnp.where(lane == pair % top, route, 0.0), axis=1, keepdims=True)
    route = route.astype(jnp.int32)
    place = jnp.dot(spread, places.astype(jnp.bfloat16), preferred_element_type=jnp.float32)
    place = jnp.sum(jnp.where(lane == route, place, 0.0), axis=1, keepdims=True).astype(jnp.int32)
    slot = jnp.zeros_like(route)
    for j in range(plan.planes):
        slot = jnp.where(route // GROUP == info[plan.planes_at + j], j, slot)
    row = (route % GROUP) // 2 - info[plan.planes_at + plan.planes]
    row = jnp.where(row < 0, row + plan.rows, row)
    side = jnp.where(route % 2 == info[plan.planes_at + plan.planes + 1], 0, 1)
    base = ((side * plan.rows + row) * plan.planes + slot) * plan.back
    target = base + place
    gate_line = base + plan.cap
    out_ref[...] = jnp.where(lane == 0, target, jnp.where(lane == 1, gate_line, place))


def target_work(plan, info, route_ids):
    vmem = pl.BlockSpec(memory_space=pltpu.VMEM)
    return pl.pallas_call(
        functools.partial(target_kernel, plan),
        out_shape=jax.ShapeDtypeStruct((plan.tokens * plan.top, LANES), jnp.int32),
        in_specs=[pl.BlockSpec(memory_space=pltpu.SMEM), vmem],
        out_specs=vmem,
        compiler_params=pltpu.CompilerParams(vmem_limit_bytes=16 * 1024 * 1024),
    )(info, route_ids)


def final_kernel(plan, target_ref, own_ref, other_ref, head_ref, out_gate_ref):
    length = plan.rows * plan.planes * plan.back
    table = jnp.concatenate([own_ref[...], other_ref[...]], axis=0)
    block = 256
    for start in range(0, plan.tokens * plan.top, block):
        at = pl.ds(start, block)
        slot_of = lax.broadcasted_iota(jnp.int32, (block, 2 * length), 1)
        hot = (slot_of == target_ref[at, 0:1]).astype(jnp.bfloat16)
        head_ref[at, :] = jnp.dot(hot, table, preferred_element_type=jnp.float32).astype(jnp.bfloat16)
        hot = (slot_of == target_ref[at, 1:2]).astype(jnp.bfloat16)
        lines = jnp.dot(hot, table, preferred_element_type=jnp.float32)
        lane_of = lax.broadcasted_iota(jnp.int32, (block, LANES), 1)
        out_gate_ref[at, :] = jnp.sum(
            jnp.where(lane_of == target_ref[at, 2:3], lines, 0.0), axis=1, keepdims=True
        )


def final_work(plan, target, own, other):
    count = plan.tokens * plan.top
    vmem = pl.BlockSpec(memory_space=pltpu.VMEM)
    return pl.pallas_call(
        functools.partial(final_kernel, plan),
        cost_estimate=pl.CostEstimate(flops=1, bytes_accessed=1, transcendentals=0),
        out_shape=(
            jax.ShapeDtypeStruct((count, plan.head_dim), jnp.bfloat16),
            jax.ShapeDtypeStruct((count, 1), jnp.float32),
        ),
        in_specs=[vmem] * 3,
        out_specs=(vmem, vmem),
        compiler_params=pltpu.CompilerParams(vmem_limit_bytes=24 * 1024 * 1024),
    )(target, own, other)


def local(mesh, head_outputs, out_grad, gate_weights, route_ids, out_proj):
    tokens, top, head_dim = head_outputs.shape
    features = out_grad.shape[1]
    plan = Plan(mesh, tokens, top, head_dim, features)
    x = lax.axis_index("dp")
    me = lax.axis_index("expert")
    z, y, c = me // GROUP, (me % GROUP) // 2, me % 2

    if plan.planes == 4:
        inner = (z == 1) | (z == 2)
        mates, middle = [(0, 1), (1, 0), (2, 3), (3, 2)], [(1, 2), (2, 1)]
        outward, inward = [(1, 0), (2, 3)], [(0, 1), (3, 2)]
        across = [(1, 3), (2, 0)]
        plane_of = [jnp.where(z < 2, 2, 1), jnp.where(z < 2, 3, 0), z ^ 1, z]
        which = jnp.where(inner, 0, 1)
    else:
        steps = [k % plan.planes for k in range(1, plan.planes + 1)]
        plane_of = [(z + k) % plan.planes for k in steps]
        which = 0
    info = plan.info(x, z, y, c, plane_of, which)

    own_weights = lax.dynamic_slice_in_dim(out_proj[0], x * plan.part, plan.part, 1)
    if plan.planes == 4:
        mate = plan.along(own_weights, mates)
        near_in = plan.along(own_weights, middle)
        near_out = plan.along(near_in, outward)
        far_in, near_out = lax.optimization_barrier((plan.along(mate, middle), near_out))
        far_out = plan.along(far_in, outward)
    else:
        weights = [[(plan.shift(own_weights, dz=-k % plan.planes), None)] for k in steps]

    meta = jnp.concatenate(
        [
            gate_weights.T,
            route_ids.T.astype(jnp.bfloat16),
            jnp.zeros((LANES - 2 * top, tokens), jnp.bfloat16),
        ],
        axis=0,
    )
    flat_heads = head_outputs.reshape(tokens, top * head_dim)
    packs = []
    for dx, dy in plan.chips():
        piece = lax.dynamic_slice_in_dim(out_grad, ((x + dx) % plan.dp) * plan.part, plan.part, 1)
        value = jnp.concatenate([piece, flat_heads, meta], axis=1)
        value = plan.shift(value, dx=dx, dy=dy)
        if plan.planes == 4:
            if dx or dy:
                value, near_in, mate = lax.optimization_barrier((value, near_in, mate))
            else:
                value, near_out = lax.optimization_barrier((value, near_out))
        packs += [value, plan.shift(value, dc=1)]

    if plan.planes == 4:
        weights = [
            [(near_in, 0), (near_out, 1)],
            [(far_in, 0), (far_out, 1)],
            [(mate, None)],
            [(own_weights, None)],
        ]

    target = target_work(plan, info, route_ids)

    sums, backs, done = [], [], target
    for j in range(plan.planes):
        last = j == plan.planes - 1
        if last and plan.planes == 4:
            near_sum = sums[0] + plan.along(sums[0], inward)
            done = (done, near_sum)
        info, done = lax.optimization_barrier((info, done))
        target = target if j else done
        kind = jnp.float32 if last else jnp.bfloat16
        part, *back = slot_work(plan, j, info, packs, weights[j], kind, backs if last else ())
        sums.append(part)
        backs = back if last else backs + back
        done = back[0]

    far_pieces = []
    if plan.planes == 4:
        far_part = plan.along(sums[1], inward)
        far_part, done = lax.optimization_barrier((far_part, done))
        far_pieces = sum_work(plan, info, [sums[1], far_part], jnp.bfloat16)
        info, far_pieces = lax.optimization_barrier((info, far_pieces))
        far_pieces = [plan.along(piece, across, dx) for dx, piece in enumerate(far_pieces)]
        received = [plan.along(sums[2], mates), plan.along(near_sum, middle)]
    else:
        received = [plan.shift(sums[j], dz=steps[j]) for j in range(plan.planes - 1)]
    pieces = sum_work(plan, info, [sums[-1]] + received, jnp.float32)
    sent = pieces[0]
    pieces = [plan.shift(piece, dx=dx) for dx, piece in enumerate(pieces)]

    backs = [
        plan.shift(rows, dx=-dx % plan.dp, dy=-dy % plan.rows)
        for rows, (dx, dy) in zip(backs, plan.chips())
    ]
    half = len(far_pieces) // 2
    backs, far_pieces[:half], _ = lax.optimization_barrier((backs, far_pieces[:half], sent))
    own, other = merge_work(plan, backs)
    grad_head, grad_gate = final_work(plan, target, own, plan.shift(other, dc=1))
    grad_proj = layout_work(plan, info, pieces + far_pieces)
    return (
        grad_head.reshape(tokens, top, head_dim),
        grad_gate.reshape(tokens, top).astype(jnp.bfloat16),
        grad_proj[None],
    )


def solution(mesh):
    return jax.shard_map(
        functools.partial(local, mesh),
        mesh=mesh,
        in_specs=(
            P(("dp", "expert"), None, None),
            P(("dp", "expert"), None),
            P(("dp", "expert"), None),
            P(("dp", "expert"), None),
            P("expert", None, None),
        ),
        out_specs=(
            P(("dp", "expert"), None, None),
            P(("dp", "expert"), None),
            P("expert", "dp", None),
        ),
        check_vma=False,
    )
```

```python
import functools

import jax
import jax.numpy as jnp
from jax import lax
from jax.experimental import pallas as pl
from jax.experimental.pallas import tpu as pltpu
from jax.sharding import PartitionSpec as P

soft_cap = 1.5
AXES = ("dp", "expert")
GROUP = 4
LANES = 128


class Plan:
    def __init__(self, mesh, tokens, top, head_dim, features):
        self.dp = mesh.shape["dp"]
        self.experts = mesh.shape["expert"]
        self.rows = GROUP // 2
        self.planes = self.experts // GROUP
        self.sources = self.dp * GROUP
        self.tokens, self.top, self.head_dim = tokens, top, head_dim
        self.part = features // self.dp
        self.own_rows = head_dim // self.dp
        cap = 9 * tokens * top // (8 * self.experts)
        self.cap = -(-cap // 8) * 8
        self.back = self.cap + 8
        self.width = self.part + top * head_dim + LANES

    def index(self, x, z, y, c):
        return x * self.experts + z * GROUP + y * 2 + c

    def pairs(self, dx=0, dz=0, dy=0, dc=0):
        out = []
        for x in range(self.dp):
            for z in range(self.planes):
                for y in range(self.rows):
                    for c in range(2):
                        target = self.index(
                            (x + dx) % self.dp,
                            (z + dz) % self.planes,
                            (y + dy) % self.rows,
                            c ^ dc,
                        )
                        out.append((self.index(x, z, y, c), target))
        return out

    def shift(self, value, **by):
        if not any(by.values()):
            return value
        return lax.ppermute(value, AXES, self.pairs(**by))

    def along(self, value, moves, dx=0, dy=0):
        out = []
        for x in range(self.dp):
            for a, b in moves:
                for y in range(self.rows):
                    for c in range(2):
                        target = self.index((x + dx) % self.dp, b, (y + dy) % self.rows, c)
                        out.append((self.index(x, a, y, c), target))
        return lax.ppermute(value, AXES, out)

    def info(self, x, z, y, c, plane_of, which):
        values = [((x + dx) % self.dp) * self.own_rows for dx in range(self.dp)]
        self.lanes_at = len(values)
        values += [((x - dx) % self.dp) * self.part for dx in range(self.dp)]
        self.which_at = len(values)
        values += [which]
        self.experts_at = len(values)
        values += [plane_of[j] * GROUP + y * 2 + c for j in range(self.planes)]
        self.planes_at = len(values)
        values += list(plane_of) + [y, c]
        return jnp.stack([jnp.asarray(value, jnp.int32) for value in values])

    def chips(self):
        return [(dx, dy) for dx in range(self.dp) for dy in range(self.rows)]


def slot_kernel(plan, index, where, earlier, info, *refs):
    packs, rest = refs[: plan.sources], refs[plan.sources :]
    weight_refs, rest = rest[: len(where)], rest[len(where) :]
    earlier_refs, rest = rest[:earlier], rest[earlier:]
    count = plan.sources // 2 if earlier else 1
    p_ref, back_refs, (grads, heads, weights) = rest[0], rest[1 : 1 + count], rest[1 + count :]
    tokens, cap, part, top, head_dim = plan.tokens, plan.cap, plan.part, plan.top, plan.head_dim
    pair_rows = 2 * cap
    pair_total = plan.sources // 2
    length = plan.planes * plan.back

    def put(s, slot, at, value):
        if earlier:
            start = (s % 2) * length + slot * plan.back + at
            back_refs[s // 2][pl.ds(start, value.shape[0]), :] = value
        else:
            back_refs[0][s, pl.ds(at, value.shape[0]), :] = value

    if len(where) > 1:
        for ref, kind in zip(weight_refs, where):

            @pl.when(info[plan.which_at] == kind)
            def _():
                weights[...] = ref[...]

        weight_ref = weights
    else:
        weight_ref = weight_refs[0]
    expert = info[plan.experts_at + index].astype(jnp.float32)
    row_of = lax.broadcasted_iota(jnp.int32, (cap, tokens), 0)
    diagonal = (row_of == lax.broadcasted_iota(jnp.int32, (cap, tokens), 1)).astype(jnp.float32)
    before = (
        lax.broadcasted_iota(jnp.int32, (tokens, tokens), 0)
        < lax.broadcasted_iota(jnp.int32, (tokens, tokens), 1)
    ).astype(jnp.bfloat16)
    block_row = lax.broadcasted_iota(jnp.int32, (8, LANES), 0)
    empty = jnp.zeros((cap, tokens), jnp.bfloat16)
    chunk = min(part, 512)

    masks, occupied, gate_rows = [], [], []
    for s in range(plan.sources):
        meta = packs[s][pl.ds(0, 2 * top), pl.ds(part + top * head_dim, LANES)].astype(jnp.float32)
        mask = (meta[top:] == expert).astype(jnp.float32)
        masks.append(mask)
        occupied.append(jnp.sum(mask, axis=0, keepdims=True))
        gate_rows.append(jnp.sum(mask * meta[:top], axis=0, keepdims=True))
    filled = occupied + [jnp.zeros((1, tokens), jnp.float32)] * (-plan.sources % 16)
    places = jnp.dot(
        jnp.concatenate(filled, axis=0).astype(jnp.bfloat16),
        before,
        preferred_element_type=jnp.float32,
    ).astype(jnp.int32)
    for q in range(pair_total):
        hots, gates = [], []
        for b in range(2):
            s = 2 * q + b
            hot = jnp.where(row_of == places[s : s + 1], occupied[s], 0.0)
            gates.append(jnp.sum(hot * gate_rows[s], axis=1, keepdims=True))
            hots.append(hot.astype(jnp.bfloat16))
            wide = jnp.concatenate(
                [(hot * masks[s][k : k + 1]).astype(jnp.bfloat16) for k in range(top)], axis=1
            )
            raw = jnp.concatenate(
                [packs[s][:, pl.ds(part + k * head_dim, head_dim)] for k in range(top)], axis=0
            )
            heads[pl.ds(s * cap, cap), :] = jnp.dot(
                wide, raw, preferred_element_type=jnp.float32
            ).astype(jnp.bfloat16)
        all_hots = jnp.concatenate(
            [
                jnp.concatenate([hots[0], empty], axis=1),
                jnp.concatenate([empty, hots[1]], axis=1),
            ],
            axis=0,
        )
        gate = jnp.broadcast_to(jnp.concatenate(gates, axis=0), (pair_rows, LANES))
        total = jnp.zeros((pair_rows, LANES), jnp.float32)
        rows_at = pl.ds(q * pair_rows, pair_rows)
        for start in range(0, part, chunk):
            both = jnp.concatenate(
                [packs[2 * q + b][:, pl.ds(start, chunk)] for b in range(2)], axis=0
            )
            grad = jnp.dot(all_hots, both, preferred_element_type=jnp.float32)
            pre = jnp.dot(
                heads[rows_at, :], weight_ref[:, pl.ds(start, chunk)], preferred_element_type=jnp.float32
            )
            for lane in range(0, chunk, LANES):
                grad_block = grad[:, lane : lane + LANES]
                capped = jnp.tanh(pre[:, lane : lane + LANES] * (1.0 / soft_cap))
                total = total + grad_block * capped
                grads[rows_at, pl.ds(start + lane, LANES)] = (
                    gate * grad_block * (1.0 - capped * capped)
                ).astype(jnp.bfloat16)
        for b in range(2):
            column = jnp.sum(total[b * cap : (b + 1) * cap], axis=1, keepdims=True) * soft_cap
            line = jnp.sum(diagonal * column, axis=0, keepdims=True)
            block = jnp.where(block_row == 0, line, 0.0).astype(jnp.bfloat16)
            put(2 * q + b, plan.planes - 1, cap, block)
    grad_all = grads[...]
    p_ref[...] = lax.dot_general(
        heads[...], grad_all, (((0,), (0,)), ((), ())), preferred_element_type=jnp.float32
    ).astype(p_ref.dtype)
    rows = lax.dot_general(
        grad_all, weight_ref[...], (((1,), (1,)), ((), ())), preferred_element_type=jnp.float32
    ).astype(jnp.bfloat16)
    for s in range(plan.sources):
        put(s, plan.planes - 1, 0, rows[s * cap : (s + 1) * cap])
    for j, ref in enumerate(earlier_refs):
        for s in range(plan.sources):
            put(s, j, 0, ref[s])


def slot_work(plan, index, info, packs, weights, kind, earlier=()):
    rows = plan.sources * plan.cap
    if earlier:
        backs = (
            jax.ShapeDtypeStruct((2 * plan.planes * plan.back, LANES), jnp.bfloat16),
        ) * (plan.sources // 2)
    else:
        backs = (jax.ShapeDtypeStruct((plan.sources, plan.back, LANES), jnp.bfloat16),)
    vmem = pl.BlockSpec(memory_space=pltpu.VMEM)
    return pl.pallas_call(
        functools.partial(slot_kernel, plan, index, [where for _, where in weights], len(earlier)),
        out_shape=(jax.ShapeDtypeStruct((plan.head_dim, plan.part), kind), *backs),
        in_specs=[pl.BlockSpec(memory_space=pltpu.SMEM)]
        + [vmem] * (plan.sources + len(weights) + len(earlier)),
        out_specs=(vmem,) * (1 + len(backs)),
        scratch_shapes=[
            pltpu.VMEM((rows, plan.part), jnp.bfloat16),
            pltpu.VMEM((rows, plan.head_dim), jnp.bfloat16),
            pltpu.VMEM((plan.head_dim, plan.part), jnp.bfloat16),
        ],
        compiler_params=pltpu.CompilerParams(vmem_limit_bytes=14 * 1024 * 1024),
    )(info, *packs, *[array for array, _ in weights], *earlier)


def sum_kernel(plan, info, *refs):
    parts, pieces = refs[: len(refs) - plan.dp], refs[len(refs) - plan.dp :]
    rows = plan.own_rows
    for j, piece in enumerate(pieces):
        at = pl.ds(pl.multiple_of(info[j], rows), rows)
        total = parts[0][at, :].astype(jnp.float32)
        for ref in parts[1:]:
            total = total + ref[at, :].astype(jnp.float32)
        piece[...] = total.astype(piece.dtype)


def sum_work(plan, info, parts, own_kind):
    rows = plan.head_dim // plan.dp
    vmem = pl.BlockSpec(memory_space=pltpu.VMEM)
    return pl.pallas_call(
        functools.partial(sum_kernel, plan),
        compiler_params=pltpu.CompilerParams(vmem_limit_bytes=6 * 1024 * 1024),
        out_shape=tuple(
            jax.ShapeDtypeStruct((rows, plan.part), jnp.bfloat16 if j else own_kind)
            for j in range(plan.dp)
        ),
        in_specs=[pl.BlockSpec(memory_space=pltpu.SMEM)] + [vmem] * len(parts),
        out_specs=(vmem,) * plan.dp,
    )(info, *parts)


def layout_kernel(plan, info, *refs):
    out_ref = refs[-1]
    for j in range(plan.dp):
        at = pl.ds(pl.multiple_of(info[plan.lanes_at + j], plan.part), plan.part)
        total = None
        for ref in refs[j : -1 : plan.dp]:
            piece = ref[...].astype(jnp.float32)
            total = piece if total is None else total + piece
        out_ref[:, at] = total


def layout_work(plan, info, pieces):
    rows = plan.head_dim // plan.dp
    vmem = pl.BlockSpec(memory_space=pltpu.VMEM)
    return pl.pallas_call(
        functools.partial(layout_kernel, plan),
        compiler_params=pltpu.CompilerParams(vmem_limit_bytes=6 * 1024 * 1024),
        out_shape=jax.ShapeDtypeStruct((rows, plan.part * plan.dp), jnp.float32),
        in_specs=[pl.BlockSpec(memory_space=pltpu.SMEM)] + [vmem] * len(pieces),
        out_specs=vmem,
    )(info, *pieces)


def merge_kernel(plan, *refs):
    parts, outs = refs[: len(refs) - 2], refs[len(refs) - 2 :]
    length = plan.planes * plan.back
    for dc, out in enumerate(outs):
        for dy in range(plan.rows):
            total = None
            for ref in parts[dy :: plan.rows]:
                piece = ref[pl.ds(dc * length, length), :].astype(jnp.float32)
                total = piece if total is None else total + piece
            out[pl.ds(dy * length, length), :] = total.astype(out.dtype)


def merge_work(plan, parts):
    vmem = pl.BlockSpec(memory_space=pltpu.VMEM)
    rows = jax.ShapeDtypeStruct((plan.rows * plan.planes * plan.back, LANES), jnp.bfloat16)
    return pl.pallas_call(
        functools.partial(merge_kernel, plan),
        compiler_params=pltpu.CompilerParams(vmem_limit_bytes=6 * 1024 * 1024),
        cost_estimate=pl.CostEstimate(flops=1, bytes_accessed=1, transcendentals=0),
        out_shape=(rows, rows),
        in_specs=[vmem] * len(parts),
        out_specs=(vmem, vmem),
    )(*parts)


def target_kernel(plan, info, route_ref, out_ref):
    tokens, top = plan.tokens, plan.top
    count = tokens * top
    lane = lax.broadcasted_iota(jnp.int32, (tokens, LANES), 1)
    routes = route_ref[...]
    named = jnp.zeros((tokens, LANES), jnp.float32)
    listed = jnp.zeros((tokens, LANES), jnp.float32)
    for k in range(top):
        column = routes[:, k : k + 1]
        named = named + (column == lane).astype(jnp.float32)
        listed = listed + jnp.where(lane == k, column, 0).astype(jnp.float32)
    earlier = (
        lax.broadcasted_iota(jnp.int32, (tokens, tokens), 1)
        < lax.broadcasted_iota(jnp.int32, (tokens, tokens), 0)
    ).astype(jnp.bfloat16)
    places = jnp.dot(earlier, named.astype(jnp.bfloat16), preferred_element_type=jnp.float32)
    pair = lax.broadcasted_iota(jnp.int32, (count, LANES), 0)
    lane = lax.broadcasted_iota(jnp.int32, (count, LANES), 1)
    spread = (pair // top == lane).astype(jnp.bfloat16)
    route = jnp.dot(spread, listed.astype(jnp.bfloat16), preferred_element_type=jnp.float32)
    route = jnp.sum(jnp.where(lane == pair % top, route, 0.0), axis=1, keepdims=True)
    route = route.astype(jnp.int32)
    place = jnp.dot(spread, places.astype(jnp.bfloat16), preferred_element_type=jnp.float32)
    place = jnp.sum(jnp.where(lane == route, place, 0.0), axis=1, keepdims=True).astype(jnp.int32)
    slot = jnp.zeros_like(route)
    for j in range(plan.planes):
        slot = jnp.where(route // GROUP == info[plan.planes_at + j], j, slot)
    row = (route % GROUP) // 2 - info[plan.planes_at + plan.planes]
    row = jnp.where(row < 0, row + plan.rows, row)
    side = jnp.where(route % 2 == info[plan.planes_at + plan.planes + 1], 0, 1)
    base = ((side * plan.rows + row) * plan.planes + slot) * plan.back
    target = base + place
    gate_line = base + plan.cap
    out_ref[...] = jnp.where(lane == 0, target, jnp.where(lane == 1, gate_line, place))


def target_work(plan, info, route_ids):
    vmem = pl.BlockSpec(memory_space=pltpu.VMEM)
    return pl.pallas_call(
        functools.partial(target_kernel, plan),
        out_shape=jax.ShapeDtypeStruct((plan.tokens * plan.top, LANES), jnp.int32),
        in_specs=[pl.BlockSpec(memory_space=pltpu.SMEM), vmem],
        out_specs=vmem,
        compiler_params=pltpu.CompilerParams(vmem_limit_bytes=8 * 1024 * 1024),
    )(info, route_ids)


def final_kernel(plan, target_ref, own_ref, other_ref, head_ref, out_gate_ref):
    length = plan.rows * plan.planes * plan.back
    table = jnp.concatenate([own_ref[...], other_ref[...]], axis=0)
    block = 256
    for start in range(0, plan.tokens * plan.top, block):
        at = pl.ds(start, block)
        slot_of = lax.broadcasted_iota(jnp.int32, (block, 2 * length), 1)
        hot = (slot_of == target_ref[at, 0:1]).astype(jnp.bfloat16)
        head_ref[at, :] = jnp.dot(hot, table, preferred_element_type=jnp.float32).astype(jnp.bfloat16)
        hot = (slot_of == target_ref[at, 1:2]).astype(jnp.bfloat16)
        lines = jnp.dot(hot, table, preferred_element_type=jnp.float32)
        lane_of = lax.broadcasted_iota(jnp.int32, (block, LANES), 1)
        out_gate_ref[at, :] = jnp.sum(
            jnp.where(lane_of == target_ref[at, 2:3], lines, 0.0), axis=1, keepdims=True
        )


def final_work(plan, target, own, other):
    count = plan.tokens * plan.top
    vmem = pl.BlockSpec(memory_space=pltpu.VMEM)
    return pl.pallas_call(
        functools.partial(final_kernel, plan),
        cost_estimate=pl.CostEstimate(flops=1, bytes_accessed=1, transcendentals=0),
        out_shape=(
            jax.ShapeDtypeStruct((count, plan.head_dim), jnp.bfloat16),
            jax.ShapeDtypeStruct((count, 1), jnp.float32),
        ),
        in_specs=[vmem] * 3,
        out_specs=(vmem, vmem),
        compiler_params=pltpu.CompilerParams(vmem_limit_bytes=8 * 1024 * 1024),
    )(target, own, other)


def local(mesh, head_outputs, out_grad, gate_weights, route_ids, out_proj):
    tokens, top, head_dim = head_outputs.shape
    features = out_grad.shape[1]
    plan = Plan(mesh, tokens, top, head_dim, features)
    x = lax.axis_index("dp")
    me = lax.axis_index("expert")
    z, y, c = me // GROUP, (me % GROUP) // 2, me % 2

    if plan.planes == 4:
        inner = (z == 1) | (z == 2)
        mates, middle = [(0, 1), (1, 0), (2, 3), (3, 2)], [(1, 2), (2, 1)]
        outward, inward = [(1, 0), (2, 3)], [(0, 1), (3, 2)]
        across = [(1, 3), (2, 0)]
        plane_of = [jnp.where(z < 2, 2, 1), jnp.where(z < 2, 3, 0), z ^ 1, z]
        which = jnp.where(inner, 0, 1)
    else:
        steps = [k % plan.planes for k in range(1, plan.planes + 1)]
        plane_of = [(z + k) % plan.planes for k in steps]
        which = 0
    info = plan.info(x, z, y, c, plane_of, which)

    own_weights = lax.dynamic_slice_in_dim(out_proj[0], x * plan.part, plan.part, 1)
    target = target_work(plan, info, route_ids)
    if plan.planes == 4:
        mate = plan.along(own_weights, mates)
        near_in = plan.along(own_weights, middle)
        mate, near_in, target = lax.optimization_barrier((mate, near_in, target))
        near_out = plan.along(near_in, outward)
        far_in, near_out = lax.optimization_barrier((plan.along(mate, middle), near_out))
        far_out = plan.along(far_in, outward)
    else:
        weights = [[(plan.shift(own_weights, dz=-k % plan.planes), None)] for k in steps]

    meta = jnp.concatenate(
        [
            gate_weights.T,
            route_ids.T.astype(jnp.bfloat16),
            jnp.zeros((LANES - 2 * top, tokens), jnp.bfloat16),
        ],
        axis=0,
    )
    flat_heads = head_outputs.reshape(tokens, top * head_dim)
    packs = []
    for dx, dy in plan.chips():
        piece = lax.dynamic_slice_in_dim(out_grad, ((x + dx) % plan.dp) * plan.part, plan.part, 1)
        value = jnp.concatenate([piece, flat_heads, meta], axis=1)
        value = plan.shift(value, dx=dx, dy=dy)
        if plan.planes == 4:
            if dx or dy:
                value, near_in, mate = lax.optimization_barrier((value, near_in, mate))
            else:
                value, near_out = lax.optimization_barrier((value, near_out))
        packs += [value, plan.shift(value, dc=1)]

    if plan.planes == 4:
        weights = [
            [(near_in, 0), (near_out, 1)],
            [(far_in, 0), (far_out, 1)],
            [(mate, None)],
            [(own_weights, None)],
        ]

    sums, backs, done = [], [], target
    for j in range(plan.planes):
        last = j == plan.planes - 1
        if last and plan.planes == 4:
            near_sum = sums[0] + plan.along(sums[0], inward)
            done = (done, near_sum)
        info, done = lax.optimization_barrier((info, done))
        target = target if j else done
        kind = jnp.float32 if last else jnp.bfloat16
        part, *back = slot_work(plan, j, info, packs, weights[j], kind, backs if last else ())
        sums.append(part)
        backs = back if last else backs + back
        done = back[0]

    far_pieces = []
    if plan.planes == 4:
        far_part = plan.along(sums[1], inward)
        far_part, done = lax.optimization_barrier((far_part, done))
        far_pieces = sum_work(plan, info, [sums[1], far_part], jnp.bfloat16)
        info, far_pieces = lax.optimization_barrier((info, far_pieces))
        far_pieces = [plan.along(piece, across, dx) for dx, piece in enumerate(far_pieces)]
        received = [plan.along(sums[2], mates), plan.along(near_sum, middle)]
    else:
        received = [plan.shift(sums[j], dz=steps[j]) for j in range(plan.planes - 1)]
    pieces = sum_work(plan, info, [sums[-1]] + received, jnp.float32)
    pieces = [plan.shift(piece, dx=dx) for dx, piece in enumerate(pieces)]

    backs = [
        plan.shift(rows, dx=-dx % plan.dp, dy=-dy % plan.rows)
        for rows, (dx, dy) in zip(backs, plan.chips())
    ]
    backs, far_pieces, pieces = lax.optimization_barrier((backs, far_pieces, pieces))
    own, other = merge_work(plan, backs)
    grad_head, grad_gate = final_work(plan, target, own, plan.shift(other, dc=1))
    grad_proj = layout_work(plan, info, pieces + far_pieces)
    return (
        grad_head.reshape(tokens, top, head_dim),
        grad_gate.reshape(tokens, top).astype(jnp.bfloat16),
        grad_proj[None],
    )


def solution(mesh):
    return jax.shard_map(
        functools.partial(local, mesh),
        mesh=mesh,
        in_specs=(
            P(("dp", "expert"), None, None),
            P(("dp", "expert"), None),
            P(("dp", "expert"), None),
            P(("dp", "expert"), None),
            P("expert", None, None),
        ),
        out_specs=(
            P(("dp", "expert"), None, None),
            P(("dp", "expert"), None),
            P("expert", "dp", None),
        ),
        check_vma=False,
    )
```

```python
import functools

import jax
import jax.numpy as jnp
from jax import lax
from jax.experimental import pallas as pl
from jax.experimental.pallas import tpu as pltpu
from jax.sharding import PartitionSpec as P

soft_cap = 1.5
AXES = ("dp", "expert")
GROUP = 4
LANES = 128


class Plan:
    def __init__(self, mesh, tokens, top, head_dim, features):
        self.dp = mesh.shape["dp"]
        self.experts = mesh.shape["expert"]
        self.rows = GROUP // 2
        self.planes = self.experts // GROUP
        self.sources = self.dp * GROUP
        self.tokens, self.top, self.head_dim = tokens, top, head_dim
        self.part = features // self.dp
        self.own_rows = head_dim // self.dp
        cap = 9 * tokens * top // (8 * self.experts)
        self.cap = -(-cap // 8) * 8
        self.back = self.cap + 8
        self.width = self.part + top * head_dim + LANES

    def index(self, x, z, y, c):
        return x * self.experts + z * GROUP + y * 2 + c

    def pairs(self, dx=0, dz=0, dy=0, dc=0):
        out = []
        for x in range(self.dp):
            for z in range(self.planes):
                for y in range(self.rows):
                    for c in range(2):
                        target = self.index(
                            (x + dx) % self.dp,
                            (z + dz) % self.planes,
                            (y + dy) % self.rows,
                            c ^ dc,
                        )
                        out.append((self.index(x, z, y, c), target))
        return out

    def shift(self, value, **by):
        if not any(by.values()):
            return value
        return lax.ppermute(value, AXES, self.pairs(**by))

    def along(self, value, moves, dx=0, dy=0):
        out = []
        for x in range(self.dp):
            for a, b in moves:
                for y in range(self.rows):
                    for c in range(2):
                        target = self.index((x + dx) % self.dp, b, (y + dy) % self.rows, c)
                        out.append((self.index(x, a, y, c), target))
        return lax.ppermute(value, AXES, out)

    def info(self, x, z, y, c, plane_of, which):
        values = [((x + dx) % self.dp) * self.own_rows for dx in range(self.dp)]
        self.lanes_at = len(values)
        values += [((x - dx) % self.dp) * self.part for dx in range(self.dp)]
        self.which_at = len(values)
        values += [which]
        self.experts_at = len(values)
        values += [plane_of[j] * GROUP + y * 2 + c for j in range(self.planes)]
        self.planes_at = len(values)
        values += list(plane_of) + [y, c]
        return jnp.stack([jnp.asarray(value, jnp.int32) for value in values])

    def chips(self):
        return [(dx, dy) for dx in range(self.dp) for dy in range(self.rows)]


def slot_kernel(plan, index, where, earlier, info, *refs):
    packs, rest = refs[: plan.sources], refs[plan.sources :]
    weight_refs, rest = rest[: len(where)], rest[len(where) :]
    earlier_refs, rest = rest[:earlier], rest[earlier:]
    count = plan.dp if earlier else 1
    p_ref, back_refs, (grads, heads, weights) = rest[0], rest[1 : 1 + count], rest[1 + count :]
    tokens, cap, part, top, head_dim = plan.tokens, plan.cap, plan.part, plan.top, plan.head_dim
    pair_rows = 2 * cap
    pair_total = plan.sources // 2
    length = plan.planes * plan.back

    def put(s, slot, at, value):
        if earlier:
            start = (s % GROUP) * length + slot * plan.back + at
            back_refs[s // GROUP][pl.ds(start, value.shape[0]), :] = value
        else:
            back_refs[0][s, pl.ds(at, value.shape[0]), :] = value

    if len(where) > 1:
        for ref, kind in zip(weight_refs, where):

            @pl.when(info[plan.which_at] == kind)
            def _():
                weights[...] = ref[...]

        weight_ref = weights
    else:
        weight_ref = weight_refs[0]
    expert = info[plan.experts_at + index].astype(jnp.float32)
    row_of = lax.broadcasted_iota(jnp.int32, (cap, tokens), 0)
    diagonal = (row_of == lax.broadcasted_iota(jnp.int32, (cap, tokens), 1)).astype(jnp.float32)
    before = (
        lax.broadcasted_iota(jnp.int32, (tokens, tokens), 0)
        < lax.broadcasted_iota(jnp.int32, (tokens, tokens), 1)
    ).astype(jnp.bfloat16)
    block_row = lax.broadcasted_iota(jnp.int32, (8, LANES), 0)
    empty = jnp.zeros((cap, tokens), jnp.bfloat16)
    chunk = min(part, 512)

    masks, occupied, gate_rows = [], [], []
    for s in range(plan.sources):
        meta = packs[s][pl.ds(0, 2 * top), pl.ds(part + top * head_dim, LANES)].astype(jnp.float32)
        mask = (meta[top:] == expert).astype(jnp.float32)
        masks.append(mask)
        occupied.append(jnp.sum(mask, axis=0, keepdims=True))
        gate_rows.append(jnp.sum(mask * meta[:top], axis=0, keepdims=True))
    filled = occupied + [jnp.zeros((1, tokens), jnp.float32)] * (-plan.sources % 16)
    places = jnp.dot(
        jnp.concatenate(filled, axis=0).astype(jnp.bfloat16),
        before,
        preferred_element_type=jnp.float32,
    ).astype(jnp.int32)
    for q in range(pair_total):
        hots, gates = [], []
        for b in range(2):
            s = 2 * q + b
            hot = jnp.where(row_of == places[s : s + 1], occupied[s], 0.0)
            gates.append(jnp.sum(hot * gate_rows[s], axis=1, keepdims=True))
            hots.append(hot.astype(jnp.bfloat16))
            wide = jnp.concatenate(
                [(hot * masks[s][k : k + 1]).astype(jnp.bfloat16) for k in range(top)], axis=1
            )
            raw = jnp.concatenate(
                [packs[s][:, pl.ds(part + k * head_dim, head_dim)] for k in range(top)], axis=0
            )
            heads[pl.ds(s * cap, cap), :] = jnp.dot(
                wide, raw, preferred_element_type=jnp.float32
            ).astype(jnp.bfloat16)
        all_hots = jnp.concatenate(
            [
                jnp.concatenate([hots[0], empty], axis=1),
                jnp.concatenate([empty, hots[1]], axis=1),
            ],
            axis=0,
        )
        gate = jnp.broadcast_to(jnp.concatenate(gates, axis=0), (pair_rows, LANES))
        total = jnp.zeros((pair_rows, LANES), jnp.float32)
        rows_at = pl.ds(q * pair_rows, pair_rows)
        for start in range(0, part, chunk):
            both = jnp.concatenate(
                [packs[2 * q + b][:, pl.ds(start, chunk)] for b in range(2)], axis=0
            )
            grad = jnp.dot(all_hots, both, preferred_element_type=jnp.float32)
            pre = jnp.dot(
                heads[rows_at, :], weight_ref[:, pl.ds(start, chunk)], preferred_element_type=jnp.float32
            )
            for lane in range(0, chunk, LANES):
                grad_block = grad[:, lane : lane + LANES]
                capped = jnp.tanh(pre[:, lane : lane + LANES] * (1.0 / soft_cap))
                total = total + grad_block * capped
                grads[rows_at, pl.ds(start + lane, LANES)] = (
                    gate * grad_block * (1.0 - capped * capped)
                ).astype(jnp.bfloat16)
        for b in range(2):
            column = jnp.sum(total[b * cap : (b + 1) * cap], axis=1, keepdims=True) * soft_cap
            line = jnp.sum(diagonal * column, axis=0, keepdims=True)
            block = jnp.where(block_row == 0, line, 0.0).astype(jnp.bfloat16)
            put(2 * q + b, plan.planes - 1, cap, block)
    grad_all = grads[...]
    p_ref[...] = lax.dot_general(
        heads[...], grad_all, (((0,), (0,)), ((), ())), preferred_element_type=jnp.float32
    ).astype(p_ref.dtype)
    rows = lax.dot_general(
        grad_all, weight_ref[...], (((1,), (1,)), ((), ())), preferred_element_type=jnp.float32
    ).astype(jnp.bfloat16)
    for s in range(plan.sources):
        put(s, plan.planes - 1, 0, rows[s * cap : (s + 1) * cap])
    for j, ref in enumerate(earlier_refs):
        for s in range(plan.sources):
            put(s, j, 0, ref[s])


def slot_work(plan, index, info, packs, weights, kind, earlier=()):
    rows = plan.sources * plan.cap
    if earlier:
        backs = (
            jax.ShapeDtypeStruct((GROUP * plan.planes * plan.back, LANES), jnp.bfloat16),
        ) * plan.dp
    else:
        backs = (jax.ShapeDtypeStruct((plan.sources, plan.back, LANES), jnp.bfloat16),)
    vmem = pl.BlockSpec(memory_space=pltpu.VMEM)
    return pl.pallas_call(
        functools.partial(slot_kernel, plan, index, [where for _, where in weights], len(earlier)),
        out_shape=(jax.ShapeDtypeStruct((plan.head_dim, plan.part), kind), *backs),
        in_specs=[pl.BlockSpec(memory_space=pltpu.SMEM)]
        + [vmem] * (plan.sources + len(weights) + len(earlier)),
        out_specs=(vmem,) * (1 + len(backs)),
        scratch_shapes=[
            pltpu.VMEM((rows, plan.part), jnp.bfloat16),
            pltpu.VMEM((rows, plan.head_dim), jnp.bfloat16),
            pltpu.VMEM((plan.head_dim, plan.part), jnp.bfloat16),
        ],
        compiler_params=pltpu.CompilerParams(vmem_limit_bytes=14 * 1024 * 1024),
    )(info, *packs, *[array for array, _ in weights], *earlier)


def sum_kernel(plan, info, *refs):
    parts, pieces = refs[: len(refs) - plan.dp], refs[len(refs) - plan.dp :]
    rows = plan.own_rows
    for j, piece in enumerate(pieces):
        at = pl.ds(pl.multiple_of(info[j], rows), rows)
        total = parts[0][at, :].astype(jnp.float32)
        for ref in parts[1:]:
            total = total + ref[at, :].astype(jnp.float32)
        piece[...] = total.astype(piece.dtype)


def sum_work(plan, info, parts, own_kind):
    rows = plan.head_dim // plan.dp
    vmem = pl.BlockSpec(memory_space=pltpu.VMEM)
    return pl.pallas_call(
        functools.partial(sum_kernel, plan),
        compiler_params=pltpu.CompilerParams(vmem_limit_bytes=6 * 1024 * 1024),
        out_shape=tuple(
            jax.ShapeDtypeStruct((rows, plan.part), jnp.bfloat16 if j else own_kind)
            for j in range(plan.dp)
        ),
        in_specs=[pl.BlockSpec(memory_space=pltpu.SMEM)] + [vmem] * len(parts),
        out_specs=(vmem,) * plan.dp,
    )(info, *parts)


def layout_kernel(plan, info, *refs):
    out_ref = refs[-1]
    for j in range(plan.dp):
        at = pl.ds(pl.multiple_of(info[plan.lanes_at + j], plan.part), plan.part)
        total = None
        for ref in refs[j : -1 : plan.dp]:
            piece = ref[...].astype(jnp.float32)
            total = piece if total is None else total + piece
        out_ref[:, at] = total


def layout_work(plan, info, pieces):
    rows = plan.head_dim // plan.dp
    vmem = pl.BlockSpec(memory_space=pltpu.VMEM)
    return pl.pallas_call(
        functools.partial(layout_kernel, plan),
        compiler_params=pltpu.CompilerParams(vmem_limit_bytes=6 * 1024 * 1024),
        out_shape=jax.ShapeDtypeStruct((rows, plan.part * plan.dp), jnp.float32),
        in_specs=[pl.BlockSpec(memory_space=pltpu.SMEM)] + [vmem] * len(pieces),
        out_specs=vmem,
    )(info, *pieces)


def merge_kernel(plan, *refs):
    parts, outs = refs[: plan.dp], refs[plan.dp :]
    length = plan.planes * plan.back
    for j, out in enumerate(outs):
        at = pl.ds(j * length, length)
        total = parts[0][at, :].astype(jnp.float32)
        for ref in parts[1:]:
            total = total + ref[at, :].astype(jnp.float32)
        out[...] = total.astype(out.dtype)


def merge_work(plan, parts):
    vmem = pl.BlockSpec(memory_space=pltpu.VMEM)
    rows = jax.ShapeDtypeStruct((plan.planes * plan.back, LANES), jnp.bfloat16)
    return pl.pallas_call(
        functools.partial(merge_kernel, plan),
        compiler_params=pltpu.CompilerParams(vmem_limit_bytes=6 * 1024 * 1024),
        out_shape=(rows,) * GROUP,
        in_specs=[vmem] * plan.dp,
        out_specs=(vmem,) * GROUP,
    )(*parts)


def target_kernel(plan, info, route_ref, out_ref):
    tokens, top = plan.tokens, plan.top
    count = tokens * top
    lane = lax.broadcasted_iota(jnp.int32, (tokens, LANES), 1)
    routes = route_ref[...]
    named = jnp.zeros((tokens, LANES), jnp.float32)
    listed = jnp.zeros((tokens, LANES), jnp.float32)
    for k in range(top):
        column = routes[:, k : k + 1]
        named = named + (column == lane).astype(jnp.float32)
        listed = listed + jnp.where(lane == k, column, 0).astype(jnp.float32)
    earlier = (
        lax.broadcasted_iota(jnp.int32, (tokens, tokens), 1)
        < lax.broadcasted_iota(jnp.int32, (tokens, tokens), 0)
    ).astype(jnp.bfloat16)
    places = jnp.dot(earlier, named.astype(jnp.bfloat16), preferred_element_type=jnp.float32)
    pair = lax.broadcasted_iota(jnp.int32, (count, LANES), 0)
    lane = lax.broadcasted_iota(jnp.int32, (count, LANES), 1)
    spread = (pair // top == lane).astype(jnp.bfloat16)
    route = jnp.dot(spread, listed.astype(jnp.bfloat16), preferred_element_type=jnp.float32)
    route = jnp.sum(jnp.where(lane == pair % top, route, 0.0), axis=1, keepdims=True)
    route = route.astype(jnp.int32)
    place = jnp.dot(spread, places.astype(jnp.bfloat16), preferred_element_type=jnp.float32)
    place = jnp.sum(jnp.where(lane == route, place, 0.0), axis=1, keepdims=True).astype(jnp.int32)
    slot = jnp.zeros_like(route)
    for j in range(plan.planes):
        slot = jnp.where(route // GROUP == info[plan.planes_at + j], j, slot)
    row = (route % GROUP) // 2 - info[plan.planes_at + plan.planes]
    row = jnp.where(row < 0, row + plan.rows, row)
    side = jnp.where(route % 2 == info[plan.planes_at + plan.planes + 1], 0, 1)
    base = ((side * plan.rows + row) * plan.planes + slot) * plan.back
    target = base + place
    gate_line = base + plan.cap
    out_ref[...] = jnp.where(lane == 0, target, jnp.where(lane == 1, gate_line, place))


def target_work(plan, info, route_ids):
    vmem = pl.BlockSpec(memory_space=pltpu.VMEM)
    return pl.pallas_call(
        functools.partial(target_kernel, plan),
        out_shape=jax.ShapeDtypeStruct((plan.tokens * plan.top, LANES), jnp.int32),
        in_specs=[pl.BlockSpec(memory_space=pltpu.SMEM), vmem],
        out_specs=vmem,
        compiler_params=pltpu.CompilerParams(vmem_limit_bytes=8 * 1024 * 1024),
    )(info, route_ids)


def final_kernel(plan, target_ref, *refs):
    head_ref, out_gate_ref = refs[GROUP:]
    length = plan.rows * plan.planes * plan.back
    table = jnp.concatenate([ref[...] for ref in refs[:GROUP]], axis=0)
    block = 256
    for start in range(0, plan.tokens * plan.top, block):
        at = pl.ds(start, block)
        slot_of = lax.broadcasted_iota(jnp.int32, (block, 2 * length), 1)
        hot = (slot_of == target_ref[at, 0:1]).astype(jnp.bfloat16)
        head_ref[at, :] = jnp.dot(hot, table, preferred_element_type=jnp.float32).astype(jnp.bfloat16)
        hot = (slot_of == target_ref[at, 1:2]).astype(jnp.bfloat16)
        lines = jnp.dot(hot, table, preferred_element_type=jnp.float32)
        lane_of = lax.broadcasted_iota(jnp.int32, (block, LANES), 1)
        out_gate_ref[at, :] = jnp.sum(
            jnp.where(lane_of == target_ref[at, 2:3], lines, 0.0), axis=1, keepdims=True
        )


def final_work(plan, target, tables):
    count = plan.tokens * plan.top
    vmem = pl.BlockSpec(memory_space=pltpu.VMEM)
    return pl.pallas_call(
        functools.partial(final_kernel, plan),
        cost_estimate=pl.CostEstimate(flops=1, bytes_accessed=1, transcendentals=0),
        out_shape=(
            jax.ShapeDtypeStruct((count, plan.head_dim), jnp.bfloat16),
            jax.ShapeDtypeStruct((count, 1), jnp.float32),
        ),
        in_specs=[vmem] * (1 + GROUP),
        out_specs=(vmem, vmem),
        compiler_params=pltpu.CompilerParams(vmem_limit_bytes=8 * 1024 * 1024),
    )(target, *tables)


def local(mesh, head_outputs, out_grad, gate_weights, route_ids, out_proj):
    tokens, top, head_dim = head_outputs.shape
    features = out_grad.shape[1]
    plan = Plan(mesh, tokens, top, head_dim, features)
    x = lax.axis_index("dp")
    me = lax.axis_index("expert")
    z, y, c = me // GROUP, (me % GROUP) // 2, me % 2

    if plan.planes == 4:
        inner = (z == 1) | (z == 2)
        mates, middle = [(0, 1), (1, 0), (2, 3), (3, 2)], [(1, 2), (2, 1)]
        outward, inward = [(1, 0), (2, 3)], [(0, 1), (3, 2)]
        across = [(1, 3), (2, 0)]
        plane_of = [jnp.where(z < 2, 2, 1), jnp.where(z < 2, 3, 0), z ^ 1, z]
        which = jnp.where(inner, 0, 1)
    else:
        steps = [k % plan.planes for k in range(1, plan.planes + 1)]
        plane_of = [(z + k) % plan.planes for k in steps]
        which = 0
    info = plan.info(x, z, y, c, plane_of, which)

    own_weights = lax.dynamic_slice_in_dim(out_proj[0], x * plan.part, plan.part, 1)
    target = target_work(plan, info, route_ids)
    if plan.planes == 4:
        mate = plan.along(own_weights, mates)
        near_in = plan.along(own_weights, middle)
        mate, near_in, target = lax.optimization_barrier((mate, near_in, target))
        near_out = plan.along(near_in, outward)
        far_in, near_out = lax.optimization_barrier((plan.along(mate, middle), near_out))
        far_out = plan.along(far_in, outward)
    else:
        weights = [[(plan.shift(own_weights, dz=-k % plan.planes), None)] for k in steps]

    meta = jnp.concatenate(
        [
            gate_weights.T,
            route_ids.T.astype(jnp.bfloat16),
            jnp.zeros((LANES - 2 * top, tokens), jnp.bfloat16),
        ],
        axis=0,
    )
    flat_heads = head_outputs.reshape(tokens, top * head_dim)
    packs = []
    for dx, dy in plan.chips():
        piece = lax.dynamic_slice_in_dim(out_grad, ((x + dx) % plan.dp) * plan.part, plan.part, 1)
        value = jnp.concatenate([piece, flat_heads, meta], axis=1)
        value = plan.shift(value, dx=dx, dy=dy)
        if plan.planes == 4:
            if dx or dy:
                value, far_in, near_out = lax.optimization_barrier((value, far_in, near_out))
            else:
                value, near_out = lax.optimization_barrier((value, near_out))
        packs += [value, plan.shift(value, dc=1)]

    if plan.planes == 4:
        weights = [
            [(near_in, 0), (near_out, 1)],
            [(far_in, 0), (far_out, 1)],
            [(mate, None)],
            [(own_weights, None)],
        ]

    sums, backs, done = [], [], target
    for j in range(plan.planes):
        last = j == plan.planes - 1
        if last and plan.planes == 4:
            near_sum = sums[0] + plan.along(sums[0], inward)
            done = (done, near_sum)
        info, done = lax.optimization_barrier((info, done))
        target = target if j else done
        kind = jnp.float32 if last else jnp.bfloat16
        part, *back = slot_work(plan, j, info, packs, weights[j], kind, backs if last else ())
        sums.append(part)
        backs = back if last else backs + back
        done = back[0]

    far_pieces = []
    if plan.planes == 4:
        far_part = plan.along(sums[1], inward)
        far_part, done = lax.optimization_barrier((far_part, done))
        far_sums = sum_work(plan, info, [sums[1], far_part], jnp.bfloat16)
        info, far_sums = lax.optimization_barrier((info, far_sums))
        far_pieces = [plan.along(piece, across, dx) for dx, piece in enumerate(far_sums)]
        received = [plan.along(sums[2], mates), plan.along(near_sum, middle)]
    else:
        received = [plan.shift(sums[j], dz=steps[j]) for j in range(plan.planes - 1)]
    pieces = sum_work(plan, info, [sums[-1]] + received, jnp.float32)
    pieces = [plan.shift(piece, dx=dx) for dx, piece in enumerate(pieces)]

    backs = [plan.shift(rows, dx=-dx % plan.dp) for dx, rows in enumerate(backs)]
    if plan.planes == 4:
        backs, far_sums = lax.optimization_barrier((backs, far_sums))
    merged = merge_work(plan, backs)
    tables = [
        plan.shift(merged[2 * dy + dc], dy=-dy % plan.rows)
        for dy in range(plan.rows)
        for dc in range(2)
    ]
    tables = tables[0::2] + [plan.shift(rows, dc=1) for rows in tables[1::2]]
    tables, far_pieces, pieces = lax.optimization_barrier((tables, far_pieces, pieces))
    grad_head, grad_gate = final_work(plan, target, tables)
    grad_proj = layout_work(plan, info, pieces + far_pieces)
    return (
        grad_head.reshape(tokens, top, head_dim),
        grad_gate.reshape(tokens, top).astype(jnp.bfloat16),
        grad_proj[None],
    )


def solution(mesh):
    return jax.shard_map(
        functools.partial(local, mesh),
        mesh=mesh,
        in_specs=(
            P(("dp", "expert"), None, None),
            P(("dp", "expert"), None),
            P(("dp", "expert"), None),
            P(("dp", "expert"), None),
            P("expert", None, None),
        ),
        out_specs=(
            P(("dp", "expert"), None, None),
            P(("dp", "expert"), None),
            P("expert", "dp", None),
        ),
        check_vma=False,
    )
```

```python
import functools

import jax
import jax.numpy as jnp
from jax import lax
from jax.experimental import pallas as pl
from jax.experimental.pallas import tpu as pltpu
from jax.sharding import PartitionSpec as P

soft_cap = 1.5
AXES = ("dp", "expert")
GROUP = 4
LANES = 128


class Plan:
    def __init__(self, mesh, tokens, top, head_dim, features):
        self.dp = mesh.shape["dp"]
        self.experts = mesh.shape["expert"]
        self.rows = GROUP // 2
        self.planes = self.experts // GROUP
        self.sources = self.dp * GROUP
        self.tokens, self.top, self.head_dim = tokens, top, head_dim
        self.part = features // self.dp
        self.own_rows = head_dim // self.dp
        cap = 9 * tokens * top // (8 * self.experts)
        self.cap = -(-cap // 8) * 8
        self.back = self.cap + 8
        self.width = self.part + top * head_dim + LANES

    def index(self, x, z, y, c):
        return x * self.experts + z * GROUP + y * 2 + c

    def pairs(self, dx=0, dz=0, dy=0, dc=0):
        out = []
        for x in range(self.dp):
            for z in range(self.planes):
                for y in range(self.rows):
                    for c in range(2):
                        target = self.index(
                            (x + dx) % self.dp,
                            (z + dz) % self.planes,
                            (y + dy) % self.rows,
                            c ^ dc,
                        )
                        out.append((self.index(x, z, y, c), target))
        return out

    def shift(self, value, **by):
        if not any(by.values()):
            return value
        return lax.ppermute(value, AXES, self.pairs(**by))

    def along(self, value, moves, dx=0, dy=0):
        out = []
        for x in range(self.dp):
            for a, b in moves:
                for y in range(self.rows):
                    for c in range(2):
                        target = self.index((x + dx) % self.dp, b, (y + dy) % self.rows, c)
                        out.append((self.index(x, a, y, c), target))
        return lax.ppermute(value, AXES, out)

    def info(self, x, z, y, c, plane_of, which):
        values = [((x + dx) % self.dp) * self.own_rows for dx in range(self.dp)]
        self.lanes_at = len(values)
        values += [((x - dx) % self.dp) * self.part for dx in range(self.dp)]
        self.which_at = len(values)
        values += [which]
        self.experts_at = len(values)
        values += [plane_of[j] * GROUP + y * 2 + c for j in range(self.planes)]
        self.planes_at = len(values)
        values += list(plane_of) + [y, c]
        return jnp.stack([jnp.asarray(value, jnp.int32) for value in values])

    def chips(self):
        return [(dx, dy) for dx in range(self.dp) for dy in range(self.rows)]


def slot_kernel(plan, index, first, where, earlier, added, info, *refs):
    count = plan.sources - 2 if first == 0 else 2
    packs, rest = refs[:count], refs[count:]
    weight_refs, rest = rest[: len(where)], rest[len(where) :]
    added_refs, rest = rest[:added], rest[added:]
    earlier_refs, rest = rest[: len(earlier)], rest[len(earlier) :]
    outs = plan.dp if earlier else 1
    p_ref, back_refs, (grads, heads, weights) = rest[0], rest[1 : 1 + outs], rest[1 + outs :]
    tokens, cap, part, top, head_dim = plan.tokens, plan.cap, plan.part, plan.top, plan.head_dim
    pair_rows = 2 * cap
    pair_total = count // 2
    length = plan.planes * plan.back

    def put(s, slot, at, value):
        if earlier:
            start = (s % GROUP) * length + slot * plan.back + at
            back_refs[s // GROUP][pl.ds(start, value.shape[0]), :] = value
        else:
            back_refs[0][s - first, pl.ds(at, value.shape[0]), :] = value

    if len(where) > 1:
        for ref, kind in zip(weight_refs, where):

            @pl.when(info[plan.which_at] == kind)
            def _():
                weights[...] = ref[...]

        weight_ref = weights
    else:
        weight_ref = weight_refs[0]
    expert = info[plan.experts_at + index].astype(jnp.float32)
    row_of = lax.broadcasted_iota(jnp.int32, (cap, tokens), 0)
    diagonal = (row_of == lax.broadcasted_iota(jnp.int32, (cap, tokens), 1)).astype(jnp.float32)
    before = (
        lax.broadcasted_iota(jnp.int32, (tokens, tokens), 0)
        < lax.broadcasted_iota(jnp.int32, (tokens, tokens), 1)
    ).astype(jnp.bfloat16)
    block_row = lax.broadcasted_iota(jnp.int32, (8, LANES), 0)
    empty = jnp.zeros((cap, tokens), jnp.bfloat16)
    chunk = min(part, 512)

    masks, occupied, gate_rows = [], [], []
    for s in range(count):
        meta = packs[s][pl.ds(0, 2 * top), pl.ds(part + top * head_dim, LANES)].astype(jnp.float32)
        mask = (meta[top:] == expert).astype(jnp.float32)
        masks.append(mask)
        occupied.append(jnp.sum(mask, axis=0, keepdims=True))
        gate_rows.append(jnp.sum(mask * meta[:top], axis=0, keepdims=True))
    filled = occupied + [jnp.zeros((1, tokens), jnp.float32)] * (-count % 16)
    places = jnp.dot(
        jnp.concatenate(filled, axis=0).astype(jnp.bfloat16),
        before,
        preferred_element_type=jnp.float32,
    ).astype(jnp.int32)
    for q in range(pair_total):
        hots, gates = [], []
        for b in range(2):
            s = 2 * q + b
            hot = jnp.where(row_of == places[s : s + 1], occupied[s], 0.0)
            gates.append(jnp.sum(hot * gate_rows[s], axis=1, keepdims=True))
            hots.append(hot.astype(jnp.bfloat16))
            wide = jnp.concatenate(
                [(hot * masks[s][k : k + 1]).astype(jnp.bfloat16) for k in range(top)], axis=1
            )
            raw = jnp.concatenate(
                [packs[s][:, pl.ds(part + k * head_dim, head_dim)] for k in range(top)], axis=0
            )
            heads[pl.ds(s * cap, cap), :] = jnp.dot(
                wide, raw, preferred_element_type=jnp.float32
            ).astype(jnp.bfloat16)
        all_hots = jnp.concatenate(
            [
                jnp.concatenate([hots[0], empty], axis=1),
                jnp.concatenate([empty, hots[1]], axis=1),
            ],
            axis=0,
        )
        gate = jnp.broadcast_to(jnp.concatenate(gates, axis=0), (pair_rows, LANES))
        total = jnp.zeros((pair_rows, LANES), jnp.float32)
        rows_at = pl.ds(q * pair_rows, pair_rows)
        for start in range(0, part, chunk):
            both = jnp.concatenate(
                [packs[2 * q + b][:, pl.ds(start, chunk)] for b in range(2)], axis=0
            )
            grad = jnp.dot(all_hots, both, preferred_element_type=jnp.float32)
            pre = jnp.dot(
                heads[rows_at, :], weight_ref[:, pl.ds(start, chunk)], preferred_element_type=jnp.float32
            )
            for lane in range(0, chunk, LANES):
                grad_block = grad[:, lane : lane + LANES]
                capped = jnp.tanh(pre[:, lane : lane + LANES] * (1.0 / soft_cap))
                total = total + grad_block * capped
                grads[rows_at, pl.ds(start + lane, LANES)] = (
                    gate * grad_block * (1.0 - capped * capped)
                ).astype(jnp.bfloat16)
        for b in range(2):
            column = jnp.sum(total[b * cap : (b + 1) * cap], axis=1, keepdims=True) * soft_cap
            line = jnp.sum(diagonal * column, axis=0, keepdims=True)
            block = jnp.where(block_row == 0, line, 0.0).astype(jnp.bfloat16)
            put(first + 2 * q + b, index, cap, block)
    grad_all = grads[...]
    total = lax.dot_general(
        heads[...], grad_all, (((0,), (0,)), ((), ())), preferred_element_type=jnp.float32
    )
    for ref in added_refs:
        total = total + ref[...]
    p_ref[...] = total.astype(p_ref.dtype)
    rows = lax.dot_general(
        grad_all, weight_ref[...], (((1,), (1,)), ((), ())), preferred_element_type=jnp.float32
    ).astype(jnp.bfloat16)
    for s in range(count):
        put(first + s, index, 0, rows[s * cap : (s + 1) * cap])
    for ref, (slot, start) in zip(earlier_refs, earlier):
        for s in range(ref.shape[0]):
            put(start + s, slot, 0, ref[s])


def slot_work(plan, index, first, info, packs, weights, kind, added=(), earlier=()):
    rows = len(packs) * plan.cap
    if earlier:
        backs = (
            jax.ShapeDtypeStruct((GROUP * plan.planes * plan.back, LANES), jnp.bfloat16),
        ) * plan.dp
    else:
        backs = (jax.ShapeDtypeStruct((len(packs), plan.back, LANES), jnp.bfloat16),)
    vmem = pl.BlockSpec(memory_space=pltpu.VMEM)
    body = functools.partial(
        slot_kernel,
        plan,
        index,
        first,
        [where for _, where in weights],
        [(slot, start) for slot, start, _ in earlier],
        len(added),
    )
    operands = [*packs, *[array for array, _ in weights], *added, *[rows for _, _, rows in earlier]]
    return pl.pallas_call(
        body,
        out_shape=(jax.ShapeDtypeStruct((plan.head_dim, plan.part), kind), *backs),
        in_specs=[pl.BlockSpec(memory_space=pltpu.SMEM)] + [vmem] * len(operands),
        out_specs=(vmem,) * (1 + len(backs)),
        scratch_shapes=[
            pltpu.VMEM((rows, plan.part), jnp.bfloat16),
            pltpu.VMEM((rows, plan.head_dim), jnp.bfloat16),
            pltpu.VMEM((plan.head_dim, plan.part), jnp.bfloat16),
        ],
        compiler_params=pltpu.CompilerParams(vmem_limit_bytes=14 * 1024 * 1024),
    )(info, *operands)


def sum_kernel(plan, info, *refs):
    parts, pieces = refs[: len(refs) - plan.dp], refs[len(refs) - plan.dp :]
    rows = plan.own_rows
    for j, piece in enumerate(pieces):
        at = pl.ds(pl.multiple_of(info[j], rows), rows)
        total = parts[0][at, :].astype(jnp.float32)
        for ref in parts[1:]:
            total = total + ref[at, :].astype(jnp.float32)
        piece[...] = total.astype(piece.dtype)


def sum_work(plan, info, parts, own_kind):
    rows = plan.head_dim // plan.dp
    vmem = pl.BlockSpec(memory_space=pltpu.VMEM)
    return pl.pallas_call(
        functools.partial(sum_kernel, plan),
        compiler_params=pltpu.CompilerParams(vmem_limit_bytes=6 * 1024 * 1024),
        out_shape=tuple(
            jax.ShapeDtypeStruct((rows, plan.part), jnp.bfloat16 if j else own_kind)
            for j in range(plan.dp)
        ),
        in_specs=[pl.BlockSpec(memory_space=pltpu.SMEM)] + [vmem] * len(parts),
        out_specs=(vmem,) * plan.dp,
    )(info, *parts)


def layout_kernel(plan, info, *refs):
    out_ref = refs[-1]
    for j in range(plan.dp):
        at = pl.ds(pl.multiple_of(info[plan.lanes_at + j], plan.part), plan.part)
        total = None
        for ref in refs[j : -1 : plan.dp]:
            piece = ref[...].astype(jnp.float32)
            total = piece if total is None else total + piece
        out_ref[:, at] = total


def layout_work(plan, info, pieces):
    rows = plan.head_dim // plan.dp
    vmem = pl.BlockSpec(memory_space=pltpu.VMEM)
    return pl.pallas_call(
        functools.partial(layout_kernel, plan),
        compiler_params=pltpu.CompilerParams(vmem_limit_bytes=6 * 1024 * 1024),
        out_shape=jax.ShapeDtypeStruct((rows, plan.part * plan.dp), jnp.float32),
        in_specs=[pl.BlockSpec(memory_space=pltpu.SMEM)] + [vmem] * len(pieces),
        out_specs=vmem,
    )(info, *pieces)


def merge_kernel(plan, *refs):
    parts, outs = refs[: plan.dp], refs[plan.dp :]
    length = plan.planes * plan.back
    for j, out in enumerate(outs):
        at = pl.ds(j * length, length)
        total = parts[0][at, :].astype(jnp.float32)
        for ref in parts[1:]:
            total = total + ref[at, :].astype(jnp.float32)
        out[...] = total.astype(out.dtype)


def merge_work(plan, parts):
    vmem = pl.BlockSpec(memory_space=pltpu.VMEM)
    rows = jax.ShapeDtypeStruct((plan.planes * plan.back, LANES), jnp.bfloat16)
    return pl.pallas_call(
        functools.partial(merge_kernel, plan),
        compiler_params=pltpu.CompilerParams(vmem_limit_bytes=6 * 1024 * 1024),
        out_shape=(rows,) * GROUP,
        in_specs=[vmem] * plan.dp,
        out_specs=(vmem,) * GROUP,
    )(*parts)


def target_kernel(plan, info, route_ref, out_ref):
    tokens, top = plan.tokens, plan.top
    count = tokens * top
    lane = lax.broadcasted_iota(jnp.int32, (tokens, LANES), 1)
    routes = route_ref[...]
    named = jnp.zeros((tokens, LANES), jnp.float32)
    listed = jnp.zeros((tokens, LANES), jnp.float32)
    for k in range(top):
        column = routes[:, k : k + 1]
        named = named + (column == lane).astype(jnp.float32)
        listed = listed + jnp.where(lane == k, column, 0).astype(jnp.float32)
    earlier = (
        lax.broadcasted_iota(jnp.int32, (tokens, tokens), 1)
        < lax.broadcasted_iota(jnp.int32, (tokens, tokens), 0)
    ).astype(jnp.bfloat16)
    places = jnp.dot(earlier, named.astype(jnp.bfloat16), preferred_element_type=jnp.float32)
    pair = lax.broadcasted_iota(jnp.int32, (count, LANES), 0)
    lane = lax.broadcasted_iota(jnp.int32, (count, LANES), 1)
    spread = (pair // top == lane).astype(jnp.bfloat16)
    route = jnp.dot(spread, listed.astype(jnp.bfloat16), preferred_element_type=jnp.float32)
    route = jnp.sum(jnp.where(lane == pair % top, route, 0.0), axis=1, keepdims=True)
    route = route.astype(jnp.int32)
    place = jnp.dot(spread, places.astype(jnp.bfloat16), preferred_element_type=jnp.float32)
    place = jnp.sum(jnp.where(lane == route, place, 0.0), axis=1, keepdims=True).astype(jnp.int32)
    slot = jnp.zeros_like(route)
    for j in range(plan.planes):
        slot = jnp.where(route // GROUP == info[plan.planes_at + j], j, slot)
    row = (route % GROUP) // 2 - info[plan.planes_at + plan.planes]
    row = jnp.where(row < 0, row + plan.rows, row)
    side = jnp.where(route % 2 == info[plan.planes_at + plan.planes + 1], 0, 1)
    base = ((side * plan.rows + row) * plan.planes + slot) * plan.back
    target = base + place
    gate_line = base + plan.cap
    out_ref[...] = jnp.where(lane == 0, target, jnp.where(lane == 1, gate_line, place))


def target_work(plan, info, route_ids):
    vmem = pl.BlockSpec(memory_space=pltpu.VMEM)
    return pl.pallas_call(
        functools.partial(target_kernel, plan),
        out_shape=jax.ShapeDtypeStruct((plan.tokens * plan.top, LANES), jnp.int32),
        in_specs=[pl.BlockSpec(memory_space=pltpu.SMEM), vmem],
        out_specs=vmem,
        compiler_params=pltpu.CompilerParams(vmem_limit_bytes=8 * 1024 * 1024),
    )(info, route_ids)


def final_kernel(plan, target_ref, *refs):
    head_ref, out_gate_ref = refs[GROUP:]
    length = plan.rows * plan.planes * plan.back
    table = jnp.concatenate([ref[...] for ref in refs[:GROUP]], axis=0)
    block = 256
    for start in range(0, plan.tokens * plan.top, block):
        at = pl.ds(start, block)
        slot_of = lax.broadcasted_iota(jnp.int32, (block, 2 * length), 1)
        hot = (slot_of == target_ref[at, 0:1]).astype(jnp.bfloat16)
        head_ref[at, :] = jnp.dot(hot, table, preferred_element_type=jnp.float32).astype(jnp.bfloat16)
        hot = (slot_of == target_ref[at, 1:2]).astype(jnp.bfloat16)
        lines = jnp.dot(hot, table, preferred_element_type=jnp.float32)
        lane_of = lax.broadcasted_iota(jnp.int32, (block, LANES), 1)
        out_gate_ref[at, :] = jnp.sum(
            jnp.where(lane_of == target_ref[at, 2:3], lines, 0.0), axis=1, keepdims=True
        )


def final_work(plan, target, tables):
    count = plan.tokens * plan.top
    vmem = pl.BlockSpec(memory_space=pltpu.VMEM)
    return pl.pallas_call(
        functools.partial(final_kernel, plan),
        cost_estimate=pl.CostEstimate(flops=1, bytes_accessed=1, transcendentals=0),
        out_shape=(
            jax.ShapeDtypeStruct((count, plan.head_dim), jnp.bfloat16),
            jax.ShapeDtypeStruct((count, 1), jnp.float32),
        ),
        in_specs=[vmem] * (1 + GROUP),
        out_specs=(vmem, vmem),
        compiler_params=pltpu.CompilerParams(vmem_limit_bytes=8 * 1024 * 1024),
    )(target, *tables)


def local(mesh, head_outputs, out_grad, gate_weights, route_ids, out_proj):
    tokens, top, head_dim = head_outputs.shape
    features = out_grad.shape[1]
    plan = Plan(mesh, tokens, top, head_dim, features)
    x = lax.axis_index("dp")
    me = lax.axis_index("expert")
    z, y, c = me // GROUP, (me % GROUP) // 2, me % 2

    if plan.planes == 4:
        inner = (z == 1) | (z == 2)
        mates, middle = [(0, 1), (1, 0), (2, 3), (3, 2)], [(1, 2), (2, 1)]
        outward, inward = [(1, 0), (2, 3)], [(0, 1), (3, 2)]
        across = [(1, 3), (2, 0)]
        plane_of = [jnp.where(z < 2, 2, 1), jnp.where(z < 2, 3, 0), z ^ 1, z]
        which = jnp.where(inner, 0, 1)
    else:
        steps = [k % plan.planes for k in range(1, plan.planes + 1)]
        plane_of = [(z + k) % plan.planes for k in steps]
        which = 0
    info = plan.info(x, z, y, c, plane_of, which)

    own_weights = lax.dynamic_slice_in_dim(out_proj[0], x * plan.part, plan.part, 1)
    target = target_work(plan, info, route_ids)
    if plan.planes == 4:
        mate = plan.along(own_weights, mates)
        near_in = plan.along(own_weights, middle)
        mate, near_in, target = lax.optimization_barrier((mate, near_in, target))
        near_out = plan.along(near_in, outward)
        far_in, near_out = lax.optimization_barrier((plan.along(mate, middle), near_out))
        far_out = plan.along(far_in, outward)
    else:
        weights = [[(plan.shift(own_weights, dz=-k % plan.planes), None)] for k in steps]

    meta = jnp.concatenate(
        [
            gate_weights.T,
            route_ids.T.astype(jnp.bfloat16),
            jnp.zeros((LANES - 2 * top, tokens), jnp.bfloat16),
        ],
        axis=0,
    )
    flat_heads = head_outputs.reshape(tokens, top * head_dim)
    packs, held = [], []
    for dx, dy in plan.chips():
        piece = lax.dynamic_slice_in_dim(out_grad, ((x + dx) % plan.dp) * plan.part, plan.part, 1)
        value = jnp.concatenate([piece, flat_heads, meta], axis=1)
        if plan.planes == 4 and not (dx or dy):
            value, near_in, mate = lax.optimization_barrier((value, near_in, mate))
        if plan.planes == 4 and dx and dy:
            value, far_in, near_out = lax.optimization_barrier((value, far_in, near_out))
        value = plan.shift(value, dx=dx, dy=dy)
        if len(packs) < plan.dp * plan.rows - 1:
            held += [value, plan.shift(value, dc=1)]
        packs.append(value)

    if plan.planes == 4:
        weights = [
            [(near_in, 0), (near_out, 1)],
            [(far_in, 0), (far_out, 1)],
            [(mate, None)],
            [(own_weights, None)],
        ]

    last = plan.planes - 1
    calls = [(j, 0) for j in [last, *range(last)]] + [(j, 1) for j in range(plan.planes)]
    if plan.planes == 4:
        calls = [(3, 0), (2, 0), (0, 0), (0, 1), (1, 0), (1, 1), (2, 1), (3, 1)]
    sums, backs, done, far = {}, [], target, None
    for j, late in calls:
        final = (j, late) == (last, 1)
        if late and far is None:
            value, info, done = lax.optimization_barrier((packs[-1], info, done))
            if plan.planes == 4:
                value, far_out = lax.optimization_barrier((value, far_out))
            far = [value, plan.shift(value, dc=1)]
        if final and plan.planes == 4:
            near_sum = sums[0] + plan.along(sums[0], inward)
            done = (done, near_sum)
        info, done = lax.optimization_barrier((info, done))
        sums[j], *back = slot_work(
            plan,
            j,
            plan.sources - 2 if late else 0,
            info,
            far if late else held,
            weights[j],
            jnp.bfloat16 if late and not final else jnp.float32,
            [sums[j]] if late else [],
            backs if final else [],
        )
        backs = back if final else backs + [(j, plan.sources - 2 if late else 0, back[0])]
        done = back[0]

    far_pieces = []
    if plan.planes == 4:
        far_part = plan.along(sums[1], inward)
        far_part, done = lax.optimization_barrier((far_part, done))
        far_sums = sum_work(plan, info, [sums[1], far_part], jnp.bfloat16)
        info, far_sums = lax.optimization_barrier((info, far_sums))
        far_pieces = [plan.along(piece, across, dx) for dx, piece in enumerate(far_sums)]
        received = [plan.along(sums[2], mates), plan.along(near_sum, middle)]
    else:
        received = [plan.shift(sums[j], dz=steps[j]) for j in range(plan.planes - 1)]
    pieces = sum_work(plan, info, [sums[last]] + received, jnp.float32)
    pieces = [plan.shift(piece, dx=dx) for dx, piece in enumerate(pieces)]

    backs = [plan.shift(rows, dx=-dx % plan.dp) for dx, rows in enumerate(backs)]
    if plan.planes == 4:
        backs, far_sums = lax.optimization_barrier((backs, far_sums))
    merged = merge_work(plan, backs)
    tables = [
        plan.shift(merged[2 * dy + dc], dy=-dy % plan.rows)
        for dy in range(plan.rows)
        for dc in range(2)
    ]
    tables = tables[0::2] + [plan.shift(rows, dc=1) for rows in tables[1::2]]
    tables, far_pieces, pieces = lax.optimization_barrier((tables, far_pieces, pieces))
    grad_head, grad_gate = final_work(plan, target, tables)
    grad_proj = layout_work(plan, info, pieces + far_pieces)
    return (
        grad_head.reshape(tokens, top, head_dim),
        grad_gate.reshape(tokens, top).astype(jnp.bfloat16),
        grad_proj[None],
    )


def solution(mesh):
    return jax.shard_map(
        functools.partial(local, mesh),
        mesh=mesh,
        in_specs=(
            P(("dp", "expert"), None, None),
            P(("dp", "expert"), None),
            P(("dp", "expert"), None),
            P(("dp", "expert"), None),
            P("expert", None, None),
        ),
        out_specs=(
            P(("dp", "expert"), None, None),
            P(("dp", "expert"), None),
            P("expert", "dp", None),
        ),
        check_vma=False,
    )
```

```python
import functools

import jax
import jax.numpy as jnp
from jax import lax
from jax.experimental import pallas as pl
from jax.experimental.pallas import tpu as pltpu
from jax.sharding import PartitionSpec as P

soft_cap = 1.5
AXES = ("dp", "expert")
GROUP = 4
LANES = 128


class Plan:
    def __init__(self, mesh, tokens, top, head_dim, features):
        self.dp = mesh.shape["dp"]
        self.experts = mesh.shape["expert"]
        self.rows = GROUP // 2
        self.planes = self.experts // GROUP
        self.sources = self.dp * GROUP
        self.tokens, self.top, self.head_dim = tokens, top, head_dim
        self.part = features // self.dp
        self.own_rows = head_dim // self.dp
        cap = 9 * tokens * top // (8 * self.experts)
        self.cap = -(-cap // 8) * 8
        self.back = self.cap + 8
        self.width = self.part + top * head_dim + LANES

    def index(self, x, z, y, c):
        return x * self.experts + z * GROUP + y * 2 + c

    def pairs(self, dx=0, dz=0, dy=0, dc=0):
        out = []
        for x in range(self.dp):
            for z in range(self.planes):
                for y in range(self.rows):
                    for c in range(2):
                        target = self.index(
                            (x + dx) % self.dp,
                            (z + dz) % self.planes,
                            (y + dy) % self.rows,
                            c ^ dc,
                        )
                        out.append((self.index(x, z, y, c), target))
        return out

    def shift(self, value, **by):
        if not any(by.values()):
            return value
        return lax.ppermute(value, AXES, self.pairs(**by))

    def along(self, value, moves, dx=0, dy=0):
        out = []
        for x in range(self.dp):
            for a, b in moves:
                for y in range(self.rows):
                    for c in range(2):
                        target = self.index((x + dx) % self.dp, b, (y + dy) % self.rows, c)
                        out.append((self.index(x, a, y, c), target))
        return lax.ppermute(value, AXES, out)

    def info(self, x, z, y, c, plane_of, which):
        values = [((x + dx) % self.dp) * self.own_rows for dx in range(self.dp)]
        self.lanes_at = len(values)
        values += [((x - dx) % self.dp) * self.part for dx in range(self.dp)]
        self.which_at = len(values)
        values += [which]
        self.experts_at = len(values)
        values += [plane_of[j] * GROUP + y * 2 + c for j in range(self.planes)]
        self.planes_at = len(values)
        values += list(plane_of) + [y, c]
        return jnp.stack([jnp.asarray(value, jnp.int32) for value in values])

    def chips(self):
        return [(dx, dy) for dx in range(self.dp) for dy in range(self.rows)]


def slot_kernel(plan, index, first, where, earlier, added, info, *refs):
    count = plan.sources - 2 if first == 0 else 2
    packs, rest = refs[:count], refs[count:]
    weight_refs, rest = rest[: len(where)], rest[len(where) :]
    added_refs, rest = rest[:added], rest[added:]
    earlier_refs, rest = rest[: len(earlier)], rest[len(earlier) :]
    outs = plan.dp if earlier else 1
    p_ref, back_refs, (grads, heads, weights) = rest[0], rest[1 : 1 + outs], rest[1 + outs :]
    tokens, cap, part, top, head_dim = plan.tokens, plan.cap, plan.part, plan.top, plan.head_dim
    pair_rows = 2 * cap
    pair_total = count // 2
    length = plan.planes * plan.back

    def put(s, slot, at, value):
        if earlier:
            start = (s % GROUP) * length + slot * plan.back + at
            back_refs[s // GROUP][pl.ds(start, value.shape[0]), :] = value
        else:
            back_refs[0][s - first, pl.ds(at, value.shape[0]), :] = value

    if len(where) > 1:
        for ref, kind in zip(weight_refs, where):

            @pl.when(info[plan.which_at] == kind)
            def _():
                weights[...] = ref[...]

        weight_ref = weights
    else:
        weight_ref = weight_refs[0]
    expert = info[plan.experts_at + index].astype(jnp.float32)
    row_of = lax.broadcasted_iota(jnp.int32, (cap, tokens), 0)
    diagonal = (row_of == lax.broadcasted_iota(jnp.int32, (cap, tokens), 1)).astype(jnp.float32)
    before = (
        lax.broadcasted_iota(jnp.int32, (tokens, tokens), 0)
        < lax.broadcasted_iota(jnp.int32, (tokens, tokens), 1)
    ).astype(jnp.bfloat16)
    block_row = lax.broadcasted_iota(jnp.int32, (8, LANES), 0)
    empty = jnp.zeros((cap, tokens), jnp.bfloat16)
    chunk = min(part, 512)

    masks, occupied, gate_rows = [], [], []
    for s in range(count):
        meta = packs[s][pl.ds(0, 2 * top), pl.ds(part + top * head_dim, LANES)].astype(jnp.float32)
        mask = (meta[top:] == expert).astype(jnp.float32)
        masks.append(mask)
        occupied.append(jnp.sum(mask, axis=0, keepdims=True))
        gate_rows.append(jnp.sum(mask * meta[:top], axis=0, keepdims=True))
    filled = occupied + [jnp.zeros((1, tokens), jnp.float32)] * (-count % 16)
    places = jnp.dot(
        jnp.concatenate(filled, axis=0).astype(jnp.bfloat16),
        before,
        preferred_element_type=jnp.float32,
    ).astype(jnp.int32)
    for q in range(pair_total):
        hots, gates = [], []
        for b in range(2):
            s = 2 * q + b
            hot = jnp.where(row_of == places[s : s + 1], occupied[s], 0.0)
            gates.append(jnp.sum(hot * gate_rows[s], axis=1, keepdims=True))
            hots.append(hot.astype(jnp.bfloat16))
            wide = jnp.concatenate(
                [(hot * masks[s][k : k + 1]).astype(jnp.bfloat16) for k in range(top)], axis=1
            )
            raw = jnp.concatenate(
                [packs[s][:, pl.ds(part + k * head_dim, head_dim)] for k in range(top)], axis=0
            )
            heads[pl.ds(s * cap, cap), :] = jnp.dot(
                wide, raw, preferred_element_type=jnp.float32
            ).astype(jnp.bfloat16)
        all_hots = jnp.concatenate(
            [
                jnp.concatenate([hots[0], empty], axis=1),
                jnp.concatenate([empty, hots[1]], axis=1),
            ],
            axis=0,
        )
        gate = jnp.broadcast_to(jnp.concatenate(gates, axis=0), (pair_rows, LANES))
        total = jnp.zeros((pair_rows, LANES), jnp.float32)
        rows_at = pl.ds(q * pair_rows, pair_rows)
        for start in range(0, part, chunk):
            both = jnp.concatenate(
                [packs[2 * q + b][:, pl.ds(start, chunk)] for b in range(2)], axis=0
            )
            grad = jnp.dot(all_hots, both, preferred_element_type=jnp.float32)
            pre = jnp.dot(
                heads[rows_at, :], weight_ref[:, pl.ds(start, chunk)], preferred_element_type=jnp.float32
            )
            for lane in range(0, chunk, LANES):
                grad_block = grad[:, lane : lane + LANES]
                capped = jnp.tanh(pre[:, lane : lane + LANES] * (1.0 / soft_cap))
                total = total + grad_block * capped
                grads[rows_at, pl.ds(start + lane, LANES)] = (
                    gate * grad_block * (1.0 - capped * capped)
                ).astype(jnp.bfloat16)
        for b in range(2):
            column = jnp.sum(total[b * cap : (b + 1) * cap], axis=1, keepdims=True) * soft_cap
            line = jnp.sum(diagonal * column, axis=0, keepdims=True)
            block = jnp.where(block_row == 0, line, 0.0).astype(jnp.bfloat16)
            put(first + 2 * q + b, index, cap, block)
    grad_all = grads[...]
    total = lax.dot_general(
        heads[...], grad_all, (((0,), (0,)), ((), ())), preferred_element_type=jnp.float32
    )
    for ref in added_refs:
        total = total + ref[...]
    p_ref[...] = total.astype(p_ref.dtype)
    rows = lax.dot_general(
        grad_all, weight_ref[...], (((1,), (1,)), ((), ())), preferred_element_type=jnp.float32
    ).astype(jnp.bfloat16)
    for s in range(count):
        put(first + s, index, 0, rows[s * cap : (s + 1) * cap])
    for ref, (slot, start) in zip(earlier_refs, earlier):
        for s in range(ref.shape[0]):
            put(start + s, slot, 0, ref[s])


def slot_work(plan, index, first, info, packs, weights, kind, added=(), earlier=()):
    rows = len(packs) * plan.cap
    if earlier:
        backs = (
            jax.ShapeDtypeStruct((GROUP * plan.planes * plan.back, LANES), jnp.bfloat16),
        ) * plan.dp
    else:
        backs = (jax.ShapeDtypeStruct((len(packs), plan.back, LANES), jnp.bfloat16),)
    vmem = pl.BlockSpec(memory_space=pltpu.VMEM)
    body = functools.partial(
        slot_kernel,
        plan,
        index,
        first,
        [where for _, where in weights],
        [(slot, start) for slot, start, _ in earlier],
        len(added),
    )
    operands = [*packs, *[array for array, _ in weights], *added, *[rows for _, _, rows in earlier]]
    return pl.pallas_call(
        body,
        out_shape=(jax.ShapeDtypeStruct((plan.head_dim, plan.part), kind), *backs),
        in_specs=[pl.BlockSpec(memory_space=pltpu.SMEM)] + [vmem] * len(operands),
        out_specs=(vmem,) * (1 + len(backs)),
        scratch_shapes=[
            pltpu.VMEM((rows, plan.part), jnp.bfloat16),
            pltpu.VMEM((rows, plan.head_dim), jnp.bfloat16),
            pltpu.VMEM((plan.head_dim, plan.part), jnp.bfloat16),
        ],
        compiler_params=pltpu.CompilerParams(vmem_limit_bytes=14 * 1024 * 1024),
    )(info, *operands)


def sum_kernel(plan, info, *refs):
    parts, pieces = refs[: len(refs) - plan.dp], refs[len(refs) - plan.dp :]
    rows = plan.own_rows
    for j, piece in enumerate(pieces):
        at = pl.ds(pl.multiple_of(info[j], rows), rows)
        total = parts[0][at, :].astype(jnp.float32)
        for ref in parts[1:]:
            total = total + ref[at, :].astype(jnp.float32)
        piece[...] = total.astype(piece.dtype)


def sum_work(plan, info, parts, own_kind):
    rows = plan.head_dim // plan.dp
    vmem = pl.BlockSpec(memory_space=pltpu.VMEM)
    return pl.pallas_call(
        functools.partial(sum_kernel, plan),
        compiler_params=pltpu.CompilerParams(vmem_limit_bytes=6 * 1024 * 1024),
        out_shape=tuple(
            jax.ShapeDtypeStruct((rows, plan.part), jnp.bfloat16 if j else own_kind)
            for j in range(plan.dp)
        ),
        in_specs=[pl.BlockSpec(memory_space=pltpu.SMEM)] + [vmem] * len(parts),
        out_specs=(vmem,) * plan.dp,
    )(info, *parts)


def layout_kernel(plan, info, *refs):
    out_ref = refs[-1]
    for j in range(plan.dp):
        at = pl.ds(pl.multiple_of(info[plan.lanes_at + j], plan.part), plan.part)
        total = None
        for ref in refs[j : -1 : plan.dp]:
            piece = ref[...].astype(jnp.float32)
            total = piece if total is None else total + piece
        out_ref[:, at] = total


def layout_work(plan, info, pieces):
    rows = plan.head_dim // plan.dp
    vmem = pl.BlockSpec(memory_space=pltpu.VMEM)
    return pl.pallas_call(
        functools.partial(layout_kernel, plan),
        compiler_params=pltpu.CompilerParams(vmem_limit_bytes=6 * 1024 * 1024),
        out_shape=jax.ShapeDtypeStruct((rows, plan.part * plan.dp), jnp.float32),
        in_specs=[pl.BlockSpec(memory_space=pltpu.SMEM)] + [vmem] * len(pieces),
        out_specs=vmem,
    )(info, *pieces)


def merge_kernel(plan, *refs):
    parts, outs = refs[: plan.dp], refs[plan.dp :]
    length = plan.planes * plan.back
    for j, out in enumerate(outs):
        at = pl.ds(j * length, length)
        total = parts[0][at, :].astype(jnp.float32)
        for ref in parts[1:]:
            total = total + ref[at, :].astype(jnp.float32)
        out[...] = total.astype(out.dtype)


def merge_work(plan, parts):
    vmem = pl.BlockSpec(memory_space=pltpu.VMEM)
    rows = jax.ShapeDtypeStruct((plan.planes * plan.back, LANES), jnp.bfloat16)
    return pl.pallas_call(
        functools.partial(merge_kernel, plan),
        compiler_params=pltpu.CompilerParams(vmem_limit_bytes=6 * 1024 * 1024),
        out_shape=(rows,) * GROUP,
        in_specs=[vmem] * plan.dp,
        out_specs=(vmem,) * GROUP,
    )(*parts)


def target_kernel(plan, info, route_ref, out_ref):
    tokens, top = plan.tokens, plan.top
    count = tokens * top
    lane = lax.broadcasted_iota(jnp.int32, (tokens, LANES), 1)
    routes = route_ref[...]
    named = jnp.zeros((tokens, LANES), jnp.float32)
    listed = jnp.zeros((tokens, LANES), jnp.float32)
    for k in range(top):
        column = routes[:, k : k + 1]
        named = named + (column == lane).astype(jnp.float32)
        listed = listed + jnp.where(lane == k, column, 0).astype(jnp.float32)
    earlier = (
        lax.broadcasted_iota(jnp.int32, (tokens, tokens), 1)
        < lax.broadcasted_iota(jnp.int32, (tokens, tokens), 0)
    ).astype(jnp.bfloat16)
    places = jnp.dot(earlier, named.astype(jnp.bfloat16), preferred_element_type=jnp.float32)
    pair = lax.broadcasted_iota(jnp.int32, (count, LANES), 0)
    lane = lax.broadcasted_iota(jnp.int32, (count, LANES), 1)
    spread = (pair // top == lane).astype(jnp.bfloat16)
    route = jnp.dot(spread, listed.astype(jnp.bfloat16), preferred_element_type=jnp.float32)
    route = jnp.sum(jnp.where(lane == pair % top, route, 0.0), axis=1, keepdims=True)
    route = route.astype(jnp.int32)
    place = jnp.dot(spread, places.astype(jnp.bfloat16), preferred_element_type=jnp.float32)
    place = jnp.sum(jnp.where(lane == route, place, 0.0), axis=1, keepdims=True).astype(jnp.int32)
    slot = jnp.zeros_like(route)
    for j in range(plan.planes):
        slot = jnp.where(route // GROUP == info[plan.planes_at + j], j, slot)
    row = (route % GROUP) // 2 - info[plan.planes_at + plan.planes]
    row = jnp.where(row < 0, row + plan.rows, row)
    side = jnp.where(route % 2 == info[plan.planes_at + plan.planes + 1], 0, 1)
    base = ((side * plan.rows + row) * plan.planes + slot) * plan.back
    target = base + place
    gate_line = base + plan.cap
    out_ref[...] = jnp.where(lane == 0, target, jnp.where(lane == 1, gate_line, place))


def target_work(plan, info, route_ids):
    vmem = pl.BlockSpec(memory_space=pltpu.VMEM)
    return pl.pallas_call(
        functools.partial(target_kernel, plan),
        out_shape=jax.ShapeDtypeStruct((plan.tokens * plan.top, LANES), jnp.int32),
        in_specs=[pl.BlockSpec(memory_space=pltpu.SMEM), vmem],
        out_specs=vmem,
        compiler_params=pltpu.CompilerParams(vmem_limit_bytes=8 * 1024 * 1024),
    )(info, route_ids)


def final_kernel(plan, target_ref, *refs):
    head_ref, out_gate_ref = refs[GROUP:]
    length = plan.rows * plan.planes * plan.back
    table = jnp.concatenate([ref[...] for ref in refs[:GROUP]], axis=0)
    block = 256
    for start in range(0, plan.tokens * plan.top, block):
        at = pl.ds(start, block)
        slot_of = lax.broadcasted_iota(jnp.int32, (block, 2 * length), 1)
        hot = (slot_of == target_ref[at, 0:1]).astype(jnp.bfloat16)
        head_ref[at, :] = jnp.dot(hot, table, preferred_element_type=jnp.float32).astype(jnp.bfloat16)
        hot = (slot_of == target_ref[at, 1:2]).astype(jnp.bfloat16)
        lines = jnp.dot(hot, table, preferred_element_type=jnp.float32)
        lane_of = lax.broadcasted_iota(jnp.int32, (block, LANES), 1)
        out_gate_ref[at, :] = jnp.sum(
            jnp.where(lane_of == target_ref[at, 2:3], lines, 0.0), axis=1, keepdims=True
        )


def final_work(plan, target, tables):
    count = plan.tokens * plan.top
    vmem = pl.BlockSpec(memory_space=pltpu.VMEM)
    return pl.pallas_call(
        functools.partial(final_kernel, plan),
        cost_estimate=pl.CostEstimate(flops=1, bytes_accessed=1, transcendentals=0),
        out_shape=(
            jax.ShapeDtypeStruct((count, plan.head_dim), jnp.bfloat16),
            jax.ShapeDtypeStruct((count, 1), jnp.float32),
        ),
        in_specs=[vmem] * (1 + GROUP),
        out_specs=(vmem, vmem),
        compiler_params=pltpu.CompilerParams(vmem_limit_bytes=8 * 1024 * 1024),
    )(target, *tables)


def local(mesh, head_outputs, out_grad, gate_weights, route_ids, out_proj):
    tokens, top, head_dim = head_outputs.shape
    features = out_grad.shape[1]
    plan = Plan(mesh, tokens, top, head_dim, features)
    x = lax.axis_index("dp")
    me = lax.axis_index("expert")
    z, y, c = me // GROUP, (me % GROUP) // 2, me % 2

    if plan.planes == 4:
        inner = (z == 1) | (z == 2)
        mates, middle = [(0, 1), (1, 0), (2, 3), (3, 2)], [(1, 2), (2, 1)]
        outward, inward = [(1, 0), (2, 3)], [(0, 1), (3, 2)]
        across = [(1, 3), (2, 0)]
        plane_of = [jnp.where(z < 2, 2, 1), jnp.where(z < 2, 3, 0), z ^ 1, z]
        which = jnp.where(inner, 0, 1)
    else:
        steps = [k % plan.planes for k in range(1, plan.planes + 1)]
        plane_of = [(z + k) % plan.planes for k in steps]
        which = 0
    info = plan.info(x, z, y, c, plane_of, which)

    own_weights = lax.dynamic_slice_in_dim(out_proj[0], x * plan.part, plan.part, 1)
    target = target_work(plan, info, route_ids)
    if plan.planes == 4:
        mate = plan.along(own_weights, mates)
        near_in = plan.along(own_weights, middle)
        mate, near_in, target = lax.optimization_barrier((mate, near_in, target))
        near_out = plan.along(near_in, outward)
        far_in, near_out = lax.optimization_barrier((plan.along(mate, middle), near_out))
        far_out = plan.along(far_in, outward)
    else:
        weights = [[(plan.shift(own_weights, dz=-k % plan.planes), None)] for k in steps]

    meta = jnp.concatenate(
        [
            gate_weights.T,
            route_ids.T.astype(jnp.bfloat16),
            jnp.zeros((LANES - 2 * top, tokens), jnp.bfloat16),
        ],
        axis=0,
    )
    flat_heads = head_outputs.reshape(tokens, top * head_dim)
    packs = []
    for dx, dy in plan.chips():
        piece = lax.dynamic_slice_in_dim(out_grad, ((x + dx) % plan.dp) * plan.part, plan.part, 1)
        value = jnp.concatenate([piece, flat_heads, meta], axis=1)
        if plan.planes == 4 and dx and dy:
            value, near_in, mate = lax.optimization_barrier((value, near_in, mate))
        value = plan.shift(value, dx=dx, dy=dy)
        packs.append(value)

    if plan.planes == 4:
        weights = [
            [(near_in, 0), (near_out, 1)],
            [(far_in, 0), (far_out, 1)],
            [(mate, None)],
            [(own_weights, None)],
        ]

    if plan.planes == 4:
        packs[:2] = lax.optimization_barrier(packs[:2])
    held = [(value, plan.shift(value, dc=1)) for value in packs[:-1]]
    held = [value for pair in held for value in pair]

    last = plan.planes - 1
    calls = [(j, 0) for j in [last, *range(last)]] + [(j, 1) for j in range(plan.planes)]
    if plan.planes == 4:
        calls = [(3, 0), (2, 0), (0, 0), (0, 1), (1, 0), (1, 1), (2, 1), (3, 1)]
    sums, backs, done, far = {}, [], target, None
    for j, late in calls:
        final = (j, late) == (last, 1)
        if late and far is None:
            value, info, done = lax.optimization_barrier((packs[-1], info, done))
            if plan.planes == 4:
                value, far_out = lax.optimization_barrier((value, far_out))
            far = [value, plan.shift(value, dc=1)]
        if final and plan.planes == 4:
            near_sum = sums[0] + plan.along(sums[0], inward)
            done = (done, near_sum)
        info, done = lax.optimization_barrier((info, done))
        sums[j], *back = slot_work(
            plan,
            j,
            plan.sources - 2 if late else 0,
            info,
            far if late else held,
            weights[j],
            jnp.bfloat16 if late and not final else jnp.float32,
            [sums[j]] if late else [],
            backs if final else [],
        )
        backs = back if final else backs + [(j, plan.sources - 2 if late else 0, back[0])]
        done = back[0]

    far_pieces = []
    if plan.planes == 4:
        far_part = plan.along(sums[1], inward)
        far_part, done = lax.optimization_barrier((far_part, done))
        far_sums = sum_work(plan, info, [sums[1], far_part], jnp.bfloat16)
        info, far_sums = lax.optimization_barrier((info, far_sums))
        far_pieces = [plan.along(piece, across, dx) for dx, piece in enumerate(far_sums)]
        mate_sums = sum_work(plan, info, [sums[2]], jnp.bfloat16)
        far_pieces += [plan.along(piece, mates, dx) for dx, piece in enumerate(mate_sums)]
        received = [plan.along(near_sum, middle)]
    else:
        received = [plan.shift(sums[j], dz=steps[j]) for j in range(plan.planes - 1)]
    pieces = sum_work(plan, info, [sums[last]] + received, jnp.float32)
    pieces = [plan.shift(piece, dx=dx) for dx, piece in enumerate(pieces)]

    backs = [plan.shift(rows, dx=-dx % plan.dp) for dx, rows in enumerate(backs)]
    if plan.planes == 4:
        backs, far_sums = lax.optimization_barrier((backs, far_sums))
    merged = merge_work(plan, backs)
    tables = [
        plan.shift(merged[2 * dy + dc], dy=-dy % plan.rows)
        for dy in range(plan.rows)
        for dc in range(2)
    ]
    tables = tables[0::2] + [plan.shift(rows, dc=1) for rows in tables[1::2]]
    tables, far_pieces, pieces = lax.optimization_barrier((tables, far_pieces, pieces))
    grad_head, grad_gate = final_work(plan, target, tables)
    grad_proj = layout_work(plan, info, pieces + far_pieces)
    return (
        grad_head.reshape(tokens, top, head_dim),
        grad_gate.reshape(tokens, top).astype(jnp.bfloat16),
        grad_proj[None],
    )


def solution(mesh):
    return jax.shard_map(
        functools.partial(local, mesh),
        mesh=mesh,
        in_specs=(
            P(("dp", "expert"), None, None),
            P(("dp", "expert"), None),
            P(("dp", "expert"), None),
            P(("dp", "expert"), None),
            P("expert", None, None),
        ),
        out_specs=(
            P(("dp", "expert"), None, None),
            P(("dp", "expert"), None),
            P("expert", "dp", None),
        ),
        check_vma=False,
    )
```

```python
import functools

import jax
import jax.numpy as jnp
from jax import lax
from jax.experimental import pallas as pl
from jax.experimental.pallas import tpu as pltpu
from jax.sharding import PartitionSpec as P

soft_cap = 1.5
AXES = ("dp", "expert")
GROUP = 4
LANES = 128


class Plan:
    def __init__(self, mesh, tokens, top, head_dim, features):
        self.dp = mesh.shape["dp"]
        self.experts = mesh.shape["expert"]
        self.rows = GROUP // 2
        self.planes = self.experts // GROUP
        self.sources = self.dp * GROUP
        self.tokens, self.top, self.head_dim = tokens, top, head_dim
        self.part = features // self.dp
        self.own_rows = head_dim // self.dp
        cap = 9 * tokens * top // (8 * self.experts)
        self.cap = -(-cap // 8) * 8
        self.back = self.cap + 8
        self.width = self.part + top * head_dim + LANES

    def index(self, x, z, y, c):
        return x * self.experts + z * GROUP + y * 2 + c

    def pairs(self, dx=0, dz=0, dy=0, dc=0):
        out = []
        for x in range(self.dp):
            for z in range(self.planes):
                for y in range(self.rows):
                    for c in range(2):
                        target = self.index(
                            (x + dx) % self.dp,
                            (z + dz) % self.planes,
                            (y + dy) % self.rows,
                            c ^ dc,
                        )
                        out.append((self.index(x, z, y, c), target))
        return out

    def shift(self, value, **by):
        if not any(by.values()):
            return value
        return lax.ppermute(value, AXES, self.pairs(**by))

    def along(self, value, moves, dx=0, dy=0):
        out = []
        for x in range(self.dp):
            for a, b in moves:
                for y in range(self.rows):
                    for c in range(2):
                        target = self.index((x + dx) % self.dp, b, (y + dy) % self.rows, c)
                        out.append((self.index(x, a, y, c), target))
        return lax.ppermute(value, AXES, out)

    def info(self, x, z, y, c, plane_of, which):
        values = [((x + dx) % self.dp) * self.own_rows for dx in range(self.dp)]
        self.lanes_at = len(values)
        values += [((x - dx) % self.dp) * self.part for dx in range(self.dp)]
        self.which_at = len(values)
        values += [which]
        self.experts_at = len(values)
        values += [plane_of[j] * GROUP + y * 2 + c for j in range(self.planes)]
        self.planes_at = len(values)
        values += list(plane_of) + [y, c]
        return jnp.stack([jnp.asarray(value, jnp.int32) for value in values])

    def chips(self):
        return [(dx, dy) for dx in range(self.dp) for dy in range(self.rows)]


def slot_kernel(plan, index, where, earlier, info, *refs):
    packs, rest = refs[: plan.sources], refs[plan.sources :]
    weight_refs, rest = rest[: len(where)], rest[len(where) :]
    earlier_refs, rest = rest[:earlier], rest[earlier:]
    count = plan.dp if earlier else 1
    p_ref, back_refs, (grads, heads, weights) = rest[0], rest[1 : 1 + count], rest[1 + count :]
    tokens, cap, part, top, head_dim = plan.tokens, plan.cap, plan.part, plan.top, plan.head_dim
    pair_rows = 2 * cap
    pair_total = plan.sources // 2
    length = plan.planes * plan.back

    def put(s, slot, at, value):
        if earlier:
            start = (s % GROUP) * length + slot * plan.back + at
            back_refs[s // GROUP][pl.ds(start, value.shape[0]), :] = value
        else:
            back_refs[0][s, pl.ds(at, value.shape[0]), :] = value

    if len(where) > 1:
        for ref, kind in zip(weight_refs, where):

            @pl.when(info[plan.which_at] == kind)
            def _():
                weights[...] = ref[...]

        weight_ref = weights
    else:
        weight_ref = weight_refs[0]
    expert = info[plan.experts_at + index].astype(jnp.float32)
    row_of = lax.broadcasted_iota(jnp.int32, (cap, tokens), 0)
    diagonal = (row_of == lax.broadcasted_iota(jnp.int32, (cap, tokens), 1)).astype(jnp.float32)
    before = (
        lax.broadcasted_iota(jnp.int32, (tokens, tokens), 0)
        < lax.broadcasted_iota(jnp.int32, (tokens, tokens), 1)
    ).astype(jnp.bfloat16)
    block_row = lax.broadcasted_iota(jnp.int32, (8, LANES), 0)
    empty = jnp.zeros((cap, tokens), jnp.bfloat16)
    chunk = min(part, 512)

    masks, occupied, gate_rows = [], [], []
    for s in range(plan.sources):
        meta = packs[s][pl.ds(0, 2 * top), pl.ds(part + top * head_dim, LANES)].astype(jnp.float32)
        mask = (meta[top:] == expert).astype(jnp.float32)
        masks.append(mask)
        occupied.append(jnp.sum(mask, axis=0, keepdims=True))
        gate_rows.append(jnp.sum(mask * meta[:top], axis=0, keepdims=True))
    filled = occupied + [jnp.zeros((1, tokens), jnp.float32)] * (-plan.sources % 16)
    places = jnp.dot(
        jnp.concatenate(filled, axis=0).astype(jnp.bfloat16),
        before,
        preferred_element_type=jnp.float32,
    ).astype(jnp.int32)
    for q in range(pair_total):
        hots, gates = [], []
        for b in range(2):
            s = 2 * q + b
            hot = jnp.where(row_of == places[s : s + 1], occupied[s], 0.0)
            gates.append(jnp.sum(hot * gate_rows[s], axis=1, keepdims=True))
            hots.append(hot.astype(jnp.bfloat16))
            wide = jnp.concatenate(
                [(hot * masks[s][k : k + 1]).astype(jnp.bfloat16) for k in range(top)], axis=1
            )
            raw = jnp.concatenate(
                [packs[s][:, pl.ds(part + k * head_dim, head_dim)] for k in range(top)], axis=0
            )
            heads[pl.ds(s * cap, cap), :] = jnp.dot(
                wide, raw, preferred_element_type=jnp.float32
            ).astype(jnp.bfloat16)
        all_hots = jnp.concatenate(
            [
                jnp.concatenate([hots[0], empty], axis=1),
                jnp.concatenate([empty, hots[1]], axis=1),
            ],
            axis=0,
        )
        gate = jnp.broadcast_to(jnp.concatenate(gates, axis=0), (pair_rows, LANES))
        total = jnp.zeros((pair_rows, LANES), jnp.float32)
        rows_at = pl.ds(q * pair_rows, pair_rows)
        for start in range(0, part, chunk):
            both = jnp.concatenate(
                [packs[2 * q + b][:, pl.ds(start, chunk)] for b in range(2)], axis=0
            )
            grad = jnp.dot(all_hots, both, preferred_element_type=jnp.float32)
            pre = jnp.dot(
                heads[rows_at, :], weight_ref[:, pl.ds(start, chunk)], preferred_element_type=jnp.float32
            )
            for lane in range(0, chunk, LANES):
                grad_block = grad[:, lane : lane + LANES]
                capped = jnp.tanh(pre[:, lane : lane + LANES] * (1.0 / soft_cap))
                total = total + grad_block * capped
                grads[rows_at, pl.ds(start + lane, LANES)] = (
                    gate * grad_block * (1.0 - capped * capped)
                ).astype(jnp.bfloat16)
        for b in range(2):
            column = jnp.sum(total[b * cap : (b + 1) * cap], axis=1, keepdims=True) * soft_cap
            line = jnp.sum(diagonal * column, axis=0, keepdims=True)
            block = jnp.where(block_row == 0, line, 0.0).astype(jnp.bfloat16)
            put(2 * q + b, plan.planes - 1, cap, block)
    grad_all = grads[...]
    p_ref[...] = lax.dot_general(
        heads[...], grad_all, (((0,), (0,)), ((), ())), preferred_element_type=jnp.float32
    ).astype(p_ref.dtype)
    rows = lax.dot_general(
        grad_all, weight_ref[...], (((1,), (1,)), ((), ())), preferred_element_type=jnp.float32
    ).astype(jnp.bfloat16)
    for s in range(plan.sources):
        put(s, plan.planes - 1, 0, rows[s * cap : (s + 1) * cap])
    for j, ref in enumerate(earlier_refs):
        for s in range(plan.sources):
            put(s, j, 0, ref[s])


def slot_work(plan, index, info, packs, weights, kind, earlier=()):
    rows = plan.sources * plan.cap
    if earlier:
        backs = (
            jax.ShapeDtypeStruct((GROUP * plan.planes * plan.back, LANES), jnp.bfloat16),
        ) * plan.dp
    else:
        backs = (jax.ShapeDtypeStruct((plan.sources, plan.back, LANES), jnp.bfloat16),)
    vmem = pl.BlockSpec(memory_space=pltpu.VMEM)
    return pl.pallas_call(
        functools.partial(slot_kernel, plan, index, [where for _, where in weights], len(earlier)),
        out_shape=(jax.ShapeDtypeStruct((plan.head_dim, plan.part), kind), *backs),
        in_specs=[pl.BlockSpec(memory_space=pltpu.SMEM)]
        + [vmem] * (plan.sources + len(weights) + len(earlier)),
        out_specs=(vmem,) * (1 + len(backs)),
        scratch_shapes=[
            pltpu.VMEM((rows, plan.part), jnp.bfloat16),
            pltpu.VMEM((rows, plan.head_dim), jnp.bfloat16),
            pltpu.VMEM((plan.head_dim, plan.part), jnp.bfloat16),
        ],
        compiler_params=pltpu.CompilerParams(vmem_limit_bytes=14 * 1024 * 1024),
    )(info, *packs, *[array for array, _ in weights], *earlier)


def sum_kernel(plan, info, *refs):
    parts, pieces = refs[: len(refs) - plan.dp], refs[len(refs) - plan.dp :]
    rows = plan.own_rows
    for j, piece in enumerate(pieces):
        at = pl.ds(pl.multiple_of(info[j], rows), rows)
        total = parts[0][at, :].astype(jnp.float32)
        for ref in parts[1:]:
            total = total + ref[at, :].astype(jnp.float32)
        piece[...] = total.astype(piece.dtype)


def sum_work(plan, info, parts, own_kind):
    rows = plan.head_dim // plan.dp
    vmem = pl.BlockSpec(memory_space=pltpu.VMEM)
    return pl.pallas_call(
        functools.partial(sum_kernel, plan),
        compiler_params=pltpu.CompilerParams(vmem_limit_bytes=6 * 1024 * 1024),
        out_shape=tuple(
            jax.ShapeDtypeStruct((rows, plan.part), jnp.bfloat16 if j else own_kind)
            for j in range(plan.dp)
        ),
        in_specs=[pl.BlockSpec(memory_space=pltpu.SMEM)] + [vmem] * len(parts),
        out_specs=(vmem,) * plan.dp,
    )(info, *parts)


def layout_kernel(plan, info, *refs):
    out_ref = refs[-1]
    for j in range(plan.dp):
        at = pl.ds(pl.multiple_of(info[plan.lanes_at + j], plan.part), plan.part)
        total = None
        for ref in refs[j : -1 : plan.dp]:
            piece = ref[...].astype(jnp.float32)
            total = piece if total is None else total + piece
        out_ref[:, at] = total


def layout_work(plan, info, pieces):
    rows = plan.head_dim // plan.dp
    vmem = pl.BlockSpec(memory_space=pltpu.VMEM)
    return pl.pallas_call(
        functools.partial(layout_kernel, plan),
        compiler_params=pltpu.CompilerParams(vmem_limit_bytes=6 * 1024 * 1024),
        out_shape=jax.ShapeDtypeStruct((rows, plan.part * plan.dp), jnp.float32),
        in_specs=[pl.BlockSpec(memory_space=pltpu.SMEM)] + [vmem] * len(pieces),
        out_specs=vmem,
    )(info, *pieces)


def merge_kernel(plan, *refs):
    parts, outs = refs[: plan.dp], refs[plan.dp :]
    length = plan.planes * plan.back
    for j, out in enumerate(outs):
        at = pl.ds(j * length, length)
        total = parts[0][at, :].astype(jnp.float32)
        for ref in parts[1:]:
            total = total + ref[at, :].astype(jnp.float32)
        out[...] = total.astype(out.dtype)


def merge_work(plan, parts):
    vmem = pl.BlockSpec(memory_space=pltpu.VMEM)
    rows = jax.ShapeDtypeStruct((plan.planes * plan.back, LANES), jnp.bfloat16)
    return pl.pallas_call(
        functools.partial(merge_kernel, plan),
        compiler_params=pltpu.CompilerParams(vmem_limit_bytes=6 * 1024 * 1024),
        out_shape=(rows,) * GROUP,
        in_specs=[vmem] * plan.dp,
        out_specs=(vmem,) * GROUP,
    )(*parts)


def target_kernel(plan, info, route_ref, out_ref):
    tokens, top = plan.tokens, plan.top
    count = tokens * top
    lane = lax.broadcasted_iota(jnp.int32, (tokens, LANES), 1)
    routes = route_ref[...]
    named = jnp.zeros((tokens, LANES), jnp.float32)
    listed = jnp.zeros((tokens, LANES), jnp.float32)
    for k in range(top):
        column = routes[:, k : k + 1]
        named = named + (column == lane).astype(jnp.float32)
        listed = listed + jnp.where(lane == k, column, 0).astype(jnp.float32)
    earlier = (
        lax.broadcasted_iota(jnp.int32, (tokens, tokens), 1)
        < lax.broadcasted_iota(jnp.int32, (tokens, tokens), 0)
    ).astype(jnp.bfloat16)
    places = jnp.dot(earlier, named.astype(jnp.bfloat16), preferred_element_type=jnp.float32)
    pair = lax.broadcasted_iota(jnp.int32, (count, LANES), 0)
    lane = lax.broadcasted_iota(jnp.int32, (count, LANES), 1)
    spread = (pair // top == lane).astype(jnp.bfloat16)
    route = jnp.dot(spread, listed.astype(jnp.bfloat16), preferred_element_type=jnp.float32)
    route = jnp.sum(jnp.where(lane == pair % top, route, 0.0), axis=1, keepdims=True)
    route = route.astype(jnp.int32)
    place = jnp.dot(spread, places.astype(jnp.bfloat16), preferred_element_type=jnp.float32)
    place = jnp.sum(jnp.where(lane == route, place, 0.0), axis=1, keepdims=True).astype(jnp.int32)
    slot = jnp.zeros_like(route)
    for j in range(plan.planes):
        slot = jnp.where(route // GROUP == info[plan.planes_at + j], j, slot)
    row = (route % GROUP) // 2 - info[plan.planes_at + plan.planes]
    row = jnp.where(row < 0, row + plan.rows, row)
    side = jnp.where(route % 2 == info[plan.planes_at + plan.planes + 1], 0, 1)
    base = ((side * plan.rows + row) * plan.planes + slot) * plan.back
    target = base + place
    gate_line = base + plan.cap
    out_ref[...] = jnp.where(lane == 0, target, jnp.where(lane == 1, gate_line, place))


def target_work(plan, info, route_ids):
    vmem = pl.BlockSpec(memory_space=pltpu.VMEM)
    return pl.pallas_call(
        functools.partial(target_kernel, plan),
        out_shape=jax.ShapeDtypeStruct((plan.tokens * plan.top, LANES), jnp.int32),
        in_specs=[pl.BlockSpec(memory_space=pltpu.SMEM), vmem],
        out_specs=vmem,
        compiler_params=pltpu.CompilerParams(vmem_limit_bytes=8 * 1024 * 1024),
    )(info, route_ids)


def final_kernel(plan, target_ref, *refs):
    head_ref, out_gate_ref = refs[GROUP:]
    length = plan.rows * plan.planes * plan.back
    table = jnp.concatenate([ref[...] for ref in refs[:GROUP]], axis=0)
    block = 256
    for start in range(0, plan.tokens * plan.top, block):
        at = pl.ds(start, block)
        slot_of = lax.broadcasted_iota(jnp.int32, (block, 2 * length), 1)
        hot = (slot_of == target_ref[at, 0:1]).astype(jnp.bfloat16)
        head_ref[at, :] = jnp.dot(hot, table, preferred_element_type=jnp.float32).astype(jnp.bfloat16)
        hot = (slot_of == target_ref[at, 1:2]).astype(jnp.bfloat16)
        lines = jnp.dot(hot, table, preferred_element_type=jnp.float32)
        lane_of = lax.broadcasted_iota(jnp.int32, (block, LANES), 1)
        out_gate_ref[at, :] = jnp.sum(
            jnp.where(lane_of == target_ref[at, 2:3], lines, 0.0), axis=1, keepdims=True
        )


def final_work(plan, target, tables):
    count = plan.tokens * plan.top
    vmem = pl.BlockSpec(memory_space=pltpu.VMEM)
    return pl.pallas_call(
        functools.partial(final_kernel, plan),
        cost_estimate=pl.CostEstimate(flops=1, bytes_accessed=1, transcendentals=0),
        out_shape=(
            jax.ShapeDtypeStruct((count, plan.head_dim), jnp.bfloat16),
            jax.ShapeDtypeStruct((count, 1), jnp.float32),
        ),
        in_specs=[vmem] * (1 + GROUP),
        out_specs=(vmem, vmem),
        compiler_params=pltpu.CompilerParams(vmem_limit_bytes=8 * 1024 * 1024),
    )(target, *tables)


def local(mesh, head_outputs, out_grad, gate_weights, route_ids, out_proj):
    tokens, top, head_dim = head_outputs.shape
    features = out_grad.shape[1]
    plan = Plan(mesh, tokens, top, head_dim, features)
    x = lax.axis_index("dp")
    me = lax.axis_index("expert")
    z, y, c = me // GROUP, (me % GROUP) // 2, me % 2

    if plan.planes == 4:
        inner = (z == 1) | (z == 2)
        mates, middle = [(0, 1), (1, 0), (2, 3), (3, 2)], [(1, 2), (2, 1)]
        outward, inward = [(1, 0), (2, 3)], [(0, 1), (3, 2)]
        across = [(1, 3), (2, 0)]
        plane_of = [jnp.where(z < 2, 2, 1), jnp.where(z < 2, 3, 0), z ^ 1, z]
        which = jnp.where(inner, 0, 1)
    else:
        steps = [k % plan.planes for k in range(1, plan.planes + 1)]
        plane_of = [(z + k) % plan.planes for k in steps]
        which = 0
    info = plan.info(x, z, y, c, plane_of, which)

    own_weights = lax.dynamic_slice_in_dim(out_proj[0], x * plan.part, plan.part, 1)
    target = target_work(plan, info, route_ids)
    if plan.planes == 4:
        mate = plan.along(own_weights, mates)
        near_in = plan.along(own_weights, middle)
        mate, near_in, target = lax.optimization_barrier((mate, near_in, target))
        near_out = plan.along(near_in, outward)
        far_in, near_out = lax.optimization_barrier((plan.along(mate, middle), near_out))
        far_out = plan.along(far_in, outward)
    else:
        weights = [[(plan.shift(own_weights, dz=-k % plan.planes), None)] for k in steps]

    meta = jnp.concatenate(
        [
            gate_weights.T,
            route_ids.T.astype(jnp.bfloat16),
            jnp.zeros((LANES - 2 * top, tokens), jnp.bfloat16),
        ],
        axis=0,
    )
    flat_heads = head_outputs.reshape(tokens, top * head_dim)
    packs = []
    for dx, dy in plan.chips():
        piece = lax.dynamic_slice_in_dim(out_grad, ((x + dx) % plan.dp) * plan.part, plan.part, 1)
        value = jnp.concatenate([piece, flat_heads, meta], axis=1)
        value = plan.shift(value, dx=dx, dy=dy)
        if plan.planes == 4:
            if dx or dy:
                value, far_in, near_out = lax.optimization_barrier((value, far_in, near_out))
            else:
                value, near_out = lax.optimization_barrier((value, near_out))
        packs += [value, plan.shift(value, dc=1)]

    if plan.planes == 4:
        weights = [
            [(near_in, 0), (near_out, 1)],
            [(far_in, 0), (far_out, 1)],
            [(mate, None)],
            [(own_weights, None)],
        ]

    sums, backs, done = [], [], target
    for j in range(plan.planes):
        last = j == plan.planes - 1
        if last and plan.planes == 4:
            near_sum = sums[0] + plan.along(sums[0], inward)
            done = (done, near_sum)
        info, done = lax.optimization_barrier((info, done))
        target = target if j else done
        kind = jnp.float32 if last else jnp.bfloat16
        part, *back = slot_work(plan, j, info, packs, weights[j], kind, backs if last else ())
        sums.append(part)
        backs = back if last else backs + back
        done = back[0]

    far_pieces = []
    if plan.planes == 4:
        far_part = plan.along(sums[1], inward)
        far_part, done = lax.optimization_barrier((far_part, done))
        far_sums = sum_work(plan, info, [sums[1], far_part], jnp.bfloat16)
        info, far_sums = lax.optimization_barrier((info, far_sums))
        far_pieces = [plan.along(piece, across, dx) for dx, piece in enumerate(far_sums)]
        received = [plan.along(sums[2], mates), plan.along(near_sum, middle)]
    else:
        received = [plan.shift(sums[j], dz=steps[j]) for j in range(plan.planes - 1)]
    pieces = sum_work(plan, info, [sums[-1]] + received, jnp.float32)
    pieces = [plan.shift(piece, dx=dx) for dx, piece in enumerate(pieces)]

    backs = [plan.shift(rows, dx=-dx % plan.dp) for dx, rows in enumerate(backs)]
    if plan.planes == 4:
        backs, far_sums = lax.optimization_barrier((backs, far_sums))
    merged = merge_work(plan, backs)
    tables = [
        plan.shift(merged[2 * dy + dc], dy=-dy % plan.rows)
        for dy in range(plan.rows)
        for dc in range(2)
    ]
    tables = tables[0::2] + [plan.shift(rows, dc=1) for rows in tables[1::2]]
    tables, far_pieces[:1] = lax.optimization_barrier((tables, far_pieces[:1]))
    grad_head, grad_gate = final_work(plan, target, tables)
    grad_proj = layout_work(plan, info, pieces + far_pieces)
    return (
        grad_head.reshape(tokens, top, head_dim),
        grad_gate.reshape(tokens, top).astype(jnp.bfloat16),
        grad_proj[None],
    )


def solution(mesh):
    return jax.shard_map(
        functools.partial(local, mesh),
        mesh=mesh,
        in_specs=(
            P(("dp", "expert"), None, None),
            P(("dp", "expert"), None),
            P(("dp", "expert"), None),
            P(("dp", "expert"), None),
            P("expert", None, None),
        ),
        out_specs=(
            P(("dp", "expert"), None, None),
            P(("dp", "expert"), None),
            P("expert", "dp", None),
        ),
        check_vma=False,
    )
```

```python
import functools

import jax
import jax.numpy as jnp
from jax import lax
from jax.experimental import pallas as pl
from jax.experimental.pallas import tpu as pltpu
from jax.sharding import PartitionSpec as P

soft_cap = 1.5
AXES = ("dp", "expert")
GROUP = 4
LANES = 128


class Plan:
    def __init__(self, mesh, tokens, top, head_dim, features):
        self.dp = mesh.shape["dp"]
        self.experts = mesh.shape["expert"]
        self.rows = GROUP // 2
        self.planes = self.experts // GROUP
        self.sources = self.dp * GROUP
        self.tokens, self.top, self.head_dim = tokens, top, head_dim
        self.part = features // self.dp
        self.own_rows = head_dim // self.dp
        cap = 9 * tokens * top // (8 * self.experts)
        self.cap = -(-cap // 8) * 8
        self.back = self.cap + 8
        self.width = self.part + top * head_dim + LANES

    def index(self, x, z, y, c):
        return x * self.experts + z * GROUP + y * 2 + c

    def pairs(self, dx=0, dz=0, dy=0, dc=0):
        out = []
        for x in range(self.dp):
            for z in range(self.planes):
                for y in range(self.rows):
                    for c in range(2):
                        target = self.index(
                            (x + dx) % self.dp,
                            (z + dz) % self.planes,
                            (y + dy) % self.rows,
                            c ^ dc,
                        )
                        out.append((self.index(x, z, y, c), target))
        return out

    def shift(self, value, **by):
        if not any(by.values()):
            return value
        return lax.ppermute(value, AXES, self.pairs(**by))

    def along(self, value, moves, dx=0, dy=0):
        out = []
        for x in range(self.dp):
            for a, b in moves:
                for y in range(self.rows):
                    for c in range(2):
                        target = self.index((x + dx) % self.dp, b, (y + dy) % self.rows, c)
                        out.append((self.index(x, a, y, c), target))
        return lax.ppermute(value, AXES, out)

    def info(self, x, z, y, c, plane_of, which):
        values = [((x + dx) % self.dp) * self.own_rows for dx in range(self.dp)]
        self.lanes_at = len(values)
        values += [((x - dx) % self.dp) * self.part for dx in range(self.dp)]
        self.which_at = len(values)
        values += [which]
        self.experts_at = len(values)
        values += [plane_of[j] * GROUP + y * 2 + c for j in range(self.planes)]
        self.planes_at = len(values)
        values += list(plane_of) + [y, c]
        return jnp.stack([jnp.asarray(value, jnp.int32) for value in values])

    def chips(self):
        return [(dx, dy) for dx in range(self.dp) for dy in range(self.rows)]


def slot_kernel(plan, index, where, earlier, info, *refs):
    packs, rest = refs[: plan.sources], refs[plan.sources :]
    weight_refs, rest = rest[: len(where)], rest[len(where) :]
    earlier_refs, rest = rest[:earlier], rest[earlier:]
    count = plan.dp if earlier else 1
    p_ref, back_refs, (grads, heads, weights) = rest[0], rest[1 : 1 + count], rest[1 + count :]
    tokens, cap, part, top, head_dim = plan.tokens, plan.cap, plan.part, plan.top, plan.head_dim
    pair_rows = 2 * cap
    pair_total = plan.sources // 2
    length = plan.planes * plan.back

    def put(s, slot, at, value):
        if earlier:
            start = (s % GROUP) * length + slot * plan.back + at
            back_refs[s // GROUP][pl.ds(start, value.shape[0]), :] = value
        else:
            back_refs[0][s, pl.ds(at, value.shape[0]), :] = value

    if len(where) > 1:
        for ref, kind in zip(weight_refs, where):

            @pl.when(info[plan.which_at] == kind)
            def _():
                weights[...] = ref[...]

        weight_ref = weights
    else:
        weight_ref = weight_refs[0]
    expert = info[plan.experts_at + index].astype(jnp.float32)
    row_of = lax.broadcasted_iota(jnp.int32, (cap, tokens), 0)
    diagonal = (row_of == lax.broadcasted_iota(jnp.int32, (cap, tokens), 1)).astype(jnp.float32)
    before = (
        lax.broadcasted_iota(jnp.int32, (tokens, tokens), 0)
        < lax.broadcasted_iota(jnp.int32, (tokens, tokens), 1)
    ).astype(jnp.bfloat16)
    block_row = lax.broadcasted_iota(jnp.int32, (8, LANES), 0)
    empty = jnp.zeros((cap, tokens), jnp.bfloat16)
    chunk = min(part, 512)

    masks, occupied, gate_rows = [], [], []
    for s in range(plan.sources):
        meta = packs[s][pl.ds(0, 2 * top), pl.ds(part + top * head_dim, LANES)].astype(jnp.float32)
        mask = (meta[top:] == expert).astype(jnp.float32)
        masks.append(mask)
        occupied.append(jnp.sum(mask, axis=0, keepdims=True))
        gate_rows.append(jnp.sum(mask * meta[:top], axis=0, keepdims=True))
    filled = occupied + [jnp.zeros((1, tokens), jnp.float32)] * (-plan.sources % 16)
    places = jnp.dot(
        jnp.concatenate(filled, axis=0).astype(jnp.bfloat16),
        before,
        preferred_element_type=jnp.float32,
    ).astype(jnp.int32)
    for q in range(pair_total):
        hots, gates = [], []
        for b in range(2):
            s = 2 * q + b
            hot = jnp.where(row_of == places[s : s + 1], occupied[s], 0.0)
            gates.append(jnp.sum(hot * gate_rows[s], axis=1, keepdims=True))
            hots.append(hot.astype(jnp.bfloat16))
            wide = jnp.concatenate(
                [(hot * masks[s][k : k + 1]).astype(jnp.bfloat16) for k in range(top)], axis=1
            )
            raw = jnp.concatenate(
                [packs[s][:, pl.ds(part + k * head_dim, head_dim)] for k in range(top)], axis=0
            )
            heads[pl.ds(s * cap, cap), :] = jnp.dot(
                wide, raw, preferred_element_type=jnp.float32
            ).astype(jnp.bfloat16)
        all_hots = jnp.concatenate(
            [
                jnp.concatenate([hots[0], empty], axis=1),
                jnp.concatenate([empty, hots[1]], axis=1),
            ],
            axis=0,
        )
        gate = jnp.broadcast_to(jnp.concatenate(gates, axis=0), (pair_rows, LANES))
        total = jnp.zeros((pair_rows, LANES), jnp.float32)
        rows_at = pl.ds(q * pair_rows, pair_rows)
        for start in range(0, part, chunk):
            both = jnp.concatenate(
                [packs[2 * q + b][:, pl.ds(start, chunk)] for b in range(2)], axis=0
            )
            grad = jnp.dot(all_hots, both, preferred_element_type=jnp.float32)
            pre = jnp.dot(
                heads[rows_at, :], weight_ref[:, pl.ds(start, chunk)], preferred_element_type=jnp.float32
            )
            for lane in range(0, chunk, LANES):
                grad_block = grad[:, lane : lane + LANES]
                capped = jnp.tanh(pre[:, lane : lane + LANES] * (1.0 / soft_cap))
                total = total + grad_block * capped
                grads[rows_at, pl.ds(start + lane, LANES)] = (
                    gate * grad_block * (1.0 - capped * capped)
                ).astype(jnp.bfloat16)
        for b in range(2):
            column = jnp.sum(total[b * cap : (b + 1) * cap], axis=1, keepdims=True) * soft_cap
            line = jnp.sum(diagonal * column, axis=0, keepdims=True)
            block = jnp.where(block_row == 0, line, 0.0).astype(jnp.bfloat16)
            put(2 * q + b, plan.planes - 1, cap, block)
    grad_all = grads[...]
    p_ref[...] = lax.dot_general(
        heads[...], grad_all, (((0,), (0,)), ((), ())), preferred_element_type=jnp.float32
    ).astype(p_ref.dtype)
    rows = lax.dot_general(
        grad_all, weight_ref[...], (((1,), (1,)), ((), ())), preferred_element_type=jnp.float32
    ).astype(jnp.bfloat16)
    for s in range(plan.sources):
        put(s, plan.planes - 1, 0, rows[s * cap : (s + 1) * cap])
    for j, ref in enumerate(earlier_refs):
        for s in range(plan.sources):
            put(s, j, 0, ref[s])


def slot_work(plan, index, info, packs, weights, kind, earlier=()):
    rows = plan.sources * plan.cap
    if earlier:
        backs = (
            jax.ShapeDtypeStruct((GROUP * plan.planes * plan.back, LANES), jnp.bfloat16),
        ) * plan.dp
    else:
        backs = (jax.ShapeDtypeStruct((plan.sources, plan.back, LANES), jnp.bfloat16),)
    vmem = pl.BlockSpec(memory_space=pltpu.VMEM)
    return pl.pallas_call(
        functools.partial(slot_kernel, plan, index, [where for _, where in weights], len(earlier)),
        out_shape=(jax.ShapeDtypeStruct((plan.head_dim, plan.part), kind), *backs),
        in_specs=[pl.BlockSpec(memory_space=pltpu.SMEM)]
        + [vmem] * (plan.sources + len(weights) + len(earlier)),
        out_specs=(vmem,) * (1 + len(backs)),
        scratch_shapes=[
            pltpu.VMEM((rows, plan.part), jnp.bfloat16),
            pltpu.VMEM((rows, plan.head_dim), jnp.bfloat16),
            pltpu.VMEM((plan.head_dim, plan.part), jnp.bfloat16),
        ],
        compiler_params=pltpu.CompilerParams(vmem_limit_bytes=14 * 1024 * 1024),
    )(info, *packs, *[array for array, _ in weights], *earlier)


def sum_kernel(plan, info, *refs):
    parts, pieces = refs[: len(refs) - plan.dp], refs[len(refs) - plan.dp :]
    rows = plan.own_rows
    for j, piece in enumerate(pieces):
        at = pl.ds(pl.multiple_of(info[j], rows), rows)
        total = parts[0][at, :].astype(jnp.float32)
        for ref in parts[1:]:
            total = total + ref[at, :].astype(jnp.float32)
        piece[...] = total.astype(piece.dtype)


def sum_work(plan, info, parts, own_kind):
    rows = plan.head_dim // plan.dp
    vmem = pl.BlockSpec(memory_space=pltpu.VMEM)
    return pl.pallas_call(
        functools.partial(sum_kernel, plan),
        compiler_params=pltpu.CompilerParams(vmem_limit_bytes=6 * 1024 * 1024),
        out_shape=tuple(
            jax.ShapeDtypeStruct((rows, plan.part), jnp.bfloat16 if j else own_kind)
            for j in range(plan.dp)
        ),
        in_specs=[pl.BlockSpec(memory_space=pltpu.SMEM)] + [vmem] * len(parts),
        out_specs=(vmem,) * plan.dp,
    )(info, *parts)


def layout_kernel(plan, info, *refs):
    out_ref = refs[-1]
    for j in range(plan.dp):
        at = pl.ds(pl.multiple_of(info[plan.lanes_at + j], plan.part), plan.part)
        total = None
        for ref in refs[j : -1 : plan.dp]:
            piece = ref[...].astype(jnp.float32)
            total = piece if total is None else total + piece
        out_ref[:, at] = total


def layout_work(plan, info, pieces):
    rows = plan.head_dim // plan.dp
    vmem = pl.BlockSpec(memory_space=pltpu.VMEM)
    return pl.pallas_call(
        functools.partial(layout_kernel, plan),
        compiler_params=pltpu.CompilerParams(vmem_limit_bytes=6 * 1024 * 1024),
        out_shape=jax.ShapeDtypeStruct((rows, plan.part * plan.dp), jnp.float32),
        in_specs=[pl.BlockSpec(memory_space=pltpu.SMEM)] + [vmem] * len(pieces),
        out_specs=vmem,
    )(info, *pieces)


def merge_kernel(plan, *refs):
    parts, outs = refs[: plan.dp], refs[plan.dp :]
    length = plan.planes * plan.back
    for j, out in enumerate(outs):
        at = pl.ds(j * length, length)
        total = parts[0][at, :].astype(jnp.float32)
        for ref in parts[1:]:
            total = total + ref[at, :].astype(jnp.float32)
        out[...] = total.astype(out.dtype)


def merge_work(plan, parts):
    vmem = pl.BlockSpec(memory_space=pltpu.VMEM)
    rows = jax.ShapeDtypeStruct((plan.planes * plan.back, LANES), jnp.bfloat16)
    return pl.pallas_call(
        functools.partial(merge_kernel, plan),
        compiler_params=pltpu.CompilerParams(vmem_limit_bytes=6 * 1024 * 1024),
        out_shape=(rows,) * GROUP,
        in_specs=[vmem] * plan.dp,
        out_specs=(vmem,) * GROUP,
    )(*parts)


def target_kernel(plan, info, route_ref, out_ref):
    tokens, top = plan.tokens, plan.top
    count = tokens * top
    lane = lax.broadcasted_iota(jnp.int32, (tokens, LANES), 1)
    routes = route_ref[...]
    named = jnp.zeros((tokens, LANES), jnp.float32)
    listed = jnp.zeros((tokens, LANES), jnp.float32)
    for k in range(top):
        column = routes[:, k : k + 1]
        named = named + (column == lane).astype(jnp.float32)
        listed = listed + jnp.where(lane == k, column, 0).astype(jnp.float32)
    earlier = (
        lax.broadcasted_iota(jnp.int32, (tokens, tokens), 1)
        < lax.broadcasted_iota(jnp.int32, (tokens, tokens), 0)
    ).astype(jnp.bfloat16)
    places = jnp.dot(earlier, named.astype(jnp.bfloat16), preferred_element_type=jnp.float32)
    pair = lax.broadcasted_iota(jnp.int32, (count, LANES), 0)
    lane = lax.broadcasted_iota(jnp.int32, (count, LANES), 1)
    spread = (pair // top == lane).astype(jnp.bfloat16)
    route = jnp.dot(spread, listed.astype(jnp.bfloat16), preferred_element_type=jnp.float32)
    route = jnp.sum(jnp.where(lane == pair % top, route, 0.0), axis=1, keepdims=True)
    route = route.astype(jnp.int32)
    place = jnp.dot(spread, places.astype(jnp.bfloat16), preferred_element_type=jnp.float32)
    place = jnp.sum(jnp.where(lane == route, place, 0.0), axis=1, keepdims=True).astype(jnp.int32)
    slot = jnp.zeros_like(route)
    for j in range(plan.planes):
        slot = jnp.where(route // GROUP == info[plan.planes_at + j], j, slot)
    row = (route % GROUP) // 2 - info[plan.planes_at + plan.planes]
    row = jnp.where(row < 0, row + plan.rows, row)
    side = jnp.where(route % 2 == info[plan.planes_at + plan.planes + 1], 0, 1)
    base = ((side * plan.rows + row) * plan.planes + slot) * plan.back
    target = base + place
    gate_line = base + plan.cap
    out_ref[...] = jnp.where(lane == 0, target, jnp.where(lane == 1, gate_line, place))


def target_work(plan, info, route_ids):
    vmem = pl.BlockSpec(memory_space=pltpu.VMEM)
    return pl.pallas_call(
        functools.partial(target_kernel, plan),
        out_shape=jax.ShapeDtypeStruct((plan.tokens * plan.top, LANES), jnp.int32),
        in_specs=[pl.BlockSpec(memory_space=pltpu.SMEM), vmem],
        out_specs=vmem,
        compiler_params=pltpu.CompilerParams(vmem_limit_bytes=8 * 1024 * 1024),
    )(info, route_ids)


def final_kernel(plan, target_ref, *refs):
    head_ref, out_gate_ref = refs[GROUP:]
    length = plan.rows * plan.planes * plan.back
    table = jnp.concatenate([ref[...] for ref in refs[:GROUP]], axis=0)
    block = 256
    for start in range(0, plan.tokens * plan.top, block):
        at = pl.ds(start, block)
        slot_of = lax.broadcasted_iota(jnp.int32, (block, 2 * length), 1)
        hot = (slot_of == target_ref[at, 0:1]).astype(jnp.bfloat16)
        head_ref[at, :] = jnp.dot(hot, table, preferred_element_type=jnp.float32).astype(jnp.bfloat16)
        hot = (slot_of == target_ref[at, 1:2]).astype(jnp.bfloat16)
        lines = jnp.dot(hot, table, preferred_element_type=jnp.float32)
        lane_of = lax.broadcasted_iota(jnp.int32, (block, LANES), 1)
        out_gate_ref[at, :] = jnp.sum(
            jnp.where(lane_of == target_ref[at, 2:3], lines, 0.0), axis=1, keepdims=True
        )


def final_work(plan, target, tables):
    count = plan.tokens * plan.top
    vmem = pl.BlockSpec(memory_space=pltpu.VMEM)
    return pl.pallas_call(
        functools.partial(final_kernel, plan),
        cost_estimate=pl.CostEstimate(flops=1, bytes_accessed=1, transcendentals=0),
        out_shape=(
            jax.ShapeDtypeStruct((count, plan.head_dim), jnp.bfloat16),
            jax.ShapeDtypeStruct((count, 1), jnp.float32),
        ),
        in_specs=[vmem] * (1 + GROUP),
        out_specs=(vmem, vmem),
        compiler_params=pltpu.CompilerParams(vmem_limit_bytes=8 * 1024 * 1024),
    )(target, *tables)


def local(mesh, head_outputs, out_grad, gate_weights, route_ids, out_proj):
    tokens, top, head_dim = head_outputs.shape
    features = out_grad.shape[1]
    plan = Plan(mesh, tokens, top, head_dim, features)
    x = lax.axis_index("dp")
    me = lax.axis_index("expert")
    z, y, c = me // GROUP, (me % GROUP) // 2, me % 2

    if plan.planes == 4:
        inner = (z == 1) | (z == 2)
        mates, middle = [(0, 1), (1, 0), (2, 3), (3, 2)], [(1, 2), (2, 1)]
        outward, inward = [(1, 0), (2, 3)], [(0, 1), (3, 2)]
        across = [(1, 3), (2, 0)]
        plane_of = [jnp.where(z < 2, 2, 1), jnp.where(z < 2, 3, 0), z ^ 1, z]
        which = jnp.where(inner, 0, 1)
    else:
        steps = [k % plan.planes for k in range(1, plan.planes + 1)]
        plane_of = [(z + k) % plan.planes for k in steps]
        which = 0
    info = plan.info(x, z, y, c, plane_of, which)

    own_weights = lax.dynamic_slice_in_dim(out_proj[0], x * plan.part, plan.part, 1)
    target = target_work(plan, info, route_ids)
    if plan.planes == 4:
        mate = plan.along(own_weights, mates)
        near_in = plan.along(own_weights, middle)
        mate, near_in, target = lax.optimization_barrier((mate, near_in, target))
        near_out = plan.along(near_in, outward)
        far_in, near_out = lax.optimization_barrier((plan.along(mate, middle), near_out))
        far_out = plan.along(far_in, outward)
    else:
        weights = [[(plan.shift(own_weights, dz=-k % plan.planes), None)] for k in steps]

    meta = jnp.concatenate(
        [
            gate_weights.T,
            route_ids.T.astype(jnp.bfloat16),
            jnp.zeros((LANES - 2 * top, tokens), jnp.bfloat16),
        ],
        axis=0,
    )
    flat_heads = head_outputs.reshape(tokens, top * head_dim)
    packs = []
    for dx, dy in plan.chips():
        piece = lax.dynamic_slice_in_dim(out_grad, ((x + dx) % plan.dp) * plan.part, plan.part, 1)
        value = jnp.concatenate([piece, flat_heads, meta], axis=1)
        value = plan.shift(value, dx=dx, dy=dy)
        if plan.planes == 4:
            if dx or dy:
                value, far_in, near_out = lax.optimization_barrier((value, far_in, near_out))
            else:
                value, near_out = lax.optimization_barrier((value, near_out))
        packs += [value, plan.shift(value, dc=1)]

    if plan.planes == 4:
        weights = [
            [(near_in, 0), (near_out, 1)],
            [(far_in, 0), (far_out, 1)],
            [(mate, None)],
            [(own_weights, None)],
        ]

    sums, backs, done = [], [], target
    for j in range(plan.planes):
        last = j == plan.planes - 1
        if last and plan.planes == 4:
            near_sum = sums[0] + plan.along(sums[0], inward)
            done = (done, near_sum)
        info, done = lax.optimization_barrier((info, done))
        target = target if j else done
        kind = jnp.float32 if last else jnp.bfloat16
        part, *back = slot_work(plan, j, info, packs, weights[j], kind, backs if last else ())
        sums.append(part)
        backs = back if last else backs + back
        done = back[0]

    far_pieces = []
    if plan.planes == 4:
        far_part = plan.along(sums[1], inward)
        far_part, done = lax.optimization_barrier((far_part, done))
        far_sums = sum_work(plan, info, [sums[1], far_part], jnp.bfloat16)
        info, far_sums = lax.optimization_barrier((info, far_sums))
        far_pieces = [plan.along(piece, across, dx) for dx, piece in enumerate(far_sums)]
        received = [plan.along(sums[2], mates), plan.along(near_sum, middle)]
    else:
        received = [plan.shift(sums[j], dz=steps[j]) for j in range(plan.planes - 1)]
    pieces = sum_work(plan, info, [sums[-1]] + received, jnp.float32)
    pieces = [plan.shift(piece, dx=dx) for dx, piece in enumerate(pieces)]

    backs = [plan.shift(rows, dx=-dx % plan.dp) for dx, rows in enumerate(backs)]
    if plan.planes == 4:
        backs, far_sums = lax.optimization_barrier((backs, far_sums))
    merged = merge_work(plan, backs)
    tables = [
        plan.shift(merged[2 * dy + dc], dy=-dy % plan.rows)
        for dy in range(plan.rows)
        for dc in range(2)
    ]
    tables = tables[0::2] + [plan.shift(rows, dc=1) for rows in tables[1::2]]
    tables, far_pieces[1:] = lax.optimization_barrier((tables, far_pieces[1:]))
    grad_head, grad_gate = final_work(plan, target, tables)
    grad_proj = layout_work(plan, info, pieces + far_pieces)
    return (
        grad_head.reshape(tokens, top, head_dim),
        grad_gate.reshape(tokens, top).astype(jnp.bfloat16),
        grad_proj[None],
    )


def solution(mesh):
    return jax.shard_map(
        functools.partial(local, mesh),
        mesh=mesh,
        in_specs=(
            P(("dp", "expert"), None, None),
            P(("dp", "expert"), None),
            P(("dp", "expert"), None),
            P(("dp", "expert"), None),
            P("expert", None, None),
        ),
        out_specs=(
            P(("dp", "expert"), None, None),
            P(("dp", "expert"), None),
            P("expert", "dp", None),
        ),
        check_vma=False,
    )
```

```python
import functools

import jax
import jax.numpy as jnp
from jax import lax
from jax.experimental import pallas as pl
from jax.experimental.pallas import tpu as pltpu
from jax.sharding import PartitionSpec as P

soft_cap = 1.5
AXES = ("dp", "expert")
GROUP = 4
LANES = 128


class Plan:
    def __init__(self, mesh, tokens, top, head_dim, features):
        self.dp = mesh.shape["dp"]
        self.experts = mesh.shape["expert"]
        self.rows = GROUP // 2
        self.planes = self.experts // GROUP
        self.sources = self.dp * GROUP
        self.tokens, self.top, self.head_dim = tokens, top, head_dim
        self.part = features // self.dp
        self.own_rows = head_dim // self.dp
        cap = 9 * tokens * top // (8 * self.experts)
        self.cap = -(-cap // 8) * 8
        self.back = self.cap + 8
        self.width = self.part + top * head_dim + LANES

    def index(self, x, z, y, c):
        return x * self.experts + z * GROUP + y * 2 + c

    def pairs(self, dx=0, dz=0, dy=0, dc=0):
        out = []
        for x in range(self.dp):
            for z in range(self.planes):
                for y in range(self.rows):
                    for c in range(2):
                        target = self.index(
                            (x + dx) % self.dp,
                            (z + dz) % self.planes,
                            (y + dy) % self.rows,
                            c ^ dc,
                        )
                        out.append((self.index(x, z, y, c), target))
        return out

    def shift(self, value, **by):
        if not any(by.values()):
            return value
        return lax.ppermute(value, AXES, self.pairs(**by))

    def along(self, value, moves, dx=0, dy=0):
        out = []
        for x in range(self.dp):
            for a, b in moves:
                for y in range(self.rows):
                    for c in range(2):
                        target = self.index((x + dx) % self.dp, b, (y + dy) % self.rows, c)
                        out.append((self.index(x, a, y, c), target))
        return lax.ppermute(value, AXES, out)

    def info(self, x, z, y, c, plane_of, which):
        values = [((x + dx) % self.dp) * self.own_rows for dx in range(self.dp)]
        self.lanes_at = len(values)
        values += [((x - dx) % self.dp) * self.part for dx in range(self.dp)]
        self.which_at = len(values)
        values += [which]
        self.experts_at = len(values)
        values += [plane_of[j] * GROUP + y * 2 + c for j in range(self.planes)]
        self.planes_at = len(values)
        values += list(plane_of) + [y, c]
        return jnp.stack([jnp.asarray(value, jnp.int32) for value in values])

    def chips(self):
        return [(dx, dy) for dx in range(self.dp) for dy in range(self.rows)]


def slot_kernel(plan, index, where, earlier, info, *refs):
    packs, rest = refs[: plan.sources], refs[plan.sources :]
    weight_refs, rest = rest[: len(where)], rest[len(where) :]
    earlier_refs, rest = rest[:earlier], rest[earlier:]
    count = plan.dp if earlier else 1
    p_ref, back_refs, (grads, heads, weights) = rest[0], rest[1 : 1 + count], rest[1 + count :]
    tokens, cap, part, top, head_dim = plan.tokens, plan.cap, plan.part, plan.top, plan.head_dim
    pair_rows = 2 * cap
    pair_total = plan.sources // 2
    length = plan.planes * plan.back

    def put(s, slot, at, value):
        if earlier:
            start = (s % GROUP) * length + slot * plan.back + at
            back_refs[s // GROUP][pl.ds(start, value.shape[0]), :] = value
        else:
            back_refs[0][s, pl.ds(at, value.shape[0]), :] = value

    if len(where) > 1:
        for ref, kind in zip(weight_refs, where):

            @pl.when(info[plan.which_at] == kind)
            def _():
                weights[...] = ref[...]

        weight_ref = weights
    else:
        weight_ref = weight_refs[0]
    expert = info[plan.experts_at + index].astype(jnp.float32)
    row_of = lax.broadcasted_iota(jnp.int32, (cap, tokens), 0)
    diagonal = (row_of == lax.broadcasted_iota(jnp.int32, (cap, tokens), 1)).astype(jnp.float32)
    before = (
        lax.broadcasted_iota(jnp.int32, (tokens, tokens), 0)
        < lax.broadcasted_iota(jnp.int32, (tokens, tokens), 1)
    ).astype(jnp.bfloat16)
    block_row = lax.broadcasted_iota(jnp.int32, (8, LANES), 0)
    empty = jnp.zeros((cap, tokens), jnp.bfloat16)
    chunk = min(part, 512)

    masks, occupied, gate_rows = [], [], []
    for s in range(plan.sources):
        meta = packs[s][pl.ds(0, 2 * top), pl.ds(part + top * head_dim, LANES)].astype(jnp.float32)
        mask = (meta[top:] == expert).astype(jnp.float32)
        masks.append(mask)
        occupied.append(jnp.sum(mask, axis=0, keepdims=True))
        gate_rows.append(jnp.sum(mask * meta[:top], axis=0, keepdims=True))
    filled = occupied + [jnp.zeros((1, tokens), jnp.float32)] * (-plan.sources % 16)
    places = jnp.dot(
        jnp.concatenate(filled, axis=0).astype(jnp.bfloat16),
        before,
        preferred_element_type=jnp.float32,
    ).astype(jnp.int32)
    for q in range(pair_total):
        hots, gates = [], []
        for b in range(2):
            s = 2 * q + b
            hot = jnp.where(row_of == places[s : s + 1], occupied[s], 0.0)
            gates.append(jnp.sum(hot * gate_rows[s], axis=1, keepdims=True))
            hots.append(hot.astype(jnp.bfloat16))
            wide = jnp.concatenate(
                [(hot * masks[s][k : k + 1]).astype(jnp.bfloat16) for k in range(top)], axis=1
            )
            raw = jnp.concatenate(
                [packs[s][:, pl.ds(part + k * head_dim, head_dim)] for k in range(top)], axis=0
            )
            heads[pl.ds(s * cap, cap), :] = jnp.dot(
                wide, raw, preferred_element_type=jnp.float32
            ).astype(jnp.bfloat16)
        all_hots = jnp.concatenate(
            [
                jnp.concatenate([hots[0], empty], axis=1),
                jnp.concatenate([empty, hots[1]], axis=1),
            ],
            axis=0,
        )
        gate = jnp.broadcast_to(jnp.concatenate(gates, axis=0), (pair_rows, LANES))
        total = jnp.zeros((pair_rows, LANES), jnp.float32)
        rows_at = pl.ds(q * pair_rows, pair_rows)
        for start in range(0, part, chunk):
            both = jnp.concatenate(
                [packs[2 * q + b][:, pl.ds(start, chunk)] for b in range(2)], axis=0
            )
            grad = jnp.dot(all_hots, both, preferred_element_type=jnp.float32)
            pre = jnp.dot(
                heads[rows_at, :], weight_ref[:, pl.ds(start, chunk)], preferred_element_type=jnp.float32
            )
            for lane in range(0, chunk, LANES):
                grad_block = grad[:, lane : lane + LANES]
                capped = jnp.tanh(pre[:, lane : lane + LANES] * (1.0 / soft_cap))
                total = total + grad_block * capped
                grads[rows_at, pl.ds(start + lane, LANES)] = (
                    gate * grad_block * (1.0 - capped * capped)
                ).astype(jnp.bfloat16)
        for b in range(2):
            column = jnp.sum(total[b * cap : (b + 1) * cap], axis=1, keepdims=True) * soft_cap
            line = jnp.sum(diagonal * column, axis=0, keepdims=True)
            block = jnp.where(block_row == 0, line, 0.0).astype(jnp.bfloat16)
            put(2 * q + b, plan.planes - 1, cap, block)
    grad_all = grads[...]
    p_ref[...] = lax.dot_general(
        heads[...], grad_all, (((0,), (0,)), ((), ())), preferred_element_type=jnp.float32
    ).astype(p_ref.dtype)
    rows = lax.dot_general(
        grad_all, weight_ref[...], (((1,), (1,)), ((), ())), preferred_element_type=jnp.float32
    ).astype(jnp.bfloat16)
    for s in range(plan.sources):
        put(s, plan.planes - 1, 0, rows[s * cap : (s + 1) * cap])
    for j, ref in enumerate(earlier_refs):
        for s in range(plan.sources):
            put(s, j, 0, ref[s])


def slot_work(plan, index, info, packs, weights, kind, earlier=()):
    rows = plan.sources * plan.cap
    if earlier:
        backs = (
            jax.ShapeDtypeStruct((GROUP * plan.planes * plan.back, LANES), jnp.bfloat16),
        ) * plan.dp
    else:
        backs = (jax.ShapeDtypeStruct((plan.sources, plan.back, LANES), jnp.bfloat16),)
    vmem = pl.BlockSpec(memory_space=pltpu.VMEM)
    return pl.pallas_call(
        functools.partial(slot_kernel, plan, index, [where for _, where in weights], len(earlier)),
        out_shape=(jax.ShapeDtypeStruct((plan.head_dim, plan.part), kind), *backs),
        in_specs=[pl.BlockSpec(memory_space=pltpu.SMEM)]
        + [vmem] * (plan.sources + len(weights) + len(earlier)),
        out_specs=(vmem,) * (1 + len(backs)),
        scratch_shapes=[
            pltpu.VMEM((rows, plan.part), jnp.bfloat16),
            pltpu.VMEM((rows, plan.head_dim), jnp.bfloat16),
            pltpu.VMEM((plan.head_dim, plan.part), jnp.bfloat16),
        ],
        compiler_params=pltpu.CompilerParams(vmem_limit_bytes=14 * 1024 * 1024),
    )(info, *packs, *[array for array, _ in weights], *earlier)


def sum_kernel(plan, info, *refs):
    parts, pieces = refs[: len(refs) - plan.dp], refs[len(refs) - plan.dp :]
    rows = plan.own_rows
    for j, piece in enumerate(pieces):
        at = pl.ds(pl.multiple_of(info[j], rows), rows)
        total = parts[0][at, :].astype(jnp.float32)
        for ref in parts[1:]:
            total = total + ref[at, :].astype(jnp.float32)
        piece[...] = total.astype(piece.dtype)


def sum_work(plan, info, parts, own_kind):
    rows = plan.head_dim // plan.dp
    vmem = pl.BlockSpec(memory_space=pltpu.VMEM)
    return pl.pallas_call(
        functools.partial(sum_kernel, plan),
        compiler_params=pltpu.CompilerParams(vmem_limit_bytes=6 * 1024 * 1024),
        out_shape=tuple(
            jax.ShapeDtypeStruct((rows, plan.part), jnp.bfloat16 if j else own_kind)
            for j in range(plan.dp)
        ),
        in_specs=[pl.BlockSpec(memory_space=pltpu.SMEM)] + [vmem] * len(parts),
        out_specs=(vmem,) * plan.dp,
    )(info, *parts)


def layout_kernel(plan, info, *refs):
    out_ref = refs[-1]
    for j in range(plan.dp):
        at = pl.ds(pl.multiple_of(info[plan.lanes_at + j], plan.part), plan.part)
        total = None
        for ref in refs[j : -1 : plan.dp]:
            piece = ref[...].astype(jnp.float32)
            total = piece if total is None else total + piece
        out_ref[:, at] = total


def layout_work(plan, info, pieces):
    rows = plan.head_dim // plan.dp
    vmem = pl.BlockSpec(memory_space=pltpu.VMEM)
    return pl.pallas_call(
        functools.partial(layout_kernel, plan),
        compiler_params=pltpu.CompilerParams(vmem_limit_bytes=6 * 1024 * 1024),
        out_shape=jax.ShapeDtypeStruct((rows, plan.part * plan.dp), jnp.float32),
        in_specs=[pl.BlockSpec(memory_space=pltpu.SMEM)] + [vmem] * len(pieces),
        out_specs=vmem,
    )(info, *pieces)


def merge_kernel(plan, *refs):
    parts, outs = refs[: plan.dp], refs[plan.dp :]
    length = 2 * plan.planes * plan.back
    for dy, out in enumerate(outs):
        at = pl.ds(dy * length, length)
        total = parts[0][at, :].astype(jnp.float32)
        for ref in parts[1:]:
            total = total + ref[at, :].astype(jnp.float32)
        out[...] = total.astype(out.dtype)


def merge_work(plan, parts):
    vmem = pl.BlockSpec(memory_space=pltpu.VMEM)
    rows = jax.ShapeDtypeStruct((2 * plan.planes * plan.back, LANES), jnp.bfloat16)
    return pl.pallas_call(
        functools.partial(merge_kernel, plan),
        compiler_params=pltpu.CompilerParams(vmem_limit_bytes=6 * 1024 * 1024),
        out_shape=(rows,) * plan.rows,
        in_specs=[vmem] * plan.dp,
        out_specs=(vmem,) * plan.rows,
    )(*parts)


def target_kernel(plan, info, route_ref, out_ref):
    tokens, top = plan.tokens, plan.top
    count = tokens * top
    lane = lax.broadcasted_iota(jnp.int32, (tokens, LANES), 1)
    routes = route_ref[...]
    named = jnp.zeros((tokens, LANES), jnp.float32)
    listed = jnp.zeros((tokens, LANES), jnp.float32)
    for k in range(top):
        column = routes[:, k : k + 1]
        named = named + (column == lane).astype(jnp.float32)
        listed = listed + jnp.where(lane == k, column, 0).astype(jnp.float32)
    earlier = (
        lax.broadcasted_iota(jnp.int32, (tokens, tokens), 1)
        < lax.broadcasted_iota(jnp.int32, (tokens, tokens), 0)
    ).astype(jnp.bfloat16)
    places = jnp.dot(earlier, named.astype(jnp.bfloat16), preferred_element_type=jnp.float32)
    pair = lax.broadcasted_iota(jnp.int32, (count, LANES), 0)
    lane = lax.broadcasted_iota(jnp.int32, (count, LANES), 1)
    spread = (pair // top == lane).astype(jnp.bfloat16)
    route = jnp.dot(spread, listed.astype(jnp.bfloat16), preferred_element_type=jnp.float32)
    route = jnp.sum(jnp.where(lane == pair % top, route, 0.0), axis=1, keepdims=True)
    route = route.astype(jnp.int32)
    place = jnp.dot(spread, places.astype(jnp.bfloat16), preferred_element_type=jnp.float32)
    place = jnp.sum(jnp.where(lane == route, place, 0.0), axis=1, keepdims=True).astype(jnp.int32)
    slot = jnp.zeros_like(route)
    for j in range(plan.planes):
        slot = jnp.where(route // GROUP == info[plan.planes_at + j], j, slot)
    row = (route % GROUP) // 2 - info[plan.planes_at + plan.planes]
    row = jnp.where(row < 0, row + plan.rows, row)
    side = jnp.where(route % 2 == info[plan.planes_at + plan.planes + 1], 0, 1)
    base = ((side * plan.rows + row) * plan.planes + slot) * plan.back
    target = base + place
    gate_line = base + plan.cap
    out_ref[...] = jnp.where(lane == 0, target, jnp.where(lane == 1, gate_line, place))


def target_work(plan, info, route_ids):
    vmem = pl.BlockSpec(memory_space=pltpu.VMEM)
    return pl.pallas_call(
        functools.partial(target_kernel, plan),
        out_shape=jax.ShapeDtypeStruct((plan.tokens * plan.top, LANES), jnp.int32),
        in_specs=[pl.BlockSpec(memory_space=pltpu.SMEM), vmem],
        out_specs=vmem,
        compiler_params=pltpu.CompilerParams(vmem_limit_bytes=8 * 1024 * 1024),
    )(info, route_ids)


def final_kernel(plan, target_ref, *refs):
    tables, (head_ref, out_gate_ref) = refs[:GROUP], refs[GROUP:]
    length = plan.rows * plan.planes * plan.back
    part = plan.planes * plan.back
    table = jnp.concatenate(
        [ref[pl.ds(0, part), :] for ref in tables[: plan.rows]]
        + [ref[pl.ds(part, part), :] for ref in tables[plan.rows :]],
        axis=0,
    )
    block = 256
    for start in range(0, plan.tokens * plan.top, block):
        at = pl.ds(start, block)
        slot_of = lax.broadcasted_iota(jnp.int32, (block, 2 * length), 1)
        hot = (slot_of == target_ref[at, 0:1]).astype(jnp.bfloat16)
        head_ref[at, :] = jnp.dot(hot, table, preferred_element_type=jnp.float32).astype(jnp.bfloat16)
        hot = (slot_of == target_ref[at, 1:2]).astype(jnp.bfloat16)
        lines = jnp.dot(hot, table, preferred_element_type=jnp.float32)
        lane_of = lax.broadcasted_iota(jnp.int32, (block, LANES), 1)
        out_gate_ref[at, :] = jnp.sum(
            jnp.where(lane_of == target_ref[at, 2:3], lines, 0.0), axis=1, keepdims=True
        )


def final_work(plan, target, tables):
    count = plan.tokens * plan.top
    vmem = pl.BlockSpec(memory_space=pltpu.VMEM)
    return pl.pallas_call(
        functools.partial(final_kernel, plan),
        cost_estimate=pl.CostEstimate(flops=1, bytes_accessed=1, transcendentals=0),
        out_shape=(
            jax.ShapeDtypeStruct((count, plan.head_dim), jnp.bfloat16),
            jax.ShapeDtypeStruct((count, 1), jnp.float32),
        ),
        in_specs=[vmem] * (1 + GROUP),
        out_specs=(vmem, vmem),
        compiler_params=pltpu.CompilerParams(vmem_limit_bytes=8 * 1024 * 1024),
    )(target, *tables)


def local(mesh, head_outputs, out_grad, gate_weights, route_ids, out_proj):
    tokens, top, head_dim = head_outputs.shape
    features = out_grad.shape[1]
    plan = Plan(mesh, tokens, top, head_dim, features)
    x = lax.axis_index("dp")
    me = lax.axis_index("expert")
    z, y, c = me // GROUP, (me % GROUP) // 2, me % 2

    if plan.planes == 4:
        inner = (z == 1) | (z == 2)
        mates, middle = [(0, 1), (1, 0), (2, 3), (3, 2)], [(1, 2), (2, 1)]
        outward, inward = [(1, 0), (2, 3)], [(0, 1), (3, 2)]
        across = [(1, 3), (2, 0)]
        plane_of = [jnp.where(z < 2, 2, 1), jnp.where(z < 2, 3, 0), z ^ 1, z]
        which = jnp.where(inner, 0, 1)
    else:
        steps = [k % plan.planes for k in range(1, plan.planes + 1)]
        plane_of = [(z + k) % plan.planes for k in steps]
        which = 0
    info = plan.info(x, z, y, c, plane_of, which)

    own_weights = lax.dynamic_slice_in_dim(out_proj[0], x * plan.part, plan.part, 1)
    target = target_work(plan, info, route_ids)
    if plan.planes == 4:
        mate = plan.along(own_weights, mates)
        near_in = plan.along(own_weights, middle)
        mate, near_in, target = lax.optimization_barrier((mate, near_in, target))
        near_out = plan.along(near_in, outward)
        far_in, near_out = lax.optimization_barrier((plan.along(mate, middle), near_out))
        far_out = plan.along(far_in, outward)
    else:
        weights = [[(plan.shift(own_weights, dz=-k % plan.planes), None)] for k in steps]

    meta = jnp.concatenate(
        [
            gate_weights.T,
            route_ids.T.astype(jnp.bfloat16),
            jnp.zeros((LANES - 2 * top, tokens), jnp.bfloat16),
        ],
        axis=0,
    )
    flat_heads = head_outputs.reshape(tokens, top * head_dim)
    packs = []
    for dx, dy in plan.chips():
        piece = lax.dynamic_slice_in_dim(out_grad, ((x + dx) % plan.dp) * plan.part, plan.part, 1)
        value = jnp.concatenate([piece, flat_heads, meta], axis=1)
        value = plan.shift(value, dx=dx, dy=dy)
        if plan.planes == 4:
            if dx or dy:
                value, far_in, near_out = lax.optimization_barrier((value, far_in, near_out))
            else:
                value, near_out = lax.optimization_barrier((value, near_out))
        packs += [value, plan.shift(value, dc=1)]

    if plan.planes == 4:
        weights = [
            [(near_in, 0), (near_out, 1)],
            [(far_in, 0), (far_out, 1)],
            [(mate, None)],
            [(own_weights, None)],
        ]

    sums, backs, done = [], [], target
    for j in range(plan.planes):
        last = j == plan.planes - 1
        if last and plan.planes == 4:
            near_sum = sums[0] + plan.along(sums[0], inward)
            done = (done, near_sum)
        info, done = lax.optimization_barrier((info, done))
        target = target if j else done
        kind = jnp.float32 if last else jnp.bfloat16
        part, *back = slot_work(plan, j, info, packs, weights[j], kind, backs if last else ())
        sums.append(part)
        backs = back if last else backs + back
        done = back[0]

    far_pieces = []
    if plan.planes == 4:
        far_part = plan.along(sums[1], inward)
        far_part, done = lax.optimization_barrier((far_part, done))
        far_sums = sum_work(plan, info, [sums[1], far_part], jnp.bfloat16)
        info, far_sums = lax.optimization_barrier((info, far_sums))
        far_pieces = [plan.along(piece, across, dx) for dx, piece in enumerate(far_sums)]
        received = [plan.along(sums[2], mates), plan.along(near_sum, middle)]
    else:
        received = [plan.shift(sums[j], dz=steps[j]) for j in range(plan.planes - 1)]
    pieces = sum_work(plan, info, [sums[-1]] + received, jnp.float32)
    pieces = [plan.shift(piece, dx=dx) for dx, piece in enumerate(pieces)]

    backs = [plan.shift(rows, dx=-dx % plan.dp) for dx, rows in enumerate(backs)]
    if plan.planes == 4:
        backs, far_sums = lax.optimization_barrier((backs, far_sums))
    merged = merge_work(plan, backs)
    tables = [plan.shift(rows, dy=-dy % plan.rows) for dy, rows in enumerate(merged)]
    tables = tables + [plan.shift(rows, dc=1) for rows in tables]
    tables, far_pieces[1:] = lax.optimization_barrier((tables, far_pieces[1:]))
    grad_head, grad_gate = final_work(plan, target, tables)
    grad_proj = layout_work(plan, info, pieces + far_pieces)
    return (
        grad_head.reshape(tokens, top, head_dim),
        grad_gate.reshape(tokens, top).astype(jnp.bfloat16),
        grad_proj[None],
    )


def solution(mesh):
    return jax.shard_map(
        functools.partial(local, mesh),
        mesh=mesh,
        in_specs=(
            P(("dp", "expert"), None, None),
            P(("dp", "expert"), None),
            P(("dp", "expert"), None),
            P(("dp", "expert"), None),
            P("expert", None, None),
        ),
        out_specs=(
            P(("dp", "expert"), None, None),
            P(("dp", "expert"), None),
            P("expert", "dp", None),
        ),
        check_vma=False,
    )
```

```python
import functools

import jax
import jax.numpy as jnp
from jax import lax
from jax.experimental import pallas as pl
from jax.experimental.pallas import tpu as pltpu
from jax.sharding import PartitionSpec as P

soft_cap = 1.5
AXES = ("dp", "expert")
GROUP = 4
LANES = 128


class Plan:
    def __init__(self, mesh, tokens, top, head_dim, features):
        self.dp = mesh.shape["dp"]
        self.experts = mesh.shape["expert"]
        self.rows = GROUP // 2
        self.planes = self.experts // GROUP
        self.sources = self.dp * GROUP
        self.tokens, self.top, self.head_dim = tokens, top, head_dim
        self.part = features // self.dp
        self.own_rows = head_dim // self.dp
        cap = 9 * tokens * top // (8 * self.experts)
        self.cap = -(-cap // 8) * 8
        self.back = self.cap + 8
        self.width = self.part + top * head_dim + LANES

    def index(self, x, z, y, c):
        return x * self.experts + z * GROUP + y * 2 + c

    def pairs(self, dx=0, dz=0, dy=0, dc=0):
        out = []
        for x in range(self.dp):
            for z in range(self.planes):
                for y in range(self.rows):
                    for c in range(2):
                        target = self.index(
                            (x + dx) % self.dp,
                            (z + dz) % self.planes,
                            (y + dy) % self.rows,
                            c ^ dc,
                        )
                        out.append((self.index(x, z, y, c), target))
        return out

    def shift(self, value, **by):
        if not any(by.values()):
            return value
        return lax.ppermute(value, AXES, self.pairs(**by))

    def along(self, value, moves, dx=0, dy=0):
        out = []
        for x in range(self.dp):
            for a, b in moves:
                for y in range(self.rows):
                    for c in range(2):
                        target = self.index((x + dx) % self.dp, b, (y + dy) % self.rows, c)
                        out.append((self.index(x, a, y, c), target))
        return lax.ppermute(value, AXES, out)

    def info(self, x, z, y, c, plane_of, which):
        values = [((x + dx) % self.dp) * self.own_rows for dx in range(self.dp)]
        self.lanes_at = len(values)
        values += [((x - dx) % self.dp) * self.part for dx in range(self.dp)]
        self.which_at = len(values)
        values += [which]
        self.experts_at = len(values)
        values += [plane_of[j] * GROUP + y * 2 + c for j in range(self.planes)]
        self.planes_at = len(values)
        values += list(plane_of) + [y, c]
        return jnp.stack([jnp.asarray(value, jnp.int32) for value in values])

    def chips(self):
        return [(dx, dy) for dx in range(self.dp) for dy in range(self.rows)]


def slot_kernel(plan, index, where, earlier, info, *refs):
    packs, rest = refs[: plan.sources], refs[plan.sources :]
    weight_refs, rest = rest[: len(where)], rest[len(where) :]
    earlier_refs, rest = rest[:earlier], rest[earlier:]
    count = plan.dp if earlier else 1
    p_ref, back_refs, (grads, heads, weights) = rest[0], rest[1 : 1 + count], rest[1 + count :]
    tokens, cap, part, top, head_dim = plan.tokens, plan.cap, plan.part, plan.top, plan.head_dim
    pair_rows = 2 * cap
    pair_total = plan.sources // 2
    length = plan.planes * plan.back

    def put(s, slot, at, value):
        if earlier:
            start = (s % GROUP) * length + slot * plan.back + at
            back_refs[s // GROUP][pl.ds(start, value.shape[0]), :] = value
        else:
            back_refs[0][s, pl.ds(at, value.shape[0]), :] = value

    if len(where) > 1:
        for ref, kind in zip(weight_refs, where):

            @pl.when(info[plan.which_at] == kind)
            def _():
                weights[...] = ref[...]

        weight_ref = weights
    else:
        weight_ref = weight_refs[0]
    expert = info[plan.experts_at + index].astype(jnp.float32)
    row_of = lax.broadcasted_iota(jnp.int32, (cap, tokens), 0)
    diagonal = (row_of == lax.broadcasted_iota(jnp.int32, (cap, tokens), 1)).astype(jnp.float32)
    before = (
        lax.broadcasted_iota(jnp.int32, (tokens, tokens), 0)
        < lax.broadcasted_iota(jnp.int32, (tokens, tokens), 1)
    ).astype(jnp.bfloat16)
    block_row = lax.broadcasted_iota(jnp.int32, (8, LANES), 0)
    empty = jnp.zeros((cap, tokens), jnp.bfloat16)
    chunk = min(part, 512)

    masks, occupied, gate_rows = [], [], []
    for s in range(plan.sources):
        meta = packs[s][pl.ds(0, 2 * top), pl.ds(part + top * head_dim, LANES)].astype(jnp.float32)
        mask = (meta[top:] == expert).astype(jnp.float32)
        masks.append(mask)
        occupied.append(jnp.sum(mask, axis=0, keepdims=True))
        gate_rows.append(jnp.sum(mask * meta[:top], axis=0, keepdims=True))
    filled = occupied + [jnp.zeros((1, tokens), jnp.float32)] * (-plan.sources % 16)
    places = jnp.dot(
        jnp.concatenate(filled, axis=0).astype(jnp.bfloat16),
        before,
        preferred_element_type=jnp.float32,
    ).astype(jnp.int32)
    for q in range(pair_total):
        hots, gates = [], []
        for b in range(2):
            s = 2 * q + b
            hot = jnp.where(row_of == places[s : s + 1], occupied[s], 0.0)
            gates.append(jnp.sum(hot * gate_rows[s], axis=1, keepdims=True))
            hots.append(hot.astype(jnp.bfloat16))
            wide = jnp.concatenate(
                [(hot * masks[s][k : k + 1]).astype(jnp.bfloat16) for k in range(top)], axis=1
            )
            raw = jnp.concatenate(
                [packs[s][:, pl.ds(part + k * head_dim, head_dim)] for k in range(top)], axis=0
            )
            heads[pl.ds(s * cap, cap), :] = jnp.dot(
                wide, raw, preferred_element_type=jnp.float32
            ).astype(jnp.bfloat16)
        all_hots = jnp.concatenate(
            [
                jnp.concatenate([hots[0], empty], axis=1),
                jnp.concatenate([empty, hots[1]], axis=1),
            ],
            axis=0,
        )
        gate = jnp.broadcast_to(jnp.concatenate(gates, axis=0), (pair_rows, LANES))
        total = jnp.zeros((pair_rows, LANES), jnp.float32)
        rows_at = pl.ds(q * pair_rows, pair_rows)
        for start in range(0, part, chunk):
            both = jnp.concatenate(
                [packs[2 * q + b][:, pl.ds(start, chunk)] for b in range(2)], axis=0
            )
            grad = jnp.dot(all_hots, both, preferred_element_type=jnp.float32)
            pre = jnp.dot(
                heads[rows_at, :], weight_ref[:, pl.ds(start, chunk)], preferred_element_type=jnp.float32
            )
            for lane in range(0, chunk, LANES):
                grad_block = grad[:, lane : lane + LANES]
                capped = jnp.tanh(pre[:, lane : lane + LANES] * (1.0 / soft_cap))
                total = total + grad_block * capped
                grads[rows_at, pl.ds(start + lane, LANES)] = (
                    gate * grad_block * (1.0 - capped * capped)
                ).astype(jnp.bfloat16)
        for b in range(2):
            column = jnp.sum(total[b * cap : (b + 1) * cap], axis=1, keepdims=True) * soft_cap
            line = jnp.sum(diagonal * column, axis=0, keepdims=True)
            block = jnp.where(block_row == 0, line, 0.0).astype(jnp.bfloat16)
            put(2 * q + b, plan.planes - 1, cap, block)
    grad_all = grads[...]
    p_ref[...] = lax.dot_general(
        heads[...], grad_all, (((0,), (0,)), ((), ())), preferred_element_type=jnp.float32
    ).astype(p_ref.dtype)
    rows = lax.dot_general(
        grad_all, weight_ref[...], (((1,), (1,)), ((), ())), preferred_element_type=jnp.float32
    ).astype(jnp.bfloat16)
    for s in range(plan.sources):
        put(s, plan.planes - 1, 0, rows[s * cap : (s + 1) * cap])
    for j, ref in enumerate(earlier_refs):
        for s in range(plan.sources):
            put(s, j, 0, ref[s])


def slot_work(plan, index, info, packs, weights, kind, earlier=()):
    rows = plan.sources * plan.cap
    if earlier:
        backs = (
            jax.ShapeDtypeStruct((GROUP * plan.planes * plan.back, LANES), jnp.bfloat16),
        ) * plan.dp
    else:
        backs = (jax.ShapeDtypeStruct((plan.sources, plan.back, LANES), jnp.bfloat16),)
    vmem = pl.BlockSpec(memory_space=pltpu.VMEM)
    return pl.pallas_call(
        functools.partial(slot_kernel, plan, index, [where for _, where in weights], len(earlier)),
        out_shape=(jax.ShapeDtypeStruct((plan.head_dim, plan.part), kind), *backs),
        in_specs=[pl.BlockSpec(memory_space=pltpu.SMEM)]
        + [vmem] * (plan.sources + len(weights) + len(earlier)),
        out_specs=(vmem,) * (1 + len(backs)),
        scratch_shapes=[
            pltpu.VMEM((rows, plan.part), jnp.bfloat16),
            pltpu.VMEM((rows, plan.head_dim), jnp.bfloat16),
            pltpu.VMEM((plan.head_dim, plan.part), jnp.bfloat16),
        ],
        compiler_params=pltpu.CompilerParams(vmem_limit_bytes=14 * 1024 * 1024),
    )(info, *packs, *[array for array, _ in weights], *earlier)


def sum_kernel(plan, info, *refs):
    parts, pieces = refs[: len(refs) - plan.dp], refs[len(refs) - plan.dp :]
    rows = plan.own_rows
    for j, piece in enumerate(pieces):
        at = pl.ds(pl.multiple_of(info[j], rows), rows)
        total = parts[0][at, :].astype(jnp.float32)
        for ref in parts[1:]:
            total = total + ref[at, :].astype(jnp.float32)
        piece[...] = total.astype(piece.dtype)


def sum_work(plan, info, parts, own_kind):
    rows = plan.head_dim // plan.dp
    vmem = pl.BlockSpec(memory_space=pltpu.VMEM)
    return pl.pallas_call(
        functools.partial(sum_kernel, plan),
        compiler_params=pltpu.CompilerParams(vmem_limit_bytes=6 * 1024 * 1024),
        out_shape=tuple(
            jax.ShapeDtypeStruct((rows, plan.part), jnp.bfloat16 if j else own_kind)
            for j in range(plan.dp)
        ),
        in_specs=[pl.BlockSpec(memory_space=pltpu.SMEM)] + [vmem] * len(parts),
        out_specs=(vmem,) * plan.dp,
    )(info, *parts)


def layout_kernel(plan, info, *refs):
    out_ref = refs[-1]
    for j in range(plan.dp):
        at = pl.ds(pl.multiple_of(info[plan.lanes_at + j], plan.part), plan.part)
        total = None
        for ref in refs[j : -1 : plan.dp]:
            piece = ref[...].astype(jnp.float32)
            total = piece if total is None else total + piece
        out_ref[:, at] = total


def layout_work(plan, info, pieces):
    rows = plan.head_dim // plan.dp
    vmem = pl.BlockSpec(memory_space=pltpu.VMEM)
    return pl.pallas_call(
        functools.partial(layout_kernel, plan),
        compiler_params=pltpu.CompilerParams(vmem_limit_bytes=6 * 1024 * 1024),
        out_shape=jax.ShapeDtypeStruct((rows, plan.part * plan.dp), jnp.float32),
        in_specs=[pl.BlockSpec(memory_space=pltpu.SMEM)] + [vmem] * len(pieces),
        out_specs=vmem,
    )(info, *pieces)


def merge_kernel(plan, *refs):
    parts, outs = refs[: plan.dp], refs[plan.dp :]
    length = plan.planes * plan.back
    for j, out in enumerate(outs):
        at = pl.ds(j * length, length)
        total = parts[0][at, :].astype(jnp.float32)
        for ref in parts[1:]:
            total = total + ref[at, :].astype(jnp.float32)
        out[...] = total.astype(out.dtype)


def merge_work(plan, parts):
    vmem = pl.BlockSpec(memory_space=pltpu.VMEM)
    rows = jax.ShapeDtypeStruct((plan.planes * plan.back, LANES), jnp.bfloat16)
    return pl.pallas_call(
        functools.partial(merge_kernel, plan),
        compiler_params=pltpu.CompilerParams(vmem_limit_bytes=6 * 1024 * 1024),
        out_shape=(rows,) * GROUP,
        in_specs=[vmem] * plan.dp,
        out_specs=(vmem,) * GROUP,
    )(*parts)


def target_kernel(plan, info, route_ref, out_ref):
    tokens, top = plan.tokens, plan.top
    count = tokens * top
    lane = lax.broadcasted_iota(jnp.int32, (tokens, LANES), 1)
    routes = route_ref[...]
    named = jnp.zeros((tokens, LANES), jnp.float32)
    listed = jnp.zeros((tokens, LANES), jnp.float32)
    for k in range(top):
        column = routes[:, k : k + 1]
        named = named + (column == lane).astype(jnp.float32)
        listed = listed + jnp.where(lane == k, column, 0).astype(jnp.float32)
    earlier = (
        lax.broadcasted_iota(jnp.int32, (tokens, tokens), 1)
        < lax.broadcasted_iota(jnp.int32, (tokens, tokens), 0)
    ).astype(jnp.bfloat16)
    places = jnp.dot(earlier, named.astype(jnp.bfloat16), preferred_element_type=jnp.float32)
    pair = lax.broadcasted_iota(jnp.int32, (count, LANES), 0)
    lane = lax.broadcasted_iota(jnp.int32, (count, LANES), 1)
    spread = (pair // top == lane).astype(jnp.bfloat16)
    route = jnp.dot(spread, listed.astype(jnp.bfloat16), preferred_element_type=jnp.float32)
    route = jnp.sum(jnp.where(lane == pair % top, route, 0.0), axis=1, keepdims=True)
    route = route.astype(jnp.int32)
    place = jnp.dot(spread, places.astype(jnp.bfloat16), preferred_element_type=jnp.float32)
    place = jnp.sum(jnp.where(lane == route, place, 0.0), axis=1, keepdims=True).astype(jnp.int32)
    slot = jnp.zeros_like(route)
    for j in range(plan.planes):
        slot = jnp.where(route // GROUP == info[plan.planes_at + j], j, slot)
    row = (route % GROUP) // 2 - info[plan.planes_at + plan.planes]
    row = jnp.where(row < 0, row + plan.rows, row)
    side = jnp.where(route % 2 == info[plan.planes_at + plan.planes + 1], 0, 1)
    base = ((side * plan.rows + row) * plan.planes + slot) * plan.back
    target = base + place
    gate_line = base + plan.cap
    out_ref[...] = jnp.where(lane == 0, target, jnp.where(lane == 1, gate_line, place))


def target_work(plan, info, route_ids):
    vmem = pl.BlockSpec(memory_space=pltpu.VMEM)
    return pl.pallas_call(
        functools.partial(target_kernel, plan),
        out_shape=jax.ShapeDtypeStruct((plan.tokens * plan.top, LANES), jnp.int32),
        in_specs=[pl.BlockSpec(memory_space=pltpu.SMEM), vmem],
        out_specs=vmem,
        compiler_params=pltpu.CompilerParams(vmem_limit_bytes=8 * 1024 * 1024),
    )(info, route_ids)


def final_kernel(plan, target_ref, *refs):
    head_ref, out_gate_ref = refs[GROUP:]
    length = plan.rows * plan.planes * plan.back
    table = jnp.concatenate([ref[...] for ref in refs[:GROUP]], axis=0)
    block = 256
    for start in range(0, plan.tokens * plan.top, block):
        at = pl.ds(start, block)
        slot_of = lax.broadcasted_iota(jnp.int32, (block, 2 * length), 1)
        hot = (slot_of == target_ref[at, 0:1]).astype(jnp.bfloat16)
        head_ref[at, :] = jnp.dot(hot, table, preferred_element_type=jnp.float32).astype(jnp.bfloat16)
        hot = (slot_of == target_ref[at, 1:2]).astype(jnp.bfloat16)
        lines = jnp.dot(hot, table, preferred_element_type=jnp.float32)
        lane_of = lax.broadcasted_iota(jnp.int32, (block, LANES), 1)
        out_gate_ref[at, :] = jnp.sum(
            jnp.where(lane_of == target_ref[at, 2:3], lines, 0.0), axis=1, keepdims=True
        )


def final_work(plan, target, tables):
    count = plan.tokens * plan.top
    vmem = pl.BlockSpec(memory_space=pltpu.VMEM)
    return pl.pallas_call(
        functools.partial(final_kernel, plan),
        cost_estimate=pl.CostEstimate(flops=1, bytes_accessed=1, transcendentals=0),
        out_shape=(
            jax.ShapeDtypeStruct((count, plan.head_dim), jnp.bfloat16),
            jax.ShapeDtypeStruct((count, 1), jnp.float32),
        ),
        in_specs=[vmem] * (1 + GROUP),
        out_specs=(vmem, vmem),
        compiler_params=pltpu.CompilerParams(vmem_limit_bytes=8 * 1024 * 1024),
    )(target, *tables)


def local(mesh, head_outputs, out_grad, gate_weights, route_ids, out_proj):
    tokens, top, head_dim = head_outputs.shape
    features = out_grad.shape[1]
    plan = Plan(mesh, tokens, top, head_dim, features)
    x = lax.axis_index("dp")
    me = lax.axis_index("expert")
    z, y, c = me // GROUP, (me % GROUP) // 2, me % 2

    if plan.planes == 4:
        inner = (z == 1) | (z == 2)
        mates, middle = [(0, 1), (1, 0), (2, 3), (3, 2)], [(1, 2), (2, 1)]
        outward, inward = [(1, 0), (2, 3)], [(0, 1), (3, 2)]
        across = [(1, 3), (2, 0)]
        plane_of = [jnp.where(z < 2, 2, 1), z, jnp.where(z < 2, 3, 0), z ^ 1]
        which = jnp.where(inner, 0, 1)
    else:
        steps = [k % plan.planes for k in range(1, plan.planes + 1)]
        plane_of = [(z + k) % plan.planes for k in steps]
        which = 0
    info = plan.info(x, z, y, c, plane_of, which)

    own_weights = lax.dynamic_slice_in_dim(out_proj[0], x * plan.part, plan.part, 1)
    target = target_work(plan, info, route_ids)
    if plan.planes == 4:
        mate = plan.along(own_weights, mates)
        near_in = plan.along(own_weights, middle)
        mate, near_in, target = lax.optimization_barrier((mate, near_in, target))
        near_out = plan.along(near_in, outward)
        far_in, near_out = lax.optimization_barrier((plan.along(mate, middle), near_out))
        far_out = plan.along(far_in, outward)
    else:
        weights = [[(plan.shift(own_weights, dz=-k % plan.planes), None)] for k in steps]

    meta = jnp.concatenate(
        [
            gate_weights.T,
            route_ids.T.astype(jnp.bfloat16),
            jnp.zeros((LANES - 2 * top, tokens), jnp.bfloat16),
        ],
        axis=0,
    )
    flat_heads = head_outputs.reshape(tokens, top * head_dim)
    packs = []
    for dx, dy in plan.chips():
        piece = lax.dynamic_slice_in_dim(out_grad, ((x + dx) % plan.dp) * plan.part, plan.part, 1)
        value = jnp.concatenate([piece, flat_heads, meta], axis=1)
        value = plan.shift(value, dx=dx, dy=dy)
        if plan.planes == 4:
            if dx or dy:
                value, far_in, near_out = lax.optimization_barrier((value, far_in, near_out))
            else:
                value, near_out = lax.optimization_barrier((value, near_out))
        packs += [value, plan.shift(value, dc=1)]

    if plan.planes == 4:
        weights = [
            [(near_in, 0), (near_out, 1)],
            [(own_weights, None)],
            [(far_in, 0), (far_out, 1)],
            [(mate, None)],
        ]

    own_at = 1 if plan.planes == 4 else plan.planes - 1
    sums, backs, done = [], [], target
    for j in range(plan.planes):
        last = j == plan.planes - 1
        if last and plan.planes == 4:
            near_sum = sums[0] + plan.along(sums[0], inward)
            done = (done, near_sum)
        info, done = lax.optimization_barrier((info, done))
        target = target if j else done
        kind = jnp.float32 if j == own_at else jnp.bfloat16
        part, *back = slot_work(plan, j, info, packs, weights[j], kind, backs if last else ())
        sums.append(part)
        backs = back if last else backs + back
        done = back[0]

    far_pieces = []
    if plan.planes == 4:
        far_part = plan.along(sums[2], inward)
        far_part, done = lax.optimization_barrier((far_part, done))
        far_sums = sum_work(plan, info, [sums[2], far_part], jnp.bfloat16)
        info, far_sums = lax.optimization_barrier((info, far_sums))
        far_pieces = [plan.along(piece, across, dx) for dx, piece in enumerate(far_sums)]
        received = [plan.along(sums[3], mates), plan.along(near_sum, middle)]
    else:
        received = [plan.shift(sums[j], dz=steps[j]) for j in range(plan.planes - 1)]
    pieces = sum_work(plan, info, [sums[own_at]] + received, jnp.float32)
    pieces = [plan.shift(piece, dx=dx) for dx, piece in enumerate(pieces)]

    backs = [plan.shift(rows, dx=-dx % plan.dp) for dx, rows in enumerate(backs)]
    if plan.planes == 4:
        backs, far_sums = lax.optimization_barrier((backs, far_sums))
    merged = merge_work(plan, backs)
    tables = [
        plan.shift(merged[2 * dy + dc], dy=-dy % plan.rows)
        for dy in range(plan.rows)
        for dc in range(2)
    ]
    tables = tables[0::2] + [plan.shift(rows, dc=1) for rows in tables[1::2]]
    tables, far_pieces[1:] = lax.optimization_barrier((tables, far_pieces[1:]))
    grad_head, grad_gate = final_work(plan, target, tables)
    grad_proj = layout_work(plan, info, pieces + far_pieces)
    return (
        grad_head.reshape(tokens, top, head_dim),
        grad_gate.reshape(tokens, top).astype(jnp.bfloat16),
        grad_proj[None],
    )


def solution(mesh):
    return jax.shard_map(
        functools.partial(local, mesh),
        mesh=mesh,
        in_specs=(
            P(("dp", "expert"), None, None),
            P(("dp", "expert"), None),
            P(("dp", "expert"), None),
            P(("dp", "expert"), None),
            P("expert", None, None),
        ),
        out_specs=(
            P(("dp", "expert"), None, None),
            P(("dp", "expert"), None),
            P("expert", "dp", None),
        ),
        check_vma=False,
    )
```
